32 devices in a mesh: dp: 8 (over y, x, core), tensor: 4 (over z).
Axes of the slice: x: 2, y: 2, z: 4, core: 2. Of those that a mesh axis runs over, the one named last changes fastest.
Arguments:
- tokens: bfloat16 [8192, 1024], P(('dp', 'tensor')), may hold values from -6 to 6
- cotangent: bfloat16 [8192, 1024], P(('dp', 'tensor')), may hold values from -6 to 6
- lengths: int32 [24], replicated, may hold values from 1 to 512, as said below
- order: int32 [24], replicated, may hold values from 0 to 23, as said below
- w_qkv: bfloat16 [2, 1024, 3, 1024], P(None, 'dp', None, 'tensor'), may hold values from -0.1875 to 0.1875
- w_out: bfloat16 [2, 1024, 1024], P(None, 'tensor', 'dp'), may hold values from -0.75 to 0.75
- w_up: bfloat16 [2, 1024, 4096], P(None, 'dp', 'tensor'), may hold values from -0.1875 to 0.1875
- w_down: bfloat16 [2, 4096, 1024], P(None, 'tensor', 'dp'), may hold values from -0.09375 to 0.09375
- gains: float32 [2, 2, 1024], P(None, None, ('dp', 'tensor')), may hold values from 0.25 to 1.75
- biases: float32 [2, 6, 1024], P(None, None, ('dp', 'tensor')), may hold values from -3 to 3
- up_bias: float32 [2, 4096], P(None, ('dp', 'tensor')), may hold values from -3 to 3
Outputs:
- mixed: bfloat16 [8192, 1024], P(('dp', 'tensor'))
- tokens_grad: float32 [8192, 1024], P(('dp', 'tensor'))
- grad_qkv: float32 [2, 1024, 3, 1024], P(None, 'dp', None, 'tensor')
- grad_out: float32 [2, 1024, 1024], P(None, 'tensor', 'dp')
- grad_up: float32 [2, 1024, 4096], P(None, 'dp', 'tensor')
- grad_down: float32 [2, 4096, 1024], P(None, 'tensor', 'dp')
- grad_gains: float32 [2, 2, 1024], P(None, None, ('dp', 'tensor'))
- grad_biases: float32 [2, 6, 1024], P(None, None, ('dp', 'tensor'))
- grad_up_bias: float32 [2, 4096], P(None, ('dp', 'tensor'))
The draws below stay inside these ranges and needn't reach their ends.
Inputs may be any that keep to these rules, and one draw needn't show every extreme that they name: The 3 sequences g * 3 to g * 3 + 2 of each group have lengths summing to at most 1024, and one of them in every group is 512 long. A permutation of the 24 sequences in which order[g * 3 + j], j = 0 .. 2, are the sequences g * 3 to g * 3 + 2, each once.
All inputs are finite; a program needn't handle non-finite values.
Results may differ from the reference program's by a relative error of at most 0.02.
Values may be sent and summed in bfloat16 or wider, within the bound.
No kernel may reach another device: no remote copies, remote signals or barrier semaphores. Data moves between devices by JAX's collectives and lax.ppermute only.
A program may use at most 128 MiB of HBM per device.

```python
from functools import partial
import jax
import jax.numpy as jnp
from jax import lax

D = 1024
HEADS = 16
HEAD_DIM = 64
FF = 4096
LAYERS = 2
SEQ_GRP = 3
TOK_GRP = 1024
MAXLEN = 512
NSEQ = 24
TOKENS = 8192
N_DP = 8


def deal_slots(key):
    long_slot = jax.random.randint(jax.random.fold_in(key, 11), (N_DP, 1), 0, SEQ_GRP)
    short_length = jax.random.randint(jax.random.fold_in(key, 12), (N_DP, SEQ_GRP), 1, MAXLEN // 2 + 1)
    slot_index = jnp.arange(SEQ_GRP, dtype=jnp.int32)[None, :]
    slot_length = jnp.where(slot_index == long_slot, MAXLEN, short_length).astype(jnp.int32)
    group_keys = jax.random.split(jax.random.fold_in(key, 13), N_DP)
    within = jax.vmap(lambda one_key: jax.random.permutation(one_key, SEQ_GRP))(group_keys).astype(jnp.int32)
    group_base = (jnp.arange(N_DP, dtype=jnp.int32) * SEQ_GRP)[:, None]
    dealing = (within + group_base).astype(jnp.int32)
    return (slot_length.reshape(NSEQ), dealing.reshape(NSEQ))


def draw_lengths(key, part):
    shared = deal_slots(key)
    return shared[0]


def draw_order(key, part):
    shared = deal_slots(key)
    return shared[1]


def levels(stream_key, shape, shards, least, high):
    gain, own = 1.0, jax.random.fold_in(stream_key, 6)
    for axis_at, shards_of in shards:
        draws = jnp.exp(jax.random.uniform(jax.random.fold_in(own, axis_at), (shards_of,), jnp.float32, least / len(shards), high / len(shards)))
        gain = gain * jnp.repeat(draws, shape[axis_at] // shards_of).reshape([-1 if axis == axis_at else 1 for axis in range(len(shape))])
    return gain


def gaussian(stream_key, dims, deviation, reach, pieces=(), held_as=jnp.bfloat16):
    entries = jax.random.normal(stream_key, dims, jnp.float32) * deviation
    if len(pieces) > 0:
        entries = levels(stream_key, dims, pieces, -0.22, 0.18) * entries
    return jnp.clip(entries, min=-reach, max=reach).astype(held_as)


def setup_inputs(seed: int = 0) -> dict:
    arg_keys = jax.random.split(jax.random.key(seed), 12)
    return {
        "tokens": gaussian(arg_keys[0], (TOKENS, D), 1.0, 6.0, ((0, 32),)),
        "cotangent": gaussian(arg_keys[1], (TOKENS, D), 1.0, 6.0, ((0, 32),)),
        "lengths": draw_lengths(jax.random.fold_in(arg_keys[11], 71), 0),
        "order": draw_order(jax.random.fold_in(arg_keys[11], 71), 0),
        "w_qkv": gaussian(arg_keys[4], (LAYERS, D, 3, D), D ** -0.5, 0.1875, ((1, 8), (3, 4))),
        "w_out": gaussian(arg_keys[5], (LAYERS, D, D), 64 ** -0.5, 0.75, ((1, 4), (2, 8))),
        "w_up": gaussian(arg_keys[6], (LAYERS, D, FF), D ** -0.5, 0.1875, ((1, 8), (2, 4))),
        "w_down": gaussian(arg_keys[7], (LAYERS, FF, D), FF ** -0.5, 0.09375, ((1, 4), (2, 8))),
        "gains": jnp.clip(1.0 + 0.15 * jax.random.normal(arg_keys[8], (LAYERS, 2, D), jnp.float32), 0.25, 1.75),
        "biases": gaussian(arg_keys[9], (LAYERS, 6, D), 0.5, 3.0, ((2, 32),), jnp.float32),
        "up_bias": gaussian(arg_keys[10], (LAYERS, FF), 0.5, 3.0, ((1, 32),), jnp.float32),
    }


EPS = 1e-05
NEG = -1e+30

@jax.custom_vjp
def low(v):
    return lax.optimization_barrier(v.astype(jnp.bfloat16)).astype(jnp.float32)

@jax.custom_vjp
def low_back(v):
    return v

def low_keep(v):
    return (low(v), None)

def low_pass(kept, grad):
    return (grad,)

def back_keep(v):
    return (v, None)

def back_low(kept, grad):
    return (low(grad),)
low.defvjp(low_keep, low_pass)
low_back.defvjp(back_keep, back_low)

def layer_norm(field_in, gain_row, shift_row):
    centre = lax.optimization_barrier(jnp.mean(field_in, axis=-1, keepdims=True))
    centred = field_in - centre
    spread = lax.optimization_barrier(jnp.mean(centred * centred, axis=-1, keepdims=True))
    return centred * lax.rsqrt(spread + EPS) * gain_row + shift_row

def matmul(left, right):
    return jnp.dot(left, right, precision=lax.Precision.HIGHEST)

def group_maps(own_len, dealt_local, group_rows):
    slot_range = jnp.arange(SEQ_GRP, dtype=jnp.int32)
    own_len = own_len.astype(jnp.int32)
    own_end = jnp.cumsum(own_len).astype(jnp.int32)
    own_start = (own_end - own_len).astype(jnp.int32)
    pick_table = dealt_local[:, None] == slot_range[None, :]
    dealt_len = lax.optimization_barrier(jnp.sum(jnp.where(pick_table, own_len[None, :], 0), axis=1)).astype(jnp.int32)
    dealt_src = lax.optimization_barrier(jnp.sum(jnp.where(pick_table, own_start[None, :], 0), axis=1)).astype(jnp.int32)
    dealt_end = jnp.cumsum(dealt_len).astype(jnp.int32)
    dealt_begin = (dealt_end - dealt_len).astype(jnp.int32)
    position = jnp.arange(group_rows, dtype=jnp.int32)
    segments = lax.optimization_barrier(jnp.sum((position[:, None] >= dealt_end[None, :]).astype(jnp.int32), axis=1)).astype(jnp.int32)
    seg_hit = segments[:, None] == slot_range[None, :]
    source = (lax.optimization_barrier(jnp.sum(jnp.where(seg_hit, dealt_src[None, :] - dealt_begin[None, :] + position[:, None], 0), axis=1)) + jnp.where(segments == SEQ_GRP, position, 0)).astype(jnp.int32)
    return (segments, source)

def attention(queries, keys_all, values_all, segments):
    block_rows = min(512, TOK_GRP)
    block_count = TOK_GRP // block_rows
    score_scale = HEAD_DIM ** (-0.5)
    query_blocks = queries.reshape(block_count, block_rows, HEADS, HEAD_DIM)
    segment_blocks = segments.reshape(block_count, block_rows)

    def one_block(items_in):
        query_part, segment_part = items_in
        scores = jnp.einsum('bhd,khd->hbk', query_part, keys_all, precision=lax.Precision.HIGHEST) * score_scale
        scores = low_back(scores)
        same_segment = segment_part[:, None] == segments[None, :]
        masked = jnp.where(same_segment[None], scores, NEG)
        row_peak = lax.optimization_barrier(jnp.max(masked, axis=2, keepdims=True))
        exponent = jnp.exp(masked - row_peak)
        soft_probs = low(exponent / lax.optimization_barrier(jnp.sum(exponent, axis=2, keepdims=True)))
        return jnp.einsum('hbk,khd->bhd', soft_probs, values_all, precision=lax.Precision.HIGHEST)
    block_outs = lax.map(jax.checkpoint(one_block), (query_blocks, segment_blocks))
    return block_outs.reshape(TOK_GRP, D)

def one_layer(hidden, segments, layer_weights):
    w_qkv, w_out, w_up, w_down, gain_pair, bias_rows, up_bias = layer_weights
    x_low = low(hidden)
    projected = low_back(matmul(x_low, w_qkv.reshape(D, 3 * D)))
    queries = low(projected[:, :D] + bias_rows[0])
    keys_all = low(projected[:, D:2 * D])
    values_all = low(projected[:, 2 * D:] + bias_rows[1])
    attended = attention(queries.reshape(TOK_GRP, HEADS, HEAD_DIM), keys_all.reshape(TOK_GRP, HEADS, HEAD_DIM), values_all.reshape(TOK_GRP, HEADS, HEAD_DIM), segments)
    attended = low(low_back(attended))
    branch = low_back(matmul(attended, w_out)) + bias_rows[2]
    normed = layer_norm(hidden + branch, gain_pair[0], bias_rows[3])
    normed_low = low(normed)
    hidden_up = low_back(matmul(normed_low, w_up)) + up_bias
    activated = low(jax.nn.gelu(hidden_up, approximate=False))
    second = low_back(matmul(activated, w_down)) + bias_rows[4]
    return layer_norm(normed + second, gain_pair[1], bias_rows[5])

def take_rows(group_rows_in, source):
    return jnp.take(group_rows_in, source, axis=0)

def reference(tokens, cotangent, lengths, order, w_qkv, w_out, w_up, w_down, gains, biases, up_bias):
    group_base = (jnp.arange(N_DP, dtype=jnp.int32) * SEQ_GRP)[:, None]
    dealt_local = (order.reshape(N_DP, SEQ_GRP) - group_base).astype(jnp.int32)
    segment_all, source_all = jax.vmap(partial(group_maps, group_rows=TOK_GRP))(lengths.reshape(N_DP, SEQ_GRP), dealt_local)
    valid_rows = (segment_all < SEQ_GRP).astype(jnp.float32).reshape(TOKENS, 1)
    weights = (w_qkv.astype(jnp.float32), w_out.astype(jnp.float32), w_up.astype(jnp.float32), w_down.astype(jnp.float32), gains.astype(jnp.float32), biases.astype(jnp.float32), up_bias.astype(jnp.float32))

    def forward(hidden_in, params):
        groups = hidden_in.reshape(N_DP, TOK_GRP, D)

        def group_pass(group_x, segments, source):
            group_x = jnp.take(group_x, source, axis=0)
            for layer_index in range(LAYERS):
                layer_weights = (params[0][layer_index], params[1][layer_index], params[2][layer_index], params[3][layer_index], params[4][layer_index], params[5][layer_index], params[6][layer_index])
                group_x = one_layer(group_x, segments, layer_weights)
            return group_x
        checked = jax.checkpoint(group_pass)

        def scan_step(scan_carry, items_in):
            return (scan_carry, checked(items_in[0], items_in[1], items_in[2]))
        _, group_outs = lax.scan(scan_step, jnp.zeros((), jnp.float32), (groups, segment_all, source_all))
        return group_outs.reshape(TOKENS, D)
    result, pullback = jax.vjp(forward, tokens.astype(jnp.float32), weights)
    cot_dealt = jax.vmap(take_rows)(cotangent.astype(jnp.float32).reshape(N_DP, TOK_GRP, D), source_all).reshape(TOKENS, D) * valid_rows
    grad_in, grad_weights = pullback(cot_dealt)
    grad_dealt = jax.vmap(take_rows)(grad_in.reshape(N_DP, TOK_GRP, D), source_all).reshape(TOKENS, D)
    return (result.astype(jnp.bfloat16), grad_dealt, grad_weights[0], grad_weights[1], grad_weights[2], grad_weights[3], grad_weights[4], grad_weights[5], grad_weights[6])
```

```python
import jax
import jax.numpy as jnp
import numpy as np
from jax import lax
from jax.sharding import Mesh, PartitionSpec as P

D = 1024
HEAD_DIM = 64
FF = 4096
LAYERS = 2
SEQ_GRP = 3

EPS = 1e-05
NEG = -1e30
ALL = ("d", "c", "zh", "zl")
SWAP = [(0, 1), (1, 0)]
bf16 = jnp.bfloat16
f32 = jnp.float32


def dot(a, b, ca, cb):
    return lax.dot_general(a, b, (((ca,), (cb,)), ((), ())), preferred_element_type=f32)


def swap(a, axis):
    return lax.ppermute(a, axis, SWAP)


def flip_d(a, bit, n_d):
    return lax.ppermute(a, "d", [(i, i ^ (1 << bit)) for i in range(n_d)])


def transpose_home(a):
    return lax.ppermute(a, ("c", "zh"), [(0, 0), (1, 2), (2, 1), (3, 3)])


def norm_parts(v):
    centred = v - jnp.mean(v, axis=-1, keepdims=True)
    r = lax.rsqrt(jnp.mean(centred * centred, axis=-1, keepdims=True) + EPS)
    return centred * r, r


def norm_back(n, r, gain, d_out):
    dn = d_out * gain
    dv = r * (
        dn - jnp.mean(dn, axis=-1, keepdims=True) - n * jnp.mean(dn * n, axis=-1, keepdims=True)
    )
    return dv, jnp.sum(d_out * n, axis=0), jnp.sum(d_out, axis=0)


def group_maps(own_len, dealt_local, group_rows):
    slot_range = jnp.arange(SEQ_GRP, dtype=jnp.int32)
    own_end = jnp.cumsum(own_len)
    own_start = own_end - own_len
    pick_table = dealt_local[:, None] == slot_range[None, :]
    dealt_len = jnp.sum(jnp.where(pick_table, own_len[None, :], 0), axis=1)
    dealt_src = jnp.sum(jnp.where(pick_table, own_start[None, :], 0), axis=1)
    dealt_end = jnp.cumsum(dealt_len)
    dealt_begin = dealt_end - dealt_len
    position = jnp.arange(group_rows, dtype=jnp.int32)
    segments = jnp.sum((position[:, None] >= dealt_end[None, :]).astype(jnp.int32), axis=1)
    seg_hit = segments[:, None] == slot_range[None, :]
    source = jnp.sum(
        jnp.where(seg_hit, dealt_src[None, :] - dealt_begin[None, :] + position[:, None], 0), axis=1
    ) + jnp.where(segments == SEQ_GRP, position, 0)
    return (segments, source)


def share_rows(own):
    far = swap(own, "zl")
    near = swap(own, "c")
    far_near = swap(far, "c")
    return own, near, far, far_near


def sum_rows(near_part, far_part, rows):
    far_own, far_near = far_part[:rows], far_part[rows:]
    chip_sum = far_own + swap(far_near.astype(bf16), "c").astype(f32)
    crossed = swap(chip_sum.astype(bf16), "zl")
    other = swap(near_part[rows:].astype(bf16), "c")
    return near_part[:rows] + other.astype(f32) + crossed.astype(f32)


def gather_weights(piece, pos, n_d):
    d, c, zh, _ = pos
    bits = list(range(n_d.bit_length() - 1))
    crossed = swap(piece, "zh")
    same = c == zh
    keep = jnp.where(same, piece, crossed)
    send = jnp.where(same, crossed, piece)
    recv = swap(send, "c")
    found = {}
    for start, order, core in ((keep, bits, c), (recv, bits[::-1], 1 - c)):
        cur, masks = start[None], [0]
        for bit in order:
            cur = jnp.concatenate([cur, flip_d(cur, bit, n_d)], 0)
            masks = masks + [m ^ (1 << bit) for m in masks]
        found[len(found)] = (cur, masks)
    stacked = jnp.concatenate([found[0][0], found[1][0]], 0)
    place_one = {m: i for i, m in enumerate(found[0][1])}
    place_two = {m: i for i, m in enumerate(found[1][1])}
    table_one = jnp.array([place_one[m] for m in range(n_d)], jnp.int32)
    table_two = jnp.array([place_two[m] for m in range(n_d)], jnp.int32)
    blocks = []
    for dd in range(n_d):
        for cc in range(2):
            mask = jnp.bitwise_xor(d, dd)
            at = jnp.where(c == cc, table_one[mask], n_d + table_two[mask])
            blocks.append(lax.dynamic_index_in_dim(stacked, at, 0, keepdims=False))
    return jnp.concatenate(blocks, 0)


def pick(a, bit_value, axis):
    return lax.dynamic_index_in_dim(a, bit_value, axis, keepdims=False)


def reduce_weights(grad, pos, n_d):
    d, c, zh, _ = pos
    bits = list(range(n_d.bit_length() - 1))
    rows, cols = grad.shape[0] // (2 * n_d), grad.shape[1]
    view = grad.reshape(n_d, 2, rows, cols)
    sums = []
    for core, order in ((c, bits[::-1]), (1 - c, bits)):
        cur = pick(view, core, 1).reshape((2,) * len(bits) + (rows, cols))
        left = list(reversed(bits))
        for bit in order:
            axis = left.index(bit)
            mine = jnp.bitwise_and(jnp.right_shift(d, bit), 1)
            send = pick(cur, 1 - mine, axis).astype(bf16)
            cur = pick(cur, mine, axis).astype(f32) + flip_d(send, bit, n_d).astype(f32)
            left.remove(bit)
        sums.append(cur)
    first, second = sums
    other = swap(second.astype(bf16), "c").astype(f32)
    same = c == zh
    keep = jnp.where(same, first, other)
    send = jnp.where(same, other, first)
    return keep + swap(send.astype(bf16), "zh").astype(f32)


def gather_small(own, pos, n_d):
    d, c, zh, zl = pos
    cur = own[None]
    for axis, me in (("zl", zl), ("zh", zh), ("c", c)):
        got = swap(cur, axis)
        cur = jnp.where(me == 0, jnp.concatenate([cur, got]), jnp.concatenate([got, cur]))
    for bit in range(n_d.bit_length() - 1):
        got = flip_d(cur, bit, n_d)
        mine = jnp.bitwise_and(jnp.right_shift(d, bit), 1)
        cur = jnp.where(mine == 0, jnp.concatenate([cur, got]), jnp.concatenate([got, cur]))
    return cur


def reduce_small(full, pos, n_d):
    d, c, zh, zl = pos
    cur = full
    for bit in reversed(range(n_d.bit_length() - 1)):
        mine = jnp.bitwise_and(jnp.right_shift(d, bit), 1)
        view = cur.reshape(2, -1, full.shape[1])
        cur = pick(view, mine, 0) + flip_d(pick(view, 1 - mine, 0), bit, n_d)
    for axis, me in (("c", c), ("zh", zh), ("zl", zl)):
        view = cur.reshape(2, -1, full.shape[1])
        cur = pick(view, me, 0) + swap(pick(view, 1 - me, 0), axis)
    return cur[0]


def heads_of(a, heads):
    return a.reshape(a.shape[0], heads, HEAD_DIM)


def attend(queries, keys, values, seg_q, seg_k, scale):
    scores = jnp.einsum("bhd,khd->hbk", queries, keys, preferred_element_type=f32) * scale
    masked = jnp.where((seg_q[:, None] == seg_k[None, :])[None], scores, NEG)
    peak = jnp.max(masked, axis=2, keepdims=True)
    exponent = jnp.exp(masked - peak)
    total = jnp.sum(exponent, axis=2, keepdims=True)
    probs = (exponent / total).astype(bf16)
    out = jnp.einsum("hbk,khd->bhd", probs, values, preferred_element_type=f32)
    return out.reshape(queries.shape[0], -1).astype(bf16), peak, total


def attend_back(queries, keys, values, seg_q, seg_k, peak, total, grad, scale):
    scores = jnp.einsum("bhd,khd->hbk", queries, keys, preferred_element_type=f32) * scale
    masked = jnp.where((seg_q[:, None] == seg_k[None, :])[None], scores, NEG)
    probs = jnp.exp(masked - peak) / total
    d_probs = jnp.einsum("bhd,khd->hbk", grad, values, preferred_element_type=f32)
    d_scores = probs * (d_probs - jnp.sum(probs * d_probs, axis=2, keepdims=True))
    low = d_scores.astype(bf16)
    d_q = jnp.einsum("hbk,khd->bhd", low, keys, preferred_element_type=f32) * scale
    d_k = jnp.einsum("hbk,bhd->khd", low, queries, preferred_element_type=f32) * scale
    d_v = jnp.einsum("hbk,bhd->khd", probs.astype(bf16), grad, preferred_element_type=f32)
    return d_q, d_k, d_v


def gelu(u):
    return jax.nn.gelu(u, approximate=False)


def body(tokens, cotangent, lengths, order, w_qkv, w_out, w_up, w_down, gains, biases, up_bias):
    rows = tokens.shape[0]
    n_d = lax.axis_size("d")
    n_dev = n_d * 8
    tensor_count = 4
    head_width = D // tensor_count
    heads = head_width // HEAD_DIM
    ff_width = FF // tensor_count
    piece = D // (2 * n_d)
    scale = HEAD_DIM ** (-0.5)
    d, c, zh, zl = (lax.axis_index(a) for a in ALL)
    pos = (d, c, zh, zl)
    slot = 2 * c + zl
    block_ids = [jnp.bitwise_xor(slot, m) for m in (0, 2, 1, 3)]

    def chunk(layer, which):
        if which == 0:
            return jnp.concatenate([w_qkv[layer].reshape(piece, -1), w_out[layer].T], 1)
        return w_up[layer] if which == 1 else w_down[layer].T

    raw = transpose_home(tokens)
    small_all = gather_small(
        jnp.concatenate([gains.reshape(-1), biases.reshape(-1), up_bias.reshape(-1)]), pos, n_d
    )
    weights = [[gather_weights(chunk(l, k), pos, n_d) for k in range(3)] for l in range(LAYERS)]
    width = D // n_dev
    up_width = FF // n_dev
    n_gain, n_bias = LAYERS * 2 * width, LAYERS * 6 * width
    gains_all = small_all[:, :n_gain].reshape(n_dev, LAYERS, 2, width)
    gains_all = gains_all.transpose(1, 2, 0, 3).reshape(LAYERS, 2, D)
    biases_all = small_all[:, n_gain : n_gain + n_bias].reshape(n_dev, LAYERS, 6, width)
    biases_all = biases_all.transpose(1, 2, 0, 3).reshape(LAYERS, 6, D)
    upb_all = small_all[:, n_gain + n_bias :].reshape(n_dev, LAYERS, up_width)
    upb_all = upb_all.transpose(1, 0, 2).reshape(LAYERS, FF)

    seq_base = (d * 2 + zh) * SEQ_GRP
    own_len = lax.dynamic_slice_in_dim(lengths, seq_base, SEQ_GRP)
    dealt_local = lax.dynamic_slice_in_dim(order, seq_base, SEQ_GRP) - seq_base
    segments, source = group_maps(own_len, dealt_local, 4 * rows)
    seg = jnp.concatenate([lax.dynamic_slice_in_dim(segments, b * rows, rows) for b in block_ids])
    src = jnp.concatenate([lax.dynamic_slice_in_dim(source, b * rows, rows) for b in block_ids])
    src_x = jnp.bitwise_xor(src // rows, slot)
    src_at = (2 * (src_x % 2) + src_x // 2) * rows + src % rows
    deal = (src_at[:, None] == jnp.arange(4 * rows, dtype=jnp.int32)[None, :]).astype(bf16)
    valid = (seg[:rows] < SEQ_GRP).astype(f32)[:, None]
    seg_near, seg_far = seg[: 2 * rows], seg[2 * rows :]

    raw_all = jnp.concatenate(share_rows(raw), 0)
    x_all = dot(deal, raw_all, 1, 0).astype(bf16)
    hidden = x_all[:rows].astype(f32)
    blocks = tuple(x_all[i * rows : (i + 1) * rows] for i in range(4))

    kept = []
    for layer in range(LAYERS):
        w_att, w_u, w_dt = weights[layer]
        w_q, w_o = w_att[:, : 3 * head_width], w_att[:, 3 * head_width :]
        bias_rows = biases_all[layer]
        q_bias = lax.dynamic_slice_in_dim(bias_rows[0], slot * head_width, head_width)
        v_bias = lax.dynamic_slice_in_dim(bias_rows[1], slot * head_width, head_width)
        u_bias = lax.dynamic_slice_in_dim(upb_all[layer], slot * ff_width, ff_width)
        add = jnp.concatenate([q_bias, jnp.zeros((head_width,), f32), v_bias])
        x_near = jnp.concatenate(blocks[:2], 0)
        x_far = jnp.concatenate(blocks[2:], 0)
        proj_near = (dot(x_near, w_q, 1, 0) + add).astype(bf16)
        proj_far = (dot(x_far, w_q, 1, 0) + add).astype(bf16)
        proj = jnp.concatenate([proj_near, proj_far], 0)
        q, k, v = (heads_of(proj[:, i * head_width : (i + 1) * head_width], heads) for i in range(3))
        att_far, peak_far, total_far = attend(q[2 * rows :], k, v, seg_far, seg, scale)
        far_part = dot(att_far, w_o, 1, 1)
        att_near, peak_near, total_near = attend(q[: 2 * rows], k, v, seg_near, seg, scale)
        near_part = dot(att_near, w_o, 1, 1)
        pre_one = hidden + sum_rows(near_part, far_part, rows) + bias_rows[2]
        n_one, r_one = norm_parts(pre_one)
        normed = n_one * gains_all[layer, 0] + bias_rows[3]
        n_blocks = share_rows(normed.astype(bf16))
        n_near = jnp.concatenate(n_blocks[:2], 0)
        n_far = jnp.concatenate(n_blocks[2:], 0)
        up_near = dot(n_near, w_u, 1, 0) + u_bias
        up_far = dot(n_far, w_u, 1, 0) + u_bias
        act_far = gelu(up_far).astype(bf16)
        far_part = dot(act_far, w_dt, 1, 1)
        act_near = gelu(up_near).astype(bf16)
        near_part = dot(act_near, w_dt, 1, 1)
        pre_two = normed + sum_rows(near_part, far_part, rows) + bias_rows[4]
        n_two, r_two = norm_parts(pre_two)
        hidden = n_two * gains_all[layer, 1] + bias_rows[5]
        if layer + 1 < LAYERS:
            blocks = share_rows(hidden.astype(bf16))
        kept.append(
            dict(
                x=(x_near, x_far), q=q, k=k, v=v, soft=((peak_near, total_near), (peak_far, total_far)),
                att=(att_near, att_far), n_one=n_one, r_one=r_one, n=(n_near, n_far),
                up=(up_near, up_far), act=(act_near, act_far), n_two=n_two, r_two=r_two,
            )
        )
    mixed = transpose_home(hidden.astype(bf16))

    raw_cot = jnp.concatenate(share_rows(transpose_home(cotangent)), 0)
    grad_y = dot(deal[:rows], raw_cot, 1, 0) * valid
    reduced = [None] * LAYERS
    smalls = [None] * LAYERS
    for layer in reversed(range(LAYERS)):
        w_att, w_u, w_dt = weights[layer]
        w_q, w_o = w_att[:, : 3 * head_width], w_att[:, 3 * head_width :]
        s = kept[layer]
        d_two, g_gain2, g_shift2 = norm_back(s["n_two"], s["r_two"], gains_all[layer, 1], grad_y)
        g_downb = jnp.sum(d_two, axis=0)
        two = share_rows(d_two.astype(bf16))
        two_near = jnp.concatenate(two[:2], 0)
        two_far = jnp.concatenate(two[2:], 0)

        def up_back(two_part, up_part):
            d_act = dot(two_part, w_dt, 1, 0)
            _, back = jax.vjp(gelu, up_part)
            (d_up,) = back(d_act)
            return d_up.astype(bf16), jnp.sum(d_up, axis=0)

        up_far, sum_far = up_back(two_far, s["up"][1])
        far_part = dot(up_far, w_u, 1, 1)
        up_near, sum_near = up_back(two_near, s["up"][0])
        near_part = dot(up_near, w_u, 1, 1)
        g_upb = sum_far + sum_near
        d_normed = d_two + sum_rows(near_part, far_part, rows)
        d_one, g_gain1, g_shift1 = norm_back(s["n_one"], s["r_one"], gains_all[layer, 0], d_normed)
        g_outb = jnp.sum(d_one, axis=0)
        one = share_rows(d_one.astype(bf16))
        one_near = jnp.concatenate(one[:2], 0)
        one_far = jnp.concatenate(one[2:], 0)
        g_down = (dot(s["act"][0], two_near, 0, 0) + dot(s["act"][1], two_far, 0, 0)).T
        g_up = dot(s["n"][0], up_near, 0, 0) + dot(s["n"][1], up_far, 0, 0)
        d_att_far = heads_of(dot(one_far, w_o, 1, 0).astype(bf16), heads)
        d_att_near = heads_of(dot(one_near, w_o, 1, 0).astype(bf16), heads)
        q, k, v = s["q"], s["k"], s["v"]
        dq_far, dk_far, dv_far = attend_back(
            q[2 * rows :], k, v, seg_far, seg, *s["soft"][1], d_att_far, scale
        )
        dq_near, dk_near, dv_near = attend_back(
            q[: 2 * rows], k, v, seg_near, seg, *s["soft"][0], d_att_near, scale
        )
        d_q = jnp.concatenate([dq_near, dq_far], 0).reshape(4 * rows, head_width)
        d_k = (dk_far + dk_near).reshape(4 * rows, head_width)
        d_v = (dv_far + dv_near).reshape(4 * rows, head_width)
        g_qb, g_vb = jnp.sum(d_q, axis=0), jnp.sum(d_v, axis=0)
        d_proj = jnp.concatenate([d_q.astype(bf16), d_k.astype(bf16), d_v.astype(bf16)], 1)
        far_part = dot(d_proj[2 * rows :], w_q, 1, 1)
        near_part = dot(d_proj[: 2 * rows], w_q, 1, 1)
        grad_y = d_one + sum_rows(near_part, far_part, rows)
        g_qkv = dot(s["x"][0], d_proj[: 2 * rows], 0, 0) + dot(s["x"][1], d_proj[2 * rows :], 0, 0)
        g_out = dot(one_near, s["att"][0], 0, 0) + dot(one_far, s["att"][1], 0, 0)
        reduced[layer] = (
            reduce_weights(jnp.concatenate([g_qkv, g_out], 1).astype(bf16), pos, n_d),
            reduce_weights(g_up.astype(bf16), pos, n_d),
            reduce_weights(g_down.astype(bf16), pos, n_d),
        )
        place = lambda vec, full: lax.dynamic_update_slice_in_dim(
            jnp.zeros((full,), f32), vec, slot * vec.shape[0], 0
        )
        smalls[layer] = (
            jnp.stack([g_gain1, g_gain2]),
            jnp.stack([place(g_qb, D), place(g_vb, D), g_outb, g_shift1, g_downb, g_shift2]),
            place(g_upb, FF),
        )
    tokens_grad = transpose_home(grad_y.astype(bf16)).astype(f32)

    def by_device(a, per):
        return jnp.moveaxis(a.reshape(a.shape[:-1] + (n_dev, per)), -2, 0).reshape(n_dev, -1)

    small_terms = jnp.concatenate(
        [
            by_device(jnp.stack([s[0] for s in smalls]), width),
            by_device(jnp.stack([s[1] for s in smalls]), width),
            by_device(jnp.stack([s[2] for s in smalls]), up_width),
        ],
        1,
    )
    small_sum = reduce_small(small_terms, pos, n_d)
    g_gains = small_sum[:n_gain].reshape(LAYERS, 2, width)
    g_biases = small_sum[n_gain : n_gain + n_bias].reshape(LAYERS, 6, width)
    g_upb = small_sum[n_gain + n_bias :].reshape(LAYERS, up_width)
    g_qkv = jnp.stack([r[0][:, : 3 * head_width].reshape(piece, 3, head_width) for r in reduced])
    g_out = jnp.stack([r[0][:, 3 * head_width :].T for r in reduced])
    g_up = jnp.stack([r[1] for r in reduced])
    g_down = jnp.stack([r[2].T for r in reduced])
    return mixed, tokens_grad, g_qkv, g_out, g_up, g_down, g_gains, g_biases, g_upb


def solution(mesh):
    n_dp, n_t = mesh.shape["dp"], mesh.shape["tensor"]
    fine = Mesh(mesh.devices.reshape(n_dp // 2, 2, n_t // 2, 2), ALL)
    dp, t = ("d", "c"), ("zh", "zl")
    return jax.shard_map(
        body,
        mesh=fine,
        in_specs=(
            P(ALL, None),
            P(ALL, None),
            P(),
            P(),
            P(None, dp, None, t),
            P(None, t, dp),
            P(None, dp, t),
            P(None, t, dp),
            P(None, None, ALL),
            P(None, None, ALL),
            P(None, ALL),
        ),
        out_specs=(
            P(ALL, None),
            P(ALL, None),
            P(None, dp, None, t),
            P(None, t, dp),
            P(None, dp, t),
            P(None, t, dp),
            P(None, None, ALL),
            P(None, None, ALL),
            P(None, ALL),
        ),
        check_vma=False,
    )
```

```python
import functools

import jax
import jax.numpy as jnp
from jax import lax
from jax.experimental import pallas as pl
from jax.experimental.pallas import tpu as pltpu
from jax.sharding import Mesh, PartitionSpec as P

D = 1024
HEAD_DIM = 64
FF = 4096
LAYERS = 2
SEQ_GRP = 3

EPS = 1e-05
NEG = -1e30
ALL = ("d", "c", "zh", "zl")
SWAP = [(0, 1), (1, 0)]
bf16 = jnp.bfloat16
f32 = jnp.float32
MIB = 1 << 20

TAIL_STEP = 0.24
TAIL = (
    0.0912286469891869,
    0.14294535326111468,
    -0.11556713177962434,
    0.5630756863681534,
    -0.5892310046041954,
    0.5271447780474939,
    -0.11959632556906954,
)
INV_SQRT_2PI = 0.3989422804014327


def nn(a, b):
    return lax.dot_general(a, b, (((1,), (0,)), ((), ())), preferred_element_type=f32)


def nt(a, b):
    return lax.dot_general(a, b, (((1,), (1,)), ((), ())), preferred_element_type=f32)


def tn(a, b):
    return lax.dot_general(a, b, (((0,), (0,)), ((), ())), preferred_element_type=f32)


def stack_rows(refs):
    return jnp.concatenate([r[...] for r in refs], 0)


def params(limit):
    return pltpu.CompilerParams(vmem_limit_bytes=limit * MIB)


def cost(flops, nbytes, exps=0):
    return pl.CostEstimate(flops=int(flops), bytes_accessed=int(nbytes), transcendentals=int(exps))


def struct(shape, dtype):
    return jax.ShapeDtypeStruct(shape, dtype)


def gelu_parts(u):
    z = jnp.abs(u)
    bell = jnp.exp(-0.5 * (u * u))
    below = 1.0 + TAIL_STEP * z
    t = pl.reciprocal(below, approx=True)
    t = t * (2.0 - below * t)
    poly = jnp.full_like(t, TAIL[-1])
    for coef in TAIL[-2::-1]:
        poly = poly * t + coef
    tail = bell * (poly * t)
    phi = jnp.where(u > 0.0, 1.0 - tail, tail)
    return u * phi, phi + u * (INV_SQRT_2PI * bell)


def project_kernel(n_x, *refs):
    x_refs, (w_ref, add_ref, out_ref) = refs[:n_x], refs[n_x:]
    out_ref[...] = (nn(stack_rows(x_refs), w_ref[...]) + add_ref[...]).astype(bf16)


def project(blocks, w_att, add, width):
    rows = sum(b.shape[0] for b in blocks)
    d = w_att.shape[0]
    return pl.pallas_call(
        functools.partial(project_kernel, len(blocks)),
        grid=(3,),
        in_specs=[pl.BlockSpec(b.shape, lambda i: (0, 0)) for b in blocks]
        + [pl.BlockSpec((d, width), lambda i: (0, i)), pl.BlockSpec((1, width), lambda i: (0, i))],
        out_specs=pl.BlockSpec((rows, width), lambda i: (0, i)),
        out_shape=struct((rows, 3 * width), bf16),
        compiler_params=params(32),
        cost_estimate=cost(6 * rows * d * width, 4 * MIB),
        name="project",
    )(*blocks, w_att, add)


def attend_kernel(scale, heads, q_ref, kn_ref, kf_ref, vn_ref, vf_ref, segq_ref, segk_ref, w_ref, *outs):
    att_ref, lse_ref, one_ref, two_ref = outs
    q = q_ref[...] * jnp.asarray(scale, bf16)
    rows, width = q.shape
    ks, vs = (kn_ref, kf_ref), (vn_ref, vf_ref)
    kv_rows = kn_ref.shape[0]
    lane = lax.broadcasted_iota(jnp.int32, (1, width), 1) // HEAD_DIM
    stat_lane = lax.broadcasted_iota(jnp.int32, (1, 128), 1)
    out = jnp.zeros((rows, width), f32)
    lse = jnp.zeros((rows, 128), f32)
    segq = segq_ref[...]
    masks = [
        jnp.where(segq == segk_ref[:, i * kv_rows : (i + 1) * kv_rows], 0.0, NEG) for i in range(2)
    ]
    for h in range(heads):
        hit = lane == h
        qh = jnp.where(hit, q, jnp.zeros_like(q))
        scores = [nt(qh, ks[i][...]) + masks[i] for i in range(2)]
        peak = jnp.maximum(*[jnp.max(s, axis=1, keepdims=True) for s in scores])
        exps = [jnp.exp(s - peak) for s in scores]
        total = sum(jnp.sum(e, axis=1, keepdims=True) for e in exps)
        inv = 1.0 / total
        head_out = sum(nn((exps[i] * inv).astype(bf16), vs[i][...]) for i in range(2))
        out = jnp.where(hit, head_out, out)
        lse = jnp.where(stat_lane == h, peak + jnp.log(total), lse)
    low = out.astype(bf16)
    att_ref[...] = low
    lse_ref[...] = lse
    part = nt(low, w_ref[...])
    half = rows // 2
    one_ref[...] = part[:half].astype(one_ref.dtype)
    two_ref[...] = part[half:].astype(two_ref.dtype)


def attend(proj_q, proj, seg_q, seg_k, w_att, scale, heads, one_type):
    rows, width = proj_q.shape[0], heads * HEAD_DIM
    kv_rows = proj[0].shape[0]
    d = w_att.shape[0]
    whole = lambda *at: (lambda i: at)
    return pl.pallas_call(
        functools.partial(attend_kernel, scale, heads),
        grid=(1,),
        in_specs=[pl.BlockSpec((rows, width), whole(0, 0))]
        + [pl.BlockSpec((kv_rows, width), whole(0, 1))] * 2
        + [pl.BlockSpec((kv_rows, width), whole(0, 2))] * 2
        + [
            pl.BlockSpec((rows, 1), whole(0, 0)),
            pl.BlockSpec((1, 2 * kv_rows), whole(0, 0)),
            pl.BlockSpec((d, width), whole(0, 3)),
        ],
        out_specs=[
            pl.BlockSpec((rows, width), whole(0, 0)),
            pl.BlockSpec((rows, 128), whole(0, 0)),
            pl.BlockSpec((rows // 2, d), whole(0, 0)),
            pl.BlockSpec((rows // 2, d), whole(0, 0)),
        ],
        out_shape=[
            struct((rows, width), bf16),
            struct((rows, 128), f32),
            struct((rows // 2, d), one_type),
            struct((rows // 2, d), bf16),
        ],
        compiler_params=params(40),
        cost_estimate=cost(16 * rows * kv_rows * 2 * width, 6 * MIB, rows * kv_rows * 2 * heads),
        name="attend",
    )(proj_q, *proj, *proj, seg_q, seg_k, w_att)


def attend_back_kernel(scale, heads, last, *refs):
    q_ref, kn_ref, kf_ref, vn_ref, vf_ref, segq_ref, segk_ref, lse_ref, a_ref, b_ref, w_ref = refs[:11]
    q = q_ref[...]
    rows, width = q.shape
    ks, vs = (kn_ref, kf_ref), (vn_ref, vf_ref)
    kv_rows = kn_ref.shape[0]
    if last:
        dqn_ref, sumq_ref, dk_in, dv_in, wq_ref = refs[11:16]
        near_ref, far_ref, sums_ref, one_ref, two_ref, dk_ref, dv_ref = refs[16:]
    else:
        dqn_ref, sumq_ref, dk_ref, dv_ref = refs[11:]
    lane = lax.broadcasted_iota(jnp.int32, (1, width), 1) // HEAD_DIM
    grad = nn(stack_rows((a_ref, b_ref)), w_ref[...]).astype(bf16)
    segq = segq_ref[...]
    masks = [
        jnp.where(segq == segk_ref[:, i * kv_rows : (i + 1) * kv_rows], 0.0, NEG) for i in range(2)
    ]
    sc = jnp.asarray(scale, bf16)
    zero = jnp.zeros_like(q)
    dq = jnp.zeros((rows, width), f32)
    for h in range(heads):
        hit = lane == h
        qh = jnp.where(hit, q, zero) * sc
        gh = jnp.where(hit, grad, zero)
        lse = lse_ref[:, h : h + 1]
        probs = [jnp.exp(nt(qh, ks[i][...]) + masks[i] - lse) for i in range(2)]
        d_probs = [nt(gh, vs[i][...]) for i in range(2)]
        dot_sum = sum(jnp.sum(p * g, axis=1, keepdims=True) for p, g in zip(probs, d_probs))
        dq_h = 0.0
        for i in range(2):
            low = (probs[i] * (d_probs[i] - dot_sum)).astype(bf16)
            at = pl.ds(i * kv_rows, kv_rows)
            d_k, d_v = tn(low, qh), tn(probs[i].astype(bf16), gh)
            if h > 0:
                d_k, d_v = d_k + dk_ref[at, :], d_v + dv_ref[at, :]
            elif last:
                d_k, d_v = d_k + dk_in[at, :], d_v + dv_in[at, :]
            dk_ref[at, :] = d_k
            dv_ref[at, :] = d_v
            dq_h = dq_h + nn(low, ks[i][...])
        dq = jnp.where(hit, dq_h, dq)
    dq = dq * scale
    sum_q = jnp.sum(dq, axis=0, keepdims=True)
    if not last:
        dqn_ref[...] = dq.astype(bf16)
        sumq_ref[...] = sum_q
        return
    sums_ref[0:1, :] = sum_q + sumq_ref[...]
    sums_ref[1:2, :] = jnp.sum(dv_ref[...], axis=0, keepdims=True)
    near_ref[:, :width] = dqn_ref[...]
    far_ref[:, :width] = dq.astype(bf16)
    for i, ref in enumerate((near_ref, far_ref)):
        at = pl.ds(i * kv_rows, kv_rows)
        ref[:, width : 2 * width] = dk_ref[at, :].astype(bf16)
        ref[:, 2 * width :] = dv_ref[at, :].astype(bf16)
    part = nt(far_ref[...], wq_ref[...]).astype(bf16)
    half = rows // 2
    one_ref[...] = part[:half]
    two_ref[...] = part[half:]


def attend_back(proj_q, proj, seg_q, seg_k, lse, one, w_att, scale, heads, earlier=None):
    rows, width = proj_q.shape[0], heads * HEAD_DIM
    kv_rows = proj[0].shape[0]
    d = w_att.shape[0]
    last = earlier is not None
    whole = lambda *at: (lambda i: at)
    in_specs = (
        [pl.BlockSpec((rows, width), whole(0, 0))]
        + [pl.BlockSpec((kv_rows, width), whole(0, 1))] * 2
        + [pl.BlockSpec((kv_rows, width), whole(0, 2))] * 2
        + [
            pl.BlockSpec((rows, 1), whole(0, 0)),
            pl.BlockSpec((1, 2 * kv_rows), whole(0, 0)),
            pl.BlockSpec((rows, 128), whole(0, 0)),
            pl.BlockSpec((rows // 2, d), whole(0, 0)),
            pl.BlockSpec((rows // 2, d), whole(0, 0)),
            pl.BlockSpec((d, width), whole(0, 3)),
        ]
    )
    args = [proj_q, *proj, *proj, seg_q, seg_k, lse, *one, w_att]
    acc = pltpu.VMEM((2 * kv_rows, width), f32)
    if last:
        in_specs += [
            pl.BlockSpec((rows, width), whole(0, 0)),
            pl.BlockSpec((1, width), whole(0, 0)),
            pl.BlockSpec((2 * kv_rows, width), whole(0, 0)),
            pl.BlockSpec((2 * kv_rows, width), whole(0, 0)),
            pl.BlockSpec((d, 3 * width), whole(0, 0)),
        ]
        args += [*earlier, w_att]
        out_shape = [
            struct((kv_rows, 3 * width), bf16),
            struct((kv_rows, 3 * width), bf16),
            struct((2, width), f32),
            struct((rows // 2, d), bf16),
            struct((rows // 2, d), bf16),
        ]
        scratch = [acc, acc]
    else:
        out_shape = [
            struct((rows, width), bf16),
            struct((1, width), f32),
            struct((2 * kv_rows, width), f32),
            struct((2 * kv_rows, width), f32),
        ]
        scratch = []
    return pl.pallas_call(
        functools.partial(attend_back_kernel, scale, heads, last),
        grid=(1,),
        in_specs=in_specs,
        out_specs=[pl.BlockSpec(o.shape, whole(0, 0)) for o in out_shape],
        out_shape=out_shape,
        scratch_shapes=scratch,
        compiler_params=params(48),
        cost_estimate=cost(40 * rows * kv_rows * 2 * width, 8 * MIB, rows * kv_rows * 2 * heads),
        name="attend_back",
    )(*args)


def ffn_kernel(a_ref, b_ref, up_ref, down_ref, bias_ref, act_ref, slope_ref, one_ref, two_ref, x, acc):
    step = pl.program_id(0)

    @pl.when(step == 0)
    def _():
        x[...] = stack_rows((a_ref, b_ref))

    value, slope = gelu_parts(nn(x[...], up_ref[...]) + bias_ref[...])
    low = value.astype(bf16)
    act_ref[...] = low
    slope_ref[...] = slope
    part = nt(low, down_ref[...])

    @pl.when(step == 0)
    def _():
        acc[...] = part

    @pl.when(step > 0)
    def _():
        acc[...] += part

    @pl.when(step == pl.num_programs(0) - 1)
    def _():
        half = acc.shape[0] // 2
        one_ref[...] = acc[:half].astype(one_ref.dtype)
        two_ref[...] = acc[half:].astype(two_ref.dtype)


def ffn(blocks, w_ud, bias, one_type, tile=256):
    rows, d = 2 * blocks[0].shape[0], w_ud.shape[0]
    ff = w_ud.shape[1] // 2
    steps = ff // tile
    fixed = lambda i: (0, 0)
    moving = lambda i: (0, i)
    return pl.pallas_call(
        ffn_kernel,
        grid=(steps,),
        in_specs=[
            pl.BlockSpec((rows // 2, d), fixed),
            pl.BlockSpec((rows // 2, d), fixed),
            pl.BlockSpec((d, tile), moving),
            pl.BlockSpec((d, tile), lambda i: (0, i + steps)),
            pl.BlockSpec((1, tile), moving),
        ],
        out_specs=[
            pl.BlockSpec((rows, tile), moving),
            pl.BlockSpec((rows, tile), moving),
            pl.BlockSpec((rows // 2, d), fixed),
            pl.BlockSpec((rows // 2, d), fixed),
        ],
        out_shape=[
            struct((rows, ff), bf16),
            struct((rows, ff), f32),
            struct((rows // 2, d), one_type),
            struct((rows // 2, d), bf16),
        ],
        scratch_shapes=[pltpu.VMEM((rows, d), bf16), pltpu.VMEM((rows, d), f32)],
        compiler_params=params(40),
        cost_estimate=cost(4 * rows * d * ff, 9 * MIB, rows * ff * 2),
        name="ffn",
    )(*blocks, w_ud, w_ud, bias)


def ffn_back_kernel(a_ref, b_ref, up_ref, down_ref, slope_ref, low_ref, sum_ref, one_ref, two_ref, x, acc):
    step = pl.program_id(0)

    @pl.when(step == 0)
    def _():
        x[...] = stack_rows((a_ref, b_ref))

    d_up = nn(x[...], down_ref[...]) * slope_ref[...]
    low = d_up.astype(bf16)
    low_ref[...] = low
    sum_ref[...] = jnp.sum(d_up, axis=0, keepdims=True)
    part = nt(low, up_ref[...])

    @pl.when(step == 0)
    def _():
        acc[...] = part

    @pl.when(step > 0)
    def _():
        acc[...] += part

    @pl.when(step == pl.num_programs(0) - 1)
    def _():
        half = acc.shape[0] // 2
        one_ref[...] = acc[:half].astype(one_ref.dtype)
        two_ref[...] = acc[half:].astype(two_ref.dtype)


def ffn_back(blocks, w_ud, slope, one_type, tile=256):
    rows, d = 2 * blocks[0].shape[0], w_ud.shape[0]
    ff = w_ud.shape[1] // 2
    steps = ff // tile
    fixed = lambda i: (0, 0)
    moving = lambda i: (0, i)
    return pl.pallas_call(
        ffn_back_kernel,
        grid=(steps,),
        in_specs=[
            pl.BlockSpec((rows // 2, d), fixed),
            pl.BlockSpec((rows // 2, d), fixed),
            pl.BlockSpec((d, tile), moving),
            pl.BlockSpec((d, tile), lambda i: (0, i + steps)),
            pl.BlockSpec((rows, tile), moving),
        ],
        out_specs=[
            pl.BlockSpec((rows, tile), moving),
            pl.BlockSpec((1, tile), moving),
            pl.BlockSpec((rows // 2, d), fixed),
            pl.BlockSpec((rows // 2, d), fixed),
        ],
        out_shape=[
            struct((rows, ff), bf16),
            struct((1, ff), f32),
            struct((rows // 2, d), one_type),
            struct((rows // 2, d), bf16),
        ],
        scratch_shapes=[pltpu.VMEM((rows, d), bf16), pltpu.VMEM((rows, d), f32)],
        compiler_params=params(40),
        cost_estimate=cost(4 * rows * d * ff, 9 * MIB),
        name="ffn_back",
    )(*blocks, w_ud, w_ud, slope)


def grad_kernel(n_d, order_ref, *refs):
    outs = refs[12:]
    tile = D // (2 * n_d)
    per = n_d // 2
    for g, out in enumerate(outs):
        for pair in range(0, per, 2):
            at = [pl.multiple_of(order_ref[g * per + pair + k] * tile, tile) for k in range(2)]
            col = 0
            for p in range(2):
                a_refs, (near, far) = refs[6 * p : 6 * p + 4], refs[6 * p + 4 : 6 * p + 6]
                width = near.shape[1]
                total = 0.0
                for half, b_ref in ((0, near), (2, far)):
                    sel = jnp.concatenate(
                        [
                            jnp.concatenate([a[:, pl.ds(s, tile)] for s in at], 1)
                            for a in a_refs[half : half + 2]
                        ],
                        0,
                    )
                    total = total + tn(sel, b_ref[...])
                for k in range(2):
                    out[pair + k, :, col : col + width] = total[k * tile : (k + 1) * tile].astype(bf16)
                col += width


def weight_grad(pairs, order, n_d):
    flat = [r for a, b in pairs for r in (*a, *b)]
    cols = sum(b[0].shape[1] for _, b in pairs)
    tile = D // (2 * n_d)
    per = n_d // 2
    rows = sum(b.shape[0] for b in pairs[0][1])
    if tile % 128 or per % 2:
        full = jnp.concatenate(
            [dot(jnp.concatenate(a, 0), jnp.concatenate(b, 0), 0, 0) for a, b in pairs], 1
        )
        tiles = jnp.take(full.astype(bf16).reshape(2 * n_d, tile, cols), order, axis=0)
        return [tiles[g * per : (g + 1) * per] for g in range(4)]
    vmem = pl.BlockSpec(memory_space=pltpu.VMEM)
    return pl.pallas_call(
        functools.partial(grad_kernel, n_d),
        in_specs=[pl.BlockSpec(memory_space=pltpu.SMEM)] + [vmem] * len(flat),
        out_specs=[vmem] * 4,
        out_shape=[struct((per, tile, cols), bf16)] * 4,
        compiler_params=params(48),
        cost_estimate=cost(2 * rows * D * cols, 12 * MIB),
        name="weight_grad",
    )(order, *flat)


def place_kernel(counts, dest_ref, *refs):
    ins, out_ref = refs[: len(counts)], refs[len(counts)]
    k = 0
    for ref, count in zip(ins, counts):
        for i in range(count):
            out_ref[dest_ref[k]] = ref[i]
            k += 1


def place_tiles(stacks, dest):
    counts = [s.shape[0] for s in stacks]
    total = sum(counts)
    rows, cols = stacks[0].shape[1:]
    vmem = pl.BlockSpec(memory_space=pltpu.VMEM)
    out = pl.pallas_call(
        functools.partial(place_kernel, counts),
        in_specs=[pl.BlockSpec(memory_space=pltpu.SMEM)] + [vmem] * len(stacks),
        out_specs=vmem,
        out_shape=struct((total, rows, cols), bf16),
        compiler_params=params(32),
        cost_estimate=cost(0, 4 * total * rows * cols),
        name="place_tiles",
    )(dest, *stacks)
    return out.reshape(total * rows, cols)


def dot(a, b, ca, cb):
    return lax.dot_general(a, b, (((ca,), (cb,)), ((), ())), preferred_element_type=f32)


def swap(a, axis):
    return lax.ppermute(a, axis, SWAP)


def flip_d(a, bit, n_d):
    return lax.ppermute(a, "d", [(i, i ^ (1 << bit)) for i in range(n_d)])


def transpose_home(a):
    return lax.ppermute(a, ("c", "zh"), [(0, 0), (1, 2), (2, 1), (3, 3)])


def after(a, *marks):
    return lax.optimization_barrier((a,) + marks)[0]


def share_rows(own):
    far = swap(own, "zl")
    near = swap(own, "c")
    far_near = swap(far, "c")
    return own, near, far, far_near


def sum_rows(near_own, near_other, far_own, far_other):
    chip_sum = far_own.astype(f32) + swap(far_other, "c").astype(f32)
    crossed = swap(chip_sum.astype(bf16), "zl")
    other = swap(near_other, "c")
    return near_own + other.astype(f32) + crossed.astype(f32)


def masks_of(order):
    masks = [0]
    for bit in order:
        masks = masks + [m ^ (1 << bit) for m in masks]
    return masks


class Gather:
    def __init__(self, piece, pos, n_d):
        self.piece, self.pos, self.n_d = piece, pos, n_d
        self.bits = list(range(n_d.bit_length() - 1))

    def cross(self, *marks):
        _, c, zh, _ = self.pos
        piece = after(self.piece, *marks) if marks else self.piece
        self.crossed = swap(piece, "zh")
        same = c == zh
        self.one = [jnp.where(same, piece, self.crossed)[None]]
        self.two = [swap(jnp.where(same, self.crossed, piece), "c")[None]]
        self.step = 0

    def spread(self, *marks):
        one, two = (p[0] if len(p) == 1 else jnp.concatenate(p, 0) for p in (self.one, self.two))
        if marks:
            one, two = lax.optimization_barrier((one, two) + marks)[:2]
        bit_one, bit_two = self.bits[self.step], self.bits[-1 - self.step]
        self.got = flip_d(one, bit_one, self.n_d)
        self.one = [one, self.got]
        self.two = [two, flip_d(two, bit_two, self.n_d)]
        self.step += 1

    def whole(self):
        while self.step < len(self.bits):
            self.spread()
        d, c, _, _ = self.pos
        dest = [2 * jnp.bitwise_xor(d, m) + c for m in masks_of(self.bits)]
        dest += [2 * jnp.bitwise_xor(d, m) + 1 - c for m in masks_of(self.bits[::-1])]
        return place_tiles(self.one + self.two, jnp.stack(dest).astype(jnp.int32))


def grad_order(pos, n_d):
    d, c, _, _ = pos
    bits = list(range(n_d.bit_length() - 1))
    half = n_d // 2
    order = []
    for core, masks in ((c, masks_of(bits)), (1 - c, masks_of(bits[::-1]))):
        order += [2 * jnp.bitwise_xor(d, m) + core for m in masks[half:] + masks[:half]]
    return jnp.stack(order).astype(jnp.int32)


def reduce_weights(stacks, pos, n_d):
    _, c, zh, _ = pos
    bits = list(range(n_d.bit_length() - 1))
    sums = []
    for send, keep, order in ((*stacks[:2], bits[::-1]), (*stacks[2:], bits)):
        for step, bit in enumerate(order):
            got = flip_d(send, bit, n_d)
            total = keep.astype(f32) + got.astype(f32)
            half = total.shape[0] // 2
            if step + 1 < len(order):
                send, keep = total[half:].astype(bf16), total[:half]
        sums.append(total[0])
    first, second = sums
    other = swap(second.astype(bf16), "c").astype(f32)
    same = c == zh
    keep = jnp.where(same, first, other)
    send = jnp.where(same, other, first)
    return keep + swap(send.astype(bf16), "zh").astype(f32)


def gather_small(own, pos, n_d):
    d, c, zh, zl = pos
    cur = own
    for axis, me in (("zl", zl), ("zh", zh), ("c", c)):
        got = swap(cur, axis)
        cur = jnp.where(me == 0, jnp.concatenate([cur, got]), jnp.concatenate([got, cur]))
    for bit in range(n_d.bit_length() - 1):
        got = flip_d(cur, bit, n_d)
        mine = jnp.bitwise_and(jnp.right_shift(d, bit), 1)
        cur = jnp.where(mine == 0, jnp.concatenate([cur, got]), jnp.concatenate([got, cur]))
    return cur


def pick(a, at, axis):
    return lax.dynamic_index_in_dim(a, at, axis, keepdims=False)


def reduce_small(full, pos, n_d):
    d, c, zh, zl = pos
    cur = full
    for bit in reversed(range(n_d.bit_length() - 1)):
        mine = jnp.bitwise_and(jnp.right_shift(d, bit), 1)
        view = cur.reshape(2, -1, full.shape[1])
        cur = pick(view, mine, 0) + flip_d(pick(view, 1 - mine, 0), bit, n_d)
    for axis, me in (("c", c), ("zh", zh), ("zl", zl)):
        view = cur.reshape(2, -1, full.shape[1])
        cur = pick(view, me, 0) + swap(pick(view, 1 - me, 0), axis)
    return cur


def norm_parts(v):
    centred = v - jnp.mean(v, axis=-1, keepdims=True)
    r = lax.rsqrt(jnp.mean(centred * centred, axis=-1, keepdims=True) + EPS)
    return centred * r, r


def column_sum(a):
    return jnp.sum(a, axis=0, keepdims=True)


def norm_back(n, r, gain, d_out):
    dn = d_out * gain
    dv = r * (
        dn - jnp.mean(dn, axis=-1, keepdims=True) - n * jnp.mean(dn * n, axis=-1, keepdims=True)
    )
    return dv, column_sum(d_out * n), column_sum(d_out)


def group_maps(own_len, dealt_local, group_rows):
    slot_range = jnp.arange(SEQ_GRP, dtype=jnp.int32)
    own_end = jnp.cumsum(own_len)
    own_start = own_end - own_len
    pick_table = dealt_local[:, None] == slot_range[None, :]
    dealt_len = jnp.sum(jnp.where(pick_table, own_len[None, :], 0), axis=1)
    dealt_src = jnp.sum(jnp.where(pick_table, own_start[None, :], 0), axis=1)
    dealt_end = jnp.cumsum(dealt_len)
    dealt_begin = dealt_end - dealt_len
    position = jnp.arange(group_rows, dtype=jnp.int32)
    segments = jnp.sum((position[:, None] >= dealt_end[None, :]).astype(jnp.int32), axis=1)
    seg_hit = segments[:, None] == slot_range[None, :]
    source = jnp.sum(
        jnp.where(seg_hit, dealt_src[None, :] - dealt_begin[None, :] + position[:, None], 0), axis=1
    ) + jnp.where(segments == SEQ_GRP, position, 0)
    return (segments, source)


def body(tokens, cotangent, lengths, order, w_qkv, w_out, w_up, w_down, gains, biases, up_bias):
    rows = tokens.shape[0]
    n_d = lax.axis_size("d")
    n_dev = n_d * 8
    head_width = D // 4
    heads = head_width // HEAD_DIM
    ff_width = FF // 4
    piece = D // (2 * n_d)
    scale = HEAD_DIM ** (-0.5)
    d, c, zh, zl = (lax.axis_index(a) for a in ALL)
    pos = (d, c, zh, zl)
    slot = 2 * c + zl
    block_ids = [jnp.bitwise_xor(slot, m) for m in (0, 2, 1, 3)]

    def chunk(layer, which):
        if which == 0:
            return jnp.concatenate([w_qkv[layer].reshape(piece, -1), w_out[layer].T], 1)
        return jnp.concatenate([w_up[layer], w_down[layer].T], 1)

    raw = transpose_home(tokens)
    g_a0, g_f0, g_a1, g_f1 = (Gather(chunk(l, k), pos, n_d) for l in range(LAYERS) for k in range(2))
    g_a0.cross()
    small_all = gather_small(
        jnp.concatenate(
            [gains.reshape(1, -1), biases.reshape(1, -1), up_bias.reshape(1, -1)], 1
        ),
        pos,
        n_d,
    )
    g_f0.cross(g_a0.crossed)
    w_a0 = g_a0.whole()
    weights = [[w_a0, None], [None, None]]
    width = D // n_dev
    up_width = FF // n_dev
    n_vec = LAYERS * 8
    vectors = small_all[:, : n_vec * width].reshape(n_dev, n_vec, width)
    vectors = vectors.transpose(1, 0, 2).reshape(n_vec, D)
    ups = small_all[:, n_vec * width :].reshape(n_dev, LAYERS, up_width)
    ups = ups.transpose(1, 0, 2).reshape(LAYERS, FF)

    def gain(layer, i):
        return vectors[2 * layer + i][None]

    def bias(layer, i):
        return vectors[2 * LAYERS + 6 * layer + i][None]

    def part_of(row, size):
        return lax.dynamic_slice(row, (0, slot * size), (1, size))

    seq_base = (d * 2 + zh) * SEQ_GRP
    own_len = lax.dynamic_slice_in_dim(lengths, seq_base, SEQ_GRP)
    dealt_local = lax.dynamic_slice_in_dim(order, seq_base, SEQ_GRP) - seq_base
    segments, source = group_maps(own_len, dealt_local, 4 * rows)
    seg = jnp.concatenate([lax.dynamic_slice_in_dim(segments, b * rows, rows) for b in block_ids])
    src = jnp.concatenate([lax.dynamic_slice_in_dim(source, b * rows, rows) for b in block_ids])
    src_x = jnp.bitwise_xor(src // rows, slot)
    src_at = (2 * (src_x % 2) + src_x // 2) * rows + src % rows
    deal = (src_at[:, None] == jnp.arange(4 * rows, dtype=jnp.int32)[None, :]).astype(bf16)
    valid = (seg[:rows] < SEQ_GRP).astype(f32)[:, None]
    seg_col, seg_row = seg[:, None], seg[None, :]
    seg_near, seg_far = seg_col[: 2 * rows], seg_col[2 * rows :]
    tile_order = grad_order(pos, n_d)

    raw_all = jnp.concatenate(share_rows(raw), 0)
    blocks = tuple(
        dot(deal[i * rows : (i + 1) * rows], raw_all, 1, 0).astype(bf16) for i in range(4)
    )
    hidden = blocks[0].astype(f32)

    kept = []
    for layer in range(LAYERS):
        first = layer == 0
        w_att = weights[layer][0]
        add = jnp.concatenate(
            [
                part_of(bias(layer, 0), head_width),
                jnp.zeros((1, head_width), f32),
                part_of(bias(layer, 1), head_width),
            ],
            1,
        )
        proj_near = project(blocks[:2], w_att, add, head_width)
        proj_far = project(blocks[2:], w_att, add, head_width)
        proj = (proj_near, proj_far)
        if first:
            g_f0.spread(w_att)
            g_f0.spread(proj_far)
            g_a1.cross(proj_far)
        else:
            g_f1.spread(proj_far)
        att_far, lse_far, far_own, far_other = attend(
            proj_far, proj, seg_far, seg_row, w_att, scale, heads, bf16
        )
        att_near, lse_near, near_own, near_other = attend(
            proj_near, proj, seg_near, seg_row, w_att, scale, heads, f32
        )
        pre_one = hidden + sum_rows(near_own, near_other, far_own, far_other) + bias(layer, 2)
        n_one, r_one = norm_parts(pre_one)
        normed = n_one * gain(layer, 0) + bias(layer, 3)
        normed_low = normed.astype(bf16)
        if first:
            g_f1.cross(normed_low)
            g_a1.spread(normed_low)
            weights[0][1] = g_f0.whole()
        else:
            weights[1][1] = g_f1.whole()
        w_ud = weights[layer][1]
        n_blocks = share_rows(normed_low)
        u_bias = part_of(ups[layer : layer + 1], ff_width)
        act_near, slope_near, near_own, near_other = ffn(n_blocks[:2], w_ud, u_bias, f32)
        if first:
            g_a1.spread(act_near)
        act_far, slope_far, far_own, far_other = ffn(n_blocks[2:], w_ud, u_bias, bf16)
        if first:
            g_f1.spread(far_own)
        pre_two = normed + sum_rows(near_own, near_other, far_own, far_other) + bias(layer, 4)
        n_two, r_two = norm_parts(pre_two)
        hidden = n_two * gain(layer, 1) + bias(layer, 5)
        hidden_low = hidden.astype(bf16)
        kept.append(
            dict(
                x=blocks, proj=proj, lse=(lse_near, lse_far), att=(att_near, att_far),
                n_one=n_one, r_one=r_one, n=n_blocks, slope=(slope_near, slope_far),
                act=(act_near, act_far), n_two=n_two, r_two=r_two,
            )
        )
        if first:
            weights[1][0] = g_a1.whole()
            blocks = share_rows(hidden_low)
    mixed = transpose_home(hidden_low)

    raw_cot = jnp.concatenate(share_rows(transpose_home(cotangent)), 0)
    grad_y = dot(deal[:rows], raw_cot, 1, 0) * valid
    reduced = [None] * LAYERS
    vector_sums = [None] * LAYERS
    up_sums = [None] * LAYERS

    def spot(vec, full):
        return lax.dynamic_update_slice(jnp.zeros((1, full), f32), vec, (0, slot * vec.shape[1]))

    for layer in reversed(range(LAYERS)):
        w_att, w_ud = weights[layer]
        s = kept[layer]
        d_two, g_gain2, g_shift2 = norm_back(s["n_two"], s["r_two"], gain(layer, 1), grad_y)
        two = share_rows(d_two.astype(bf16))
        up_near, sum_near, near_own, near_other = ffn_back(two[:2], w_ud, s["slope"][0], f32)
        up_far, sum_far, far_own, far_other = ffn_back(two[2:], w_ud, s["slope"][1], bf16)
        d_normed = d_two + sum_rows(near_own, near_other, far_own, far_other)
        d_one, g_gain1, g_shift1 = norm_back(s["n_one"], s["r_one"], gain(layer, 0), d_normed)
        one = share_rows(d_one.astype(bf16))
        g_ff = weight_grad(((s["n"], (up_near, up_far)), (two, s["act"])), tile_order, n_d)
        earlier = attend_back(
            s["proj"][0], s["proj"], seg_near, seg_row, s["lse"][0], one[:2], w_att, scale, heads
        )
        d_near, d_far, sums, far_own, far_other = attend_back(
            s["proj"][1], s["proj"], seg_far, seg_row, s["lse"][1], one[2:], w_att, scale, heads,
            earlier,
        )
        w_q = w_att[:, : 3 * head_width]
        near_own = dot(d_near[:rows], w_q, 1, 1)
        near_other = dot(d_near[rows:], w_q, 1, 1).astype(bf16)
        grad_y = d_one + sum_rows(near_own, near_other, far_own, far_other)
        g_att = weight_grad(((s["x"], (d_near, d_far)), (one, s["att"])), tile_order, n_d)
        reduced[layer] = (reduce_weights(g_att, pos, n_d), reduce_weights(g_ff, pos, n_d))
        vector_sums[layer] = (
            [g_gain1, g_gain2],
            [
                spot(sums[0:1], D), spot(sums[1:2], D), column_sum(d_one),
                g_shift1, column_sum(d_two), g_shift2,
            ],
        )
        up_sums[layer] = spot(sum_near + sum_far, FF)
    tokens_grad = transpose_home(grad_y.astype(bf16)).astype(f32)

    terms = jnp.concatenate(
        [g for s in vector_sums for g in s[0]] + [b for s in vector_sums for b in s[1]], 0
    )
    small_terms = jnp.concatenate(
        [
            terms.reshape(n_vec, n_dev, width).transpose(1, 0, 2).reshape(n_dev, n_vec * width),
            jnp.concatenate(up_sums, 0)
            .reshape(LAYERS, n_dev, up_width)
            .transpose(1, 0, 2)
            .reshape(n_dev, LAYERS * up_width),
        ],
        1,
    )
    small_sum = reduce_small(small_terms, pos, n_d)
    n_gain = LAYERS * 2 * width
    g_gains = small_sum[:, :n_gain].reshape(LAYERS, 2, width)
    g_biases = small_sum[:, n_gain : n_vec * width].reshape(LAYERS, 6, width)
    g_upb = small_sum[:, n_vec * width :].reshape(LAYERS, up_width)
    g_qkv = jnp.stack([r[0][:, : 3 * head_width].reshape(piece, 3, head_width) for r in reduced])
    g_out = jnp.stack([r[0][:, 3 * head_width :].T for r in reduced])
    g_up = jnp.stack([r[1][:, :ff_width] for r in reduced])
    g_down = jnp.stack([r[1][:, ff_width:].T for r in reduced])
    return mixed, tokens_grad, g_qkv, g_out, g_up, g_down, g_gains, g_biases, g_upb


def solution(mesh):
    n_dp, n_t = mesh.shape["dp"], mesh.shape["tensor"]
    fine = Mesh(mesh.devices.reshape(n_dp // 2, 2, n_t // 2, 2), ALL)
    dp, t = ("d", "c"), ("zh", "zl")
    return jax.shard_map(
        body,
        mesh=fine,
        in_specs=(
            P(ALL, None),
            P(ALL, None),
            P(),
            P(),
            P(None, dp, None, t),
            P(None, t, dp),
            P(None, dp, t),
            P(None, t, dp),
            P(None, None, ALL),
            P(None, None, ALL),
            P(None, ALL),
        ),
        out_specs=(
            P(ALL, None),
            P(ALL, None),
            P(None, dp, None, t),
            P(None, t, dp),
            P(None, dp, t),
            P(None, t, dp),
            P(None, None, ALL),
            P(None, None, ALL),
            P(None, ALL),
        ),
        check_vma=False,
    )
```

```python
import functools

import jax
import jax.numpy as jnp
from jax import lax
from jax.experimental import pallas as pl
from jax.experimental.pallas import tpu as pltpu
from jax.sharding import Mesh, PartitionSpec as P

D = 1024
HEAD_DIM = 64
FF = 4096
LAYERS = 2
SEQ_GRP = 3

EPS = 1e-05
NEG = -1e30
ALL = ("d", "c", "zh", "zl")
SWAP = [(0, 1), (1, 0)]
bf16 = jnp.bfloat16
f32 = jnp.float32
MIB = 1 << 20

TAIL_STEP = 0.24
TAIL = (
    0.0912286469891869,
    0.14294535326111468,
    -0.11556713177962434,
    0.5630756863681534,
    -0.5892310046041954,
    0.5271447780474939,
    -0.11959632556906954,
)
INV_SQRT_2PI = 0.3989422804014327


def nn(a, b):
    return lax.dot_general(a, b, (((1,), (0,)), ((), ())), preferred_element_type=f32)


def nt(a, b):
    return lax.dot_general(a, b, (((1,), (1,)), ((), ())), preferred_element_type=f32)


def tn(a, b):
    return lax.dot_general(a, b, (((0,), (0,)), ((), ())), preferred_element_type=f32)


def stack_rows(refs):
    return jnp.concatenate([r[...] for r in refs], 0)


def params(limit):
    return pltpu.CompilerParams(vmem_limit_bytes=limit * MIB)


def cost(flops, nbytes, exps=0):
    return pl.CostEstimate(flops=int(flops), bytes_accessed=int(nbytes), transcendentals=int(exps))


def struct(shape, dtype):
    return jax.ShapeDtypeStruct(shape, dtype)


def hbm(shape, dtype):
    return pltpu.HBM(shape, dtype)


def far(*arrays):
    return [pltpu.with_memory_space_constraint(a, pltpu.HBM) for a in arrays]


SCALARS = pl.BlockSpec(memory_space=pltpu.SMEM)
ROWS = pl.BlockSpec(memory_space=pltpu.HBM)


def full(a):
    shape = a.shape
    return pl.BlockSpec(shape, lambda *_: (0,) * len(shape))


def blocks_in(arrays):
    return [full(a) for a in arrays]


def gelu_parts(u):
    z = jnp.abs(u)
    bell = jnp.exp(-0.5 * (u * u))
    below = 1.0 + TAIL_STEP * z
    t = pl.reciprocal(below, approx=True)
    t = t * (2.0 - below * t)
    poly = jnp.full_like(t, TAIL[-1])
    for coef in TAIL[-2::-1]:
        poly = poly * t + coef
    tail = bell * (poly * t)
    phi = jnp.where(u > 0.0, 1.0 - tail, tail)
    return u * phi, phi + u * (INV_SQRT_2PI * bell)


def whole(*at):
    return lambda i: at


def project_kernel(*refs):
    x_refs, (w_ref, add_ref, out_ref, x_ref) = refs[:2], refs[2:]

    @pl.when(pl.program_id(0) == 0)
    def _():
        x_ref[...] = stack_rows(x_refs)

    out_ref[...] = (nn(x_ref[...], w_ref[0]) + add_ref[...]).astype(bf16)


def project(x, w_qkv, add):
    rows = 2 * x[0].shape[0]
    _, d, width = w_qkv.shape
    return pl.pallas_call(
        project_kernel,
        grid=(3,),
        in_specs=blocks_in(x)
        + [pl.BlockSpec((1, d, width), lambda i: (i, 0, 0)), pl.BlockSpec((1, width), lambda i: (0, i))],
        out_specs=[pl.BlockSpec((rows, width), lambda i: (0, i)), pl.BlockSpec((rows, d), whole(0, 0))],
        out_shape=[struct((rows, 3 * width), bf16), hbm((rows, d), bf16)],
        compiler_params=params(12),
        cost_estimate=cost(6 * rows * d * width, 4 * MIB),
        name="project",
    )(*x, w_qkv, add)


def input_grad_kernel(g_ref, w_ref, mine_ref, theirs_ref):
    width = w_ref.shape[2]
    part = sum(nt(g_ref[:, j * width : (j + 1) * width], w_ref[j]) for j in range(3))
    half = part.shape[0] // 2
    mine_ref[...] = part[:half]
    theirs_ref[...] = part[half:].astype(bf16)


def input_grad(d_proj, w_qkv):
    rows = d_proj.shape[0]
    _, d, width = w_qkv.shape
    outs = [struct((rows // 2, d), f32), struct((rows // 2, d), bf16)]
    return pl.pallas_call(
        input_grad_kernel,
        grid=(1,),
        in_specs=blocks_in((d_proj, w_qkv)),
        out_specs=blocks_in(outs),
        out_shape=outs,
        compiler_params=params(16),
        cost_estimate=cost(6 * rows * d * width, 4 * MIB),
        name="input_grad",
    )(d_proj, w_qkv)


def attend_kernel(scale, heads, q_ref, k0_ref, k1_ref, v0_ref, v1_ref, segq_ref, segk_ref, w_ref, *outs):
    att_ref, lse_ref, mine_ref, theirs_ref = outs
    q = q_ref[...] * jnp.asarray(scale, bf16)
    rows, width = q.shape
    ks, vs = (k0_ref, k1_ref), (v0_ref, v1_ref)
    kv_rows = k0_ref.shape[0]
    lane = lax.broadcasted_iota(jnp.int32, (1, width), 1) // HEAD_DIM
    stat_lane = lax.broadcasted_iota(jnp.int32, (1, 128), 1)
    out = jnp.zeros((rows, width), f32)
    lse = jnp.zeros((rows, 128), f32)
    segq = segq_ref[...]
    masks = [
        jnp.where(segq == segk_ref[:, i * kv_rows : (i + 1) * kv_rows], 0.0, NEG) for i in range(2)
    ]
    for h in range(heads):
        hit = lane == h
        qh = jnp.where(hit, q, jnp.zeros_like(q))
        scores = [nt(qh, ks[i][...]) + masks[i] for i in range(2)]
        peak = jnp.maximum(*[jnp.max(s, axis=1, keepdims=True) for s in scores])
        exps = [jnp.exp(s - peak) for s in scores]
        total = sum(jnp.sum(e, axis=1, keepdims=True) for e in exps)
        inv = 1.0 / total
        head_out = sum(nn((exps[i] * inv).astype(bf16), vs[i][...]) for i in range(2))
        out = jnp.where(hit, head_out, out)
        lse = jnp.where(stat_lane == h, peak + jnp.log(total), lse)
    low = out.astype(bf16)
    att_ref[...] = low
    lse_ref[...] = lse
    part = nn(low, w_ref[...])
    half = rows // 2
    mine_ref[...] = part[:half]
    theirs_ref[...] = part[half:].astype(bf16)


def attend(proj_q, proj, seg_q, seg_k, w_out, scale, heads):
    rows, width = proj_q.shape[0], heads * HEAD_DIM
    d = w_out.shape[1]
    return pl.pallas_call(
        functools.partial(attend_kernel, scale, heads),
        grid=(1,),
        in_specs=[pl.BlockSpec((rows, width), whole(0, 0))]
        + [pl.BlockSpec((rows, width), whole(0, 1))] * 2
        + [pl.BlockSpec((rows, width), whole(0, 2))] * 2
        + [
            pl.BlockSpec((rows, 1), whole(0, 0)),
            pl.BlockSpec((1, 2 * rows), whole(0, 0)),
            pl.BlockSpec((width, d), whole(0, 0)),
        ],
        out_specs=[
            pl.BlockSpec((rows, width), whole(0, 0)),
            pl.BlockSpec((rows, 128), whole(0, 0)),
            pl.BlockSpec((rows // 2, d), whole(0, 0)),
            pl.BlockSpec((rows // 2, d), whole(0, 0)),
        ],
        out_shape=[
            hbm((rows, width), bf16),
            hbm((rows, 128), f32),
            struct((rows // 2, d), f32),
            struct((rows // 2, d), bf16),
        ],
        compiler_params=params(28),
        cost_estimate=cost(32 * rows * rows * width, 6 * MIB, rows * rows * 2 * heads),
        name="attend",
    )(proj_q, *proj, *proj, seg_q, seg_k, w_out)


def attend_back_kernel(scale, heads, last, *refs):
    q_ref, k0_ref, k1_ref, v0_ref, v1_ref, segq_ref, segk_ref, lse_ref = refs[:8]
    one_refs, w_ref, refs = refs[8:10], refs[10], refs[11:]
    q = q_ref[...]
    rows, width = q.shape
    ks, vs = (k0_ref, k1_ref), (v0_ref, v1_ref)
    if last:
        dq0_ref, sumq_ref, dk_in, dv_in = refs[:4]
        g0_ref, g1_ref, sums_ref, keep_ref, dk_ref, dv_ref = refs[4:]
    else:
        dq0_ref, sumq_ref, dk_ref, dv_ref, keep_ref = refs
    lane = lax.broadcasted_iota(jnp.int32, (1, width), 1) // HEAD_DIM
    one = stack_rows(one_refs)
    keep_ref[...] = one
    grad = nt(one, w_ref[...]).astype(bf16)
    segq = segq_ref[...]
    masks = [jnp.where(segq == segk_ref[:, i * rows : (i + 1) * rows], 0.0, NEG) for i in range(2)]
    sc = jnp.asarray(scale, bf16)
    zero = jnp.zeros_like(q)
    dq = jnp.zeros((rows, width), f32)
    for h in range(heads):
        hit = lane == h
        qh = jnp.where(hit, q, zero) * sc
        gh = jnp.where(hit, grad, zero)
        lse = lse_ref[:, h : h + 1]
        probs = [jnp.exp(nt(qh, ks[i][...]) + masks[i] - lse) for i in range(2)]
        d_probs = [nt(gh, vs[i][...]) for i in range(2)]
        dot_sum = sum(jnp.sum(p * g, axis=1, keepdims=True) for p, g in zip(probs, d_probs))
        dq_h = 0.0
        for i in range(2):
            low = (probs[i] * (d_probs[i] - dot_sum)).astype(bf16)
            at = pl.ds(i * rows, rows)
            d_k, d_v = tn(low, qh), tn(probs[i].astype(bf16), gh)
            if h > 0:
                d_k, d_v = d_k + dk_ref[at, :], d_v + dv_ref[at, :]
            elif last:
                d_k, d_v = d_k + dk_in[at, :], d_v + dv_in[at, :]
            dk_ref[at, :] = d_k
            dv_ref[at, :] = d_v
            dq_h = dq_h + nn(low, ks[i][...])
        dq = jnp.where(hit, dq_h, dq)
    dq = dq * scale
    sum_q = jnp.sum(dq, axis=0, keepdims=True)
    if not last:
        dq0_ref[...] = dq.astype(bf16)
        sumq_ref[...] = sum_q
        return
    sums_ref[0:1, :] = sum_q + sumq_ref[...]
    sums_ref[1:2, :] = jnp.sum(dv_ref[...], axis=0, keepdims=True)
    g0_ref[:, :width] = dq0_ref[...]
    g1_ref[:, :width] = dq.astype(bf16)
    for i, ref in enumerate((g0_ref, g1_ref)):
        at = pl.ds(i * rows, rows)
        ref[:, width : 2 * width] = dk_ref[at, :].astype(bf16)
        ref[:, 2 * width :] = dv_ref[at, :].astype(bf16)


def attend_back(proj_q, proj, seg_q, seg_k, lse, one, w_out, scale, heads, earlier=None):
    rows, width = proj_q.shape[0], heads * HEAD_DIM
    d = w_out.shape[1]
    last = earlier is not None
    in_specs = (
        [pl.BlockSpec((rows, width), whole(0, 0))]
        + [pl.BlockSpec((rows, width), whole(0, 1))] * 2
        + [pl.BlockSpec((rows, width), whole(0, 2))] * 2
        + [
            pl.BlockSpec((rows, 1), whole(0, 0)),
            pl.BlockSpec((1, 2 * rows), whole(0, 0)),
            pl.BlockSpec((rows, 128), whole(0, 0)),
        ]
        + blocks_in(one)
        + [pl.BlockSpec((width, d), whole(0, 0))]
    )
    args = [proj_q, *proj, *proj, seg_q, seg_k, lse, *one, w_out]
    keep = [hbm((rows, d), bf16)]
    sums = [struct((2 * rows, width), f32)] * 2
    if last:
        in_specs += [pl.BlockSpec(e.shape, whole(0, 0)) for e in earlier]
        args += [*earlier]
        out_shape = [struct((rows, 3 * width), bf16)] * 2 + [struct((2, width), f32)] + keep
        scratch = [pltpu.VMEM(o.shape, f32) for o in sums]
    else:
        out_shape = [struct((rows, width), bf16), struct((1, width), f32)] + sums + keep
        scratch = []
    return pl.pallas_call(
        functools.partial(attend_back_kernel, scale, heads, last),
        grid=(1,),
        in_specs=in_specs,
        out_specs=[pl.BlockSpec(o.shape, whole(0, 0)) for o in out_shape],
        out_shape=out_shape,
        scratch_shapes=scratch,
        compiler_params=params(40),
        cost_estimate=cost(80 * rows * rows * width, 8 * MIB, rows * rows * 2 * heads),
        name="attend_back",
    )(*args)


def ffn_kernel(*refs):
    x_refs, refs = refs[:2], refs[2:]
    up_ref, down_ref, bias_ref, act_ref, slope_ref, mine_ref, theirs_ref, x, acc = refs
    step = pl.program_id(0)

    @pl.when(step == 0)
    def _():
        x[...] = stack_rows(x_refs)

    value, slope = gelu_parts(nn(x[...], up_ref[...]) + bias_ref[...])
    low = value.astype(bf16)
    act_ref[...] = low
    slope_ref[...] = slope
    add_up(step, nn(low, down_ref[...]), acc, mine_ref, theirs_ref)


def add_up(step, part, acc, mine_ref, theirs_ref):
    @pl.when(step == 0)
    def _():
        acc[...] = part

    @pl.when(step > 0)
    def _():
        acc[...] += part

    @pl.when(step == pl.num_programs(0) - 1)
    def _():
        half = acc.shape[0] // 2
        mine_ref[...] = acc[:half]
        theirs_ref[...] = acc[half:].astype(bf16)


def ffn(x, w_up, w_down, bias, tile=1024):
    rows, d = 2 * x[0].shape[0], x[0].shape[1]
    half = rows // 2
    ff = w_up.shape[1]
    moving = lambda i: (0, i)
    return pl.pallas_call(
        ffn_kernel,
        grid=(ff // tile,),
        in_specs=[
            *blocks_in(x),
            pl.BlockSpec((d, tile), moving),
            pl.BlockSpec((tile, d), lambda i: (i, 0)),
            pl.BlockSpec((1, tile), moving),
        ],
        out_specs=[
            pl.BlockSpec((rows, tile), moving),
            pl.BlockSpec((rows, tile), moving),
            pl.BlockSpec((half, d), whole(0, 0)),
            pl.BlockSpec((half, d), whole(0, 0)),
            pl.BlockSpec((rows, d), whole(0, 0)),
        ],
        out_shape=[
            hbm((rows, ff), bf16),
            hbm((rows, ff), f32),
            struct((half, d), f32),
            struct((half, d), bf16),
            hbm((rows, d), bf16),
        ],
        scratch_shapes=[pltpu.VMEM((rows, d), f32)],
        compiler_params=params(20),
        cost_estimate=cost(4 * rows * d * ff, 9 * MIB, rows * ff * 2),
        name="ffn",
    )(*x, w_up, w_down, bias)


def ffn_back_kernel(*refs):
    x_refs, refs = refs[:2], refs[2:]
    up_ref, down_ref, slope_ref, low_ref, sum_ref, mine_ref, theirs_ref, x, acc = refs
    step = pl.program_id(0)

    @pl.when(step == 0)
    def _():
        x[...] = stack_rows(x_refs)

    d_up = nt(x[...], down_ref[...]) * slope_ref[...]
    low = d_up.astype(bf16)
    low_ref[...] = low
    sum_ref[...] = jnp.sum(d_up, axis=0, keepdims=True)
    add_up(step, nt(low, up_ref[...]), acc, mine_ref, theirs_ref)


def ffn_back(x, w_up, w_down, slope, tile=1024):
    rows, d = 2 * x[0].shape[0], x[0].shape[1]
    half = rows // 2
    ff = w_up.shape[1]
    moving = lambda i: (0, i)
    return pl.pallas_call(
        ffn_back_kernel,
        grid=(ff // tile,),
        in_specs=[
            *blocks_in(x),
            pl.BlockSpec((d, tile), moving),
            pl.BlockSpec((tile, d), lambda i: (i, 0)),
            pl.BlockSpec((rows, tile), moving),
        ],
        out_specs=[
            pl.BlockSpec((rows, tile), moving),
            pl.BlockSpec((1, tile), moving),
            pl.BlockSpec((half, d), whole(0, 0)),
            pl.BlockSpec((half, d), whole(0, 0)),
            pl.BlockSpec((rows, d), whole(0, 0)),
        ],
        out_shape=[
            hbm((rows, ff), bf16),
            struct((1, ff), f32),
            struct((half, d), f32),
            struct((half, d), bf16),
            hbm((rows, d), bf16),
        ],
        scratch_shapes=[pltpu.VMEM((rows, d), f32)],
        compiler_params=params(20),
        cost_estimate=cost(4 * rows * d * ff, 9 * MIB),
        name="ffn_back",
    )(*x, w_up, w_down, *far(slope))


def lines_of(field, head_width, ff_width):
    return {"qkv": 3 * head_width, "out": head_width, "up": ff_width, "down": ff_width}[field]


def pack_kernel(fields, *refs):
    out_ref, at = refs[-1], 0
    for field, ref in zip(fields, refs):
        if field == "qkv":
            for j in range(3):
                for h in range(0, ref.shape[3], 128):
                    out_ref[at : at + 128, :] = ref[0, j, :, h : h + 128]
                    at += 128
        elif field == "up":
            for h in range(0, ref.shape[2], 128):
                out_ref[at : at + 128, :] = ref[0, :, h : h + 128]
                at += 128
        else:
            out_ref[at : at + ref.shape[1], :] = ref[0]
            at += ref.shape[1]


def pack(fields, args, layer):
    ins = [args[f] for f in fields]
    piece = args["up"].shape[1]
    if piece != 128:
        flat = {
            "qkv": lambda a: a[layer].transpose(0, 2, 1).reshape(-1, piece),
            "up": lambda a: a[layer].T,
            "out": lambda a: a[layer],
            "down": lambda a: a[layer],
        }
        return jnp.concatenate([flat[f](a) for f, a in zip(fields, ins)], 0)
    lines = sum(a.size // a.shape[0] for a in ins) // piece
    return pl.pallas_call(
        functools.partial(pack_kernel, fields),
        grid=(1,),
        in_specs=[
            pl.BlockSpec((1,) + a.shape[1:], whole(layer, *([0] * (a.ndim - 1)))) for a in ins
        ],
        out_specs=pl.BlockSpec((lines, piece), whole(0, 0)),
        out_shape=struct((lines, piece), bf16),
        compiler_params=params(8),
        cost_estimate=cost(0, 4 * lines * piece),
        name="pack",
    )(*far(*ins))


def maps_kernel(group_rows, lengths_ref, order_ref, spot_ref, src_ref, segc_ref, segr_ref):
    group, slot, rows = spot_ref[0], spot_ref[1], group_rows // 4
    base = group * SEQ_GRP
    lens = [lengths_ref[base + i] for i in range(SEQ_GRP)]
    starts = [0, lens[0], lens[0] + lens[1]]
    end, ends, shifts = 0, [], []
    for j in range(SEQ_GRP):
        seq = order_ref[base + j] - base
        length, start = lens[SEQ_GRP - 1], starts[SEQ_GRP - 1]
        for i in range(SEQ_GRP - 1):
            length = jnp.where(seq == i, lens[i], length)
            start = jnp.where(seq == i, starts[i], start)
        shifts.append(start - end)
        end = end + length
        ends.append(end)

    def turn(x):
        return x % 2 * 2 + x // 2

    def position(shape, axis):
        at = lax.broadcasted_iota(jnp.int32, shape, axis)
        return jnp.bitwise_xor(turn(at // rows), slot) * rows + at % rows

    def segment(place):
        return sum((place >= e).astype(jnp.int32) for e in ends)

    segr_ref[...] = segment(position(segr_ref.shape, 1))
    place = position(segc_ref.shape, 0)
    seg = segment(place)
    segc_ref[...] = seg
    source = place
    for j in range(SEQ_GRP):
        source = jnp.where(seg == j, place + shifts[j], source)
    src_ref[...] = turn(jnp.bitwise_xor(source // rows, slot)) * rows + source % rows


def maps(lengths, order, spot, group_rows):
    outs = [struct((group_rows, 1), jnp.int32)] * 2 + [struct((1, group_rows), jnp.int32)]
    return pl.pallas_call(
        functools.partial(maps_kernel, group_rows),
        grid=(1,),
        in_specs=[SCALARS] * 3,
        out_specs=blocks_in(outs),
        out_shape=outs,
        compiler_params=params(8),
        cost_estimate=cost(100 * group_rows, 8 * group_rows),
        name="maps",
    )(lengths, order, spot)


def tile_at(where_ref, spec):
    masked, d, core = spec
    d = jnp.bitwise_xor(where_ref[0], d) if masked else d
    tile = 2 * d + jnp.bitwise_xor(where_ref[1], core)
    return pl.ds(pl.multiple_of(tile * 128, 128), 128)


def tile_order(where, specs):
    return jnp.stack([2 * (where[0] ^ d if m else d) + (where[1] ^ core) for m, d, core in specs])


def place_kernel(fields, counts, specs, where_ref, *refs):
    ins, outs = refs[: len(counts)], refs[len(counts) :]
    k = 0
    for ref, count in zip(ins, counts):
        for i in range(count):
            here = tile_at(where_ref, specs[k])
            at = 0
            for field, out in zip(fields, outs):
                if field == "qkv":
                    for j in range(3):
                        for h in range(0, out.shape[2], 128):
                            out[j, here, h : h + 128] = ref[i, at : at + 128, :]
                            at += 128
                elif field == "up":
                    for h in range(0, out.shape[1], 128):
                        out[here, h : h + 128] = ref[i, at : at + 128, :]
                        at += 128
                else:
                    out[:, here] = ref[i, at : at + out.shape[0], :]
                    at += out.shape[0]
            k += 1


def place(fields, stacks, specs, where, head_width, ff_width):
    counts = [s.shape[0] for s in stacks]
    piece = stacks[0].shape[2]
    if piece != 128:
        tiles = jnp.take(jnp.concatenate(stacks, 0), jnp.argsort(tile_order(where, specs)), axis=0)
        flat = tiles.transpose(1, 0, 2).reshape(-1, D)
        found, at = [], 0
        for f in fields:
            lines = lines_of(f, head_width, ff_width)
            part = flat[at : at + lines]
            at += lines
            if f == "qkv":
                part = part.reshape(3, head_width, D).transpose(0, 2, 1)
            found.append(part.T if f == "up" else part)
        return found
    shapes = {
        "qkv": (3, D, head_width),
        "out": (head_width, D),
        "up": (D, ff_width),
        "down": (ff_width, D),
    }
    outs = [struct(shapes[f], bf16) for f in fields]
    return pl.pallas_call(
        functools.partial(place_kernel, fields, counts, specs),
        grid=(1,),
        in_specs=[SCALARS] + blocks_in(stacks),
        out_specs=blocks_in(outs),
        out_shape=outs,
        compiler_params=params(20),
        cost_estimate=cost(0, 4 * sum(s.size for s in stacks)),
        name="place",
    )(where, *stacks)


def grad_kernel(fields, counts, specs, where_ref, *refs):
    count = len(fields)
    ins, refs = refs[: 4 * count], refs[4 * count :]
    outs, bufs, sems = refs[: len(counts)], refs[len(counts) : -1], refs[-1]
    rows = ins[0].shape[0]
    copies = []
    for n in range(4 * count):
        there = bufs[n // 2].at[pl.ds(n % 2 * rows, rows), :]
        copies.append(pltpu.make_async_copy(ins[n], there, sems.at[n]))
        copies[-1].start()
    spots = [(out, i) for out, total in zip(outs, counts) for i in range(total)]
    at = 0
    for n, field in enumerate(fields):
        for copy in copies[4 * n : 4 * n + 4]:
            copy.wait()
        a_ref, b_ref = bufs[2 * n : 2 * n + 2]
        b = b_ref[...]
        lines = b.shape[1]
        for g in range(0, len(specs), 4):
            a = jnp.concatenate([a_ref[:, tile_at(where_ref, t)] for t in specs[g : g + 4]], 1)
            by_rows = field in ("qkv", "up")
            total = (tn(a, b) if by_rows else tn(b, a)).astype(bf16)
            for k, (out, i) in enumerate(spots[g : g + 4]):
                tile = slice(k * 128, (k + 1) * 128)
                if by_rows:
                    for h in range(0, lines, 128):
                        out[i, at + h : at + h + 128, :] = total[tile, h : h + 128]
                else:
                    out[i, at : at + lines, :] = total[:, tile]
        at += lines


def weight_grad(fields, pairs, specs, counts, where):
    flat = [r for a, b in pairs for r in (*a, *b)]
    lines = sum(b[0].shape[1] for _, b in pairs)
    rows = sum(b.shape[0] for b in pairs[0][1])
    piece = D // len(specs)
    if piece != 128:
        products = [dot(jnp.concatenate(b, 0), jnp.concatenate(a, 0), 0, 0) for a, b in pairs]
        tiles = jnp.concatenate(products, 0).astype(bf16).reshape(lines, len(specs), piece)
        tiles = jnp.take(tiles.transpose(1, 0, 2), tile_order(where, specs), axis=0)
        ends = [sum(counts[: i + 1]) for i in range(len(counts))]
        return [tiles[e - n : e] for e, n in zip(ends, counts)]
    kind = struct if len(counts) > 1 else hbm
    outs = [kind((n, lines, piece), bf16) for n in counts]
    bufs = [pltpu.VMEM((rows, r.shape[1]), bf16) for r in flat[::2]]
    return pl.pallas_call(
        functools.partial(grad_kernel, fields, counts, specs),
        grid=(1,),
        in_specs=[SCALARS] + [ROWS] * len(flat),
        out_specs=blocks_in(outs),
        out_shape=outs,
        scratch_shapes=bufs + [pltpu.SemaphoreType.DMA((len(flat),))],
        compiler_params=params(32),
        cost_estimate=cost(2 * rows * D * lines, 12 * MIB),
        name="weight_grad",
    )(where, *far(*flat))


def finish_kernel(fields, has_prev, keep_ref, got_ref, *refs):
    outs = refs[len(fields) if has_prev else 0 :]
    at = 0
    for field, out in zip(fields, outs):
        if field == "qkv":
            for j in range(3):
                for h in range(0, out.shape[3], 128):
                    out[0, j, :, h : h + 128] = keep_ref[at : at + 128, :] + got_ref[at : at + 128, :].astype(f32)
                    at += 128
        elif field == "up":
            for h in range(0, out.shape[2], 128):
                out[0, :, h : h + 128] = keep_ref[at : at + 128, :] + got_ref[at : at + 128, :].astype(f32)
                at += 128
        else:
            n = out.shape[1]
            out[0] = keep_ref[at : at + n, :] + got_ref[at : at + n, :].astype(f32)
            at += n


def finish(fields, keep, got, layer, prev, head_width, ff_width):
    piece = keep.shape[1]
    shapes = {
        "qkv": (3, piece, head_width),
        "out": (head_width, piece),
        "up": (piece, ff_width),
        "down": (ff_width, piece),
    }
    if piece != 128:
        total, at, found = keep + got.astype(f32), 0, []
        for n, f in enumerate(fields):
            lines = lines_of(f, head_width, ff_width)
            part = total[at : at + lines]
            at += lines
            if f == "qkv":
                part = part.reshape(3, head_width, piece).transpose(0, 2, 1)
            part = part.T if f == "up" else part
            base = jnp.zeros((LAYERS,) + shapes[f], f32) if prev is None else prev[n]
            found.append(base.at[layer].set(part))
        return found
    outs = [struct((LAYERS,) + shapes[f], f32) for f in fields]
    specs = [
        pl.BlockSpec((1,) + o.shape[1:], whole(layer, *([0] * (len(o.shape) - 1)))) for o in outs
    ]
    return pl.pallas_call(
        functools.partial(finish_kernel, fields, prev is not None),
        grid=(1,),
        in_specs=[pl.BlockSpec(keep.shape, whole(0, 0))] * 2
        + ([] if prev is None else [pl.BlockSpec(memory_space=pl.ANY)] * len(outs)),
        out_specs=specs,
        out_shape=outs,
        input_output_aliases={} if prev is None else {2 + n: n for n in range(len(outs))},
        compiler_params=params(16),
        cost_estimate=cost(0, 10 * keep.size),
        name="finish",
    )(keep, got, *([] if prev is None else prev))


def deal_kernel(src_ref, *refs):
    raw, outs = stack_rows(refs[:4]), refs[4:]
    rows = outs[0].shape[0]
    spot = lax.broadcasted_iota(jnp.int32, (1, raw.shape[0]), 1)
    hit = src_ref[...] == spot
    dealt = nn(jnp.where(hit, 1.0, 0.0).astype(bf16), raw)
    for i in range(4):
        outs[i][...] = dealt[i * rows : (i + 1) * rows].astype(bf16)
    outs[4][...] = dealt[:rows]


def deal_rows(src, raw):
    rows, d = raw[0].shape
    outs = [struct((rows, d), bf16)] * 4 + [struct((rows, d), f32)]
    outs = pl.pallas_call(
        deal_kernel,
        grid=(1,),
        in_specs=blocks_in((src, *raw)),
        out_specs=blocks_in(outs),
        out_shape=outs,
        compiler_params=params(20),
        cost_estimate=cost(32 * rows * rows * d, 6 * MIB),
        name="deal_rows",
    )(src, *raw)
    return outs[:2], outs[2:4], outs[4]


def total_of(refs):
    total = refs[0][...]
    for ref in refs[1:]:
        total = total + ref[...].astype(f32)
    return total


def norm_kernel(n_terms, bias_row, gain_row, shift_row, *refs):
    terms, (vec_ref, y_ref, low_ref, n_ref, r_ref) = refs[:n_terms], refs[n_terms:]
    row = lambda i: vec_ref[i : i + 1, :]
    v = total_of(terms) + row(bias_row)
    centred = v - jnp.mean(v, axis=-1, keepdims=True)
    r = lax.rsqrt(jnp.mean(centred * centred, axis=-1, keepdims=True) + EPS)
    n = centred * r
    y = n * row(gain_row) + row(shift_row)
    y_ref[...] = y
    low_ref[...] = y.astype(bf16)
    n_ref[...] = n
    r_ref[...] = r


def term_specs(terms):
    shape = terms[0].shape
    return [pl.BlockSpec(shape, whole(0, 0)) for _ in terms]


def norm(terms, vectors, bias_row, gain_row, shift_row):
    shape = terms[0].shape
    outs = [struct(shape, f32), struct(shape, bf16), hbm(shape, f32), struct((shape[0], 1), f32)]
    return pl.pallas_call(
        functools.partial(norm_kernel, len(terms), bias_row, gain_row, shift_row),
        grid=(1,),
        in_specs=term_specs(terms) + [full(vectors)],
        out_specs=blocks_in(outs),
        out_shape=outs,
        compiler_params=params(8),
        cost_estimate=cost(20 * terms[0].size, 2 * MIB),
        name="norm",
    )(*terms, vectors)


def norm_back_kernel(n_terms, gain_row, has_sums, *refs):
    terms, refs = refs[:n_terms], refs[n_terms:]
    n_ref, r_ref, vec_ref = refs[:3]
    dv_ref, low_ref, sums_ref = refs[-3:]
    d_out, n = total_of(terms), n_ref[...]
    dn = d_out * vec_ref[gain_row : gain_row + 1, :]
    dv = r_ref[...] * (
        dn - jnp.mean(dn, axis=-1, keepdims=True) - n * jnp.mean(dn * n, axis=-1, keepdims=True)
    )
    dv_ref[...] = dv
    low_ref[...] = dv.astype(bf16)
    for i, a in enumerate((d_out * n, d_out, dv)):
        column = jnp.sum(a, axis=0, keepdims=True)
        sums_ref[i : i + 1, :] = column + refs[3][i : i + 1, :] if has_sums else column


def norm_back(terms, n, r, vectors, gain_row, sums=None):
    shape = terms[0].shape
    outs = [struct(shape, f32), struct(shape, bf16), struct((3, shape[1]), f32)]
    more = [] if sums is None else [sums]
    return pl.pallas_call(
        functools.partial(norm_back_kernel, len(terms), gain_row, sums is not None),
        grid=(1,),
        in_specs=term_specs(terms) + blocks_in((n, r, vectors, *more)),
        out_specs=blocks_in(outs),
        out_shape=outs,
        compiler_params=params(8),
        cost_estimate=cost(20 * terms[0].size, 3 * MIB),
        name="norm_back",
    )(*terms, n, r, vectors, *more)


def dot(a, b, ca, cb):
    return lax.dot_general(a, b, (((ca,), (cb,)), ((), ())), preferred_element_type=f32)


def swap(a, axis):
    return lax.ppermute(a, axis, SWAP)


def flip_d(a, bit, n_d):
    return lax.ppermute(a, "d", [(i, i ^ (1 << bit)) for i in range(n_d)])


def to_home(a):
    return lax.ppermute(a, ("c", "zh"), [(1, 2), (2, 1)])


def after(a, *marks):
    return lax.optimization_barrier((a,) + marks)[0]


def send_rows(own):
    return (own, swap(own, "c")), swap(own, "zl")


def far_rows(far, *marks):
    if marks:
        far = after(far, *marks)
    return far, swap(far, "c")


def chip_sum(mine, theirs, *arrivals):
    other = swap(after(theirs, *arrivals) if arrivals else theirs, "c")
    return mine, other


def cross_sum(terms):
    total = (terms[0] + terms[1].astype(f32)).astype(bf16)
    return total, swap(total, "zl")


def masks_of(order):
    masks = [0]
    for bit in order:
        masks = masks + [m ^ (1 << bit) for m in masks]
    return masks


def absolute_specs(n_d):
    return [(False, d, core) for d in range(n_d) for core in range(2)]


def reduce_specs(n_d):
    bits = list(range(n_d.bit_length() - 1))
    half = n_d // 2
    order = []
    for core, masks in ((0, masks_of(bits)), (1, masks_of(bits[::-1]))):
        order += [(True, m, core) for m in masks[half:] + masks[:half]]
    return order


class Gather:
    def __init__(self, fields, args, layer, pos, where, n_d):
        self.fields, self.pos, self.where, self.n_d = fields, pos, where, n_d
        self.widths = args["out"].shape[1], args["down"].shape[1]
        self.tile = pack(fields, args, layer)
        self.crossed = []

    def cross(self, *marks, parts=1):
        lines = self.tile.shape[0] // parts
        part = self.tile[len(self.crossed) * lines : (len(self.crossed) + 1) * lines]
        self.crossed.append(swap(after(part, *marks) if marks else part, "zh"))
        return self.crossed[-1]

    def cores(self, *marks):
        _, c, zh, _ = self.pos
        same = c == zh
        crossed = jnp.concatenate(self.crossed, 0) if len(self.crossed) > 1 else self.crossed[0]
        crossed = after(crossed, *marks) if marks else crossed
        self.own = jnp.where(same, self.tile, crossed)
        self.other = swap(jnp.where(same, crossed, self.tile), "c")
        return self.other

    def collect(self, *marks):
        both = jnp.stack([self.own, self.other])
        if marks:
            both = after(both, *marks)
        self.stacks = [lax.all_gather(both, "d", axis=0, tiled=True)]
        self.specs = absolute_specs(self.n_d)
        return self.stacks[0]

    def weights(self):
        found = place(self.fields, self.stacks, self.specs, self.where, *self.widths)
        return dict(zip(self.fields, found))


class Reduce:
    def __init__(self, fields, pairs, pos, where, n_d, by_halves):
        self.fields, self.pos, self.n_d, self.step = fields, pos, n_d, 0
        specs = reduce_specs(n_d) if by_halves else absolute_specs(n_d)
        counts = [n_d // 2] * 4 if by_halves else [2 * n_d]
        self.stacks = weight_grad(fields, pairs, specs, counts, where)

    def collect(self, *marks):
        both = lax.psum_scatter(after(self.stacks[0], *marks), "d", scatter_dimension=0, tiled=True)
        self.first, self.second = both[0], both[1]
        return both

    def halve(self, *marks):
        bits = list(range(self.n_d.bit_length() - 1))
        if self.step == len(bits):
            return []
        if self.step == 0:
            self.sends, self.keeps = [self.stacks[0], self.stacks[2]], [self.stacks[1], self.stacks[3]]
        sends = lax.optimization_barrier((*self.sends, *marks))[:2] if marks else self.sends
        orders = (bits[::-1], bits)
        gots = [flip_d(a, o[self.step], self.n_d) for a, o in zip(sends, orders)]
        self.step += 1
        half = self.keeps[0].shape[0] // 2
        if self.step < len(bits):
            self.sends = [
                (k[half:].astype(f32) + g[half:].astype(f32)).astype(bf16)
                for k, g in zip(self.keeps, gots)
            ]
            self.keeps = [k[:half].astype(f32) + g[:half].astype(f32) for k, g in zip(self.keeps, gots)]
        else:
            self.first, self.second = (k[0].astype(f32) + g[0].astype(f32) for k, g in zip(self.keeps, gots))
        return gots

    def cores(self, *marks):
        while len(self.stacks) > 1 and self.step < self.n_d.bit_length() - 1:
            self.halve()
        second = self.second.astype(bf16)
        self.other = swap(after(second, *marks) if marks else second, "c")
        self.crossed, self.at = [], 0
        return self.other

    def cross(self, lines, *marks):
        _, c, zh, _ = self.pos
        same = c == zh
        part = slice(self.at, self.at + lines)
        send = jnp.where(same, self.other[part], self.first[part].astype(bf16))
        self.crossed.append(swap(after(send, *marks) if marks else send, "zh"))
        self.at += lines
        return self.crossed[-1]

    def finish(self, outs, layer, widths, *marks):
        _, c, zh, _ = self.pos
        got = jnp.concatenate(self.crossed, 0) if len(self.crossed) > 1 else self.crossed[0]
        first = after(self.first, *marks) if marks else self.first
        keep = jnp.where(c == zh, first.astype(f32), self.other.astype(f32))
        prev = None if outs[self.fields[0]] is None else [outs[f] for f in self.fields]
        outs.update(zip(self.fields, finish(self.fields, keep, got, layer, prev, *widths)))


def gather_small(own, pos, n_d):
    d, c, _, zl = pos
    cur = own
    for axis, me in (("zl", zl), ("c", c)):
        got = swap(cur, axis)
        cur = jnp.where(me == 0, jnp.concatenate([cur, got]), jnp.concatenate([got, cur]))
    for bit in range(n_d.bit_length() - 1):
        got = flip_d(cur, bit, n_d)
        mine = jnp.bitwise_and(jnp.right_shift(d, bit), 1)
        cur = jnp.where(mine == 0, jnp.concatenate([cur, got]), jnp.concatenate([got, cur]))
    return cur


def pick(a, at, axis):
    return lax.dynamic_index_in_dim(a, at, axis, keepdims=False)


def halve_small(cur, me, send):
    view = cur.reshape(2, -1, cur.shape[1])
    return pick(view, me, 0) + send(pick(view, 1 - me, 0))


def body(tokens, cotangent, lengths, order, w_qkv, w_out, w_up, w_down, gains, biases, up_bias):
    rows = tokens.shape[0]
    n_d = lax.axis_size("d")
    n_dev = n_d * 8
    head_width = D // 4
    heads = head_width // HEAD_DIM
    ff_width = FF // 4
    widths = (head_width, ff_width)
    scale = HEAD_DIM ** (-0.5)
    d, c, zh, zl = (lax.axis_index(a) for a in ALL)
    pos = (d, c, zh, zl)
    slot = 2 * c + zl
    where = jnp.stack([d, c]).astype(jnp.int32)
    stay = c == zh
    args = {"qkv": w_qkv.transpose(0, 2, 1, 3), "out": w_out, "up": w_up, "down": w_down}

    def gather(fields, layer):
        return Gather(fields, args, layer, pos, where, n_d)

    g_a0 = gather(("qkv", "out"), 0)
    a0_crossed = g_a0.cross()
    g_f0, g_a1, g_f1 = gather(("up", "down"), 0), gather(("qkv", "out"), 1), gather(("up", "down"), 1)
    small_own = jnp.concatenate([a.reshape(1, -1) for a in (gains, biases, up_bias)], 1)
    src, seg_col, seg_row = maps(
        lengths, order, jnp.stack([d * 2 + zh, slot]).astype(jnp.int32), 4 * rows
    )
    seg_near, seg_far = seg_col[: 2 * rows], seg_col[2 * rows :]
    g_a0.cores(src, small_own, *[g.tile for g in (g_f0, g_a1, g_f1)])
    g_a0.collect()
    raw_got = to_home(after(tokens, a0_crossed))
    raw = jnp.where(stay, tokens, raw_got)
    raw_near, raw_far = send_rows(raw)
    f0_crossed = g_f0.cross(raw_got)
    x_near, x_far, hidden = deal_rows(src, [*raw_near, *far_rows(raw_far)])
    small_near = gather_small(after(small_own, g_a0.other), pos, n_d)
    small_far = swap(small_near, "zh")
    width = D // n_dev
    up_width = FF // n_dev
    n_vec = LAYERS * 8
    small_all = jnp.where(zh == 0, jnp.stack([small_near, small_far]), jnp.stack([small_far, small_near]))
    small_all = small_all.reshape(2, n_d * 2, 2, -1)
    vectors = small_all[..., : n_vec * width].reshape(2, n_d * 2, 2, n_vec, width)
    vectors = vectors.transpose(3, 1, 0, 2, 4).reshape(n_vec, D)
    ups = small_all[..., n_vec * width :].reshape(2, n_d * 2, 2, LAYERS, up_width)
    ups = ups.transpose(3, 1, 0, 2, 4).reshape(LAYERS, FF)
    ups = lax.dynamic_slice(ups, (0, slot * ff_width), (LAYERS, ff_width))
    own_vectors = lax.dynamic_slice(vectors, (0, slot * head_width), (n_vec, head_width))
    gain_row = lambda layer, i: 2 * layer + i
    bias_row = lambda layer, i: 2 * LAYERS + 6 * layer + i
    f0_other = g_f0.cores(x_near[0])
    g_f0.collect()
    a1_crossed = g_a1.cross(f0_other)
    weights = [g_a0.weights(), {}]

    kept = []
    x_sent = None
    for layer in range(LAYERS):
        first = layer == 0
        w = weights[layer]
        q_row, v_row = bias_row(layer, 0), bias_row(layer, 1)
        add = jnp.concatenate(
            [
                own_vectors[q_row : q_row + 1],
                jnp.zeros((1, head_width), f32),
                own_vectors[v_row : v_row + 1],
            ],
            1,
        )
        proj_near, keep_near = project(x_near, w["qkv"], add)
        if not first:
            x_far = far_rows(x_sent, keep_near)
        proj_far, keep_far = project(x_far, w["qkv"], add)
        proj = (proj_near, proj_far)
        x_kept = (keep_near, keep_far)
        due = [a1_crossed] if first else []
        if not first:
            cot_got = to_home(after(cotangent, proj_far))
        att_far, lse_far, mine, theirs = attend(
            proj_far, proj, seg_far, seg_row, w["out"], scale, heads
        )
        chip, crossed = cross_sum(chip_sum(mine, theirs, *due))
        att_near, lse_near, mine, theirs = attend(
            after(proj_near, chip), proj, seg_near, seg_row, w["out"], scale, heads
        )
        due = [crossed] if first else [crossed, cot_got]
        terms = (*chip_sum(mine, theirs, *due), crossed)
        at = [bias_row(layer, 2), gain_row(layer, 0), bias_row(layer, 3)]
        normed, low, n_one, r_one = norm((hidden, *terms), vectors, *at)
        n_near, n_sent = send_rows(low)
        due = [n_sent]
        if first:
            w.update(g_f0.weights())
            g_a1.cores(low)
            g_a1.collect()
            due += [g_f1.cross(low, parts=2)]
        else:
            w.update(g_f1.weights())
        u_bias = ups[layer : layer + 1]
        act_near, slope_near, mine_near, theirs_near, keep_near = ffn(n_near, w["up"], w["down"], u_bias)
        near = chip_sum(mine_near, theirs_near, *due)
        n_far = far_rows(n_sent, keep_near)
        due = []
        if first:
            due += [g_f1.cross(keep_near, parts=2)]
        else:
            cot = jnp.where(stay, cotangent, cot_got)
            cot_near, cot_sent = send_rows(after(cot, keep_near))
            due += [cot_sent]
        act_far, slope_far, mine, theirs, keep_far = ffn(n_far, w["up"], w["down"], u_bias)
        chip, crossed = cross_sum(chip_sum(mine, theirs, *due))
        if first:
            g_f1.cores(chip)
            g_f1.collect()
        at = [bias_row(layer, 4), gain_row(layer, 1), bias_row(layer, 5)]
        hidden, low, n_two, r_two = norm((normed, *near, crossed), vectors, *at)
        kept.append(
            dict(
                x=x_kept, proj=proj, lse=(lse_near, lse_far), att=(att_near, att_far),
                one=(n_one, r_one), n=(keep_near, keep_far), slope=(slope_near, slope_far),
                act=(act_near, act_far), two=(n_two, r_two),
            )
        )
        if first:
            weights[1].update(g_a1.weights())
            x_near, x_sent = send_rows(low)
    last_low = low

    deal = (src[:rows] == jnp.arange(4 * rows, dtype=jnp.int32)[None, :]).astype(bf16)
    cot = jnp.concatenate([*cot_near, *far_rows(cot_sent)], 0)
    valid = (seg_near[:rows] < SEQ_GRP).astype(f32)
    grad_y = (dot(deal, cot, 1, 0) * valid,)
    vector_sums = [None] * LAYERS
    up_sums = [None] * LAYERS
    late = None

    def spot(vec, full_width):
        return lax.dynamic_update_slice(jnp.zeros((1, full_width), f32), vec, (0, slot * vec.shape[1]))

    for layer in reversed(range(LAYERS)):
        w, k = weights[layer], kept[layer]
        d_two, low, sums_two = norm_back(grad_y, *k["two"], vectors, gain_row(layer, 1))
        two_near, two_sent = send_rows(low)
        if late:
            late[0].cores(low)
        up_near, sum_near, mine_near, theirs_near, keep_two_near = ffn_back(
            two_near, w["up"], w["down"], k["slope"][0]
        )
        near = chip_sum(mine_near, theirs_near, two_sent)
        two_far = far_rows(two_sent, up_near)
        due = []
        if late:
            due += [late[0].cross(ff_width, up_near)]
        up_far, sum_far, mine, theirs, keep_two_far = ffn_back(
            two_far, w["up"], w["down"], k["slope"][1]
        )
        chip, crossed = cross_sum(chip_sum(mine, theirs, *due))
        two_pair = ((keep_two_near, keep_two_far), (k["act"][0], after(k["act"][1], chip)))
        up_pair = (k["n"], (up_near, after(up_far, chip)))
        due = []
        if late:
            due += [late[0].cross(ff_width, chip)]
            r_down = Reduce(("down",), (two_pair,), pos, where, n_d, True)
            down_got = r_down.halve()
            up_pair = (up_pair[0], (up_near, after(up_far, r_down.stacks[0])))
            r_ff = Reduce(("up",), (up_pair,), pos, where, n_d, True)
            up_got = r_ff.halve()
        else:
            r_ff = Reduce(("up", "down"), (up_pair, two_pair), pos, where, n_d, False)
        d_two = after(d_two, r_ff.stacks[0], *due)
        d_one, low, sums_one = norm_back((d_two, *near, crossed), *k["one"], vectors, gain_row(layer, 0))
        one_near, one_sent = send_rows(low)
        if not late:
            r_ff.collect(low)
        *earlier, keep_one_near = attend_back(
            k["proj"][0], k["proj"], seg_near, seg_row, k["lse"][0], one_near, w["out"], scale, heads
        )
        one_far = far_rows(one_sent, earlier[0])
        due = []
        if late:
            earlier[0] = after(earlier[0], *down_got, *up_got)
            due += r_down.halve(earlier[0]) + r_ff.halve(earlier[0])
            late[1].cores(earlier[0])
            due += [late[1].cross(4 * head_width, earlier[0])]
        else:
            mixed_got = to_home(after(last_low, earlier[0]))
            due += [mixed_got]
        d_near, d_far, head_sums, keep_one_far = attend_back(
            k["proj"][1], k["proj"], seg_far, seg_row, k["lse"][1], one_far, w["out"], scale, heads,
            earlier,
        )
        d_far = after(d_far, *due)
        mine, theirs = input_grad(d_far, w["qkv"])
        chip, crossed = cross_sum(chip_sum(mine, theirs))
        att_pairs = ((k["x"], (d_near, after(d_far, chip))), ((keep_one_near, keep_one_far), k["att"]))
        if late:
            r_att = Reduce(("qkv", "out"), att_pairs, pos, where, n_d, True)
            r_att.halve()
            d_near = after(d_near, r_att.stacks[0])
            near = chip_sum(*input_grad(d_near, w["qkv"]))
        else:
            near = chip_sum(*input_grad(after(d_near, chip), w["qkv"]))
            r_att = Reduce(("qkv", "out"), att_pairs, pos, where, n_d, False)
            late = (r_ff, r_att)
            d_one = after(d_one, r_att.stacks[0])
            r_att.collect(crossed)
        grad_y = (d_one, *near, crossed)
        vector_sums[layer] = (
            [sums_one[0:1], sums_two[0:1]],
            [
                spot(head_sums[0:1], D), spot(head_sums[1:2], D), sums_one[2:3],
                sums_one[1:2], sums_two[2:3], sums_two[1:2],
            ],
        )
        up_sums[layer] = spot(sum_near + sum_far, FF)

    r_down.cores(d_far)
    down_crossed = r_down.cross(ff_width)
    r_ff.cores(d_far)
    up_crossed = r_ff.cross(ff_width, down_crossed)
    att_got = r_att.halve(down_crossed)
    base, mine, other, crossed = grad_y
    own_grad = (base + mine + other.astype(f32) + crossed.astype(f32)).astype(bf16)
    grad_got = to_home(after(own_grad, *att_got))
    r_att.cores(up_crossed)
    r_att.cross(4 * head_width)
    outs = {f: None for f in ("qkv", "out", "up", "down")}
    for r in late:
        r.finish(outs, 1, widths, *att_got)
    r_down.finish(outs, 0, widths, *att_got)
    r_ff.finish(outs, 0, widths, *att_got)
    r_att.finish(outs, 0, widths)
    tokens_grad = jnp.where(stay, own_grad, grad_got).astype(f32)
    mixed = jnp.where(stay, last_low, after(mixed_got, *att_got))

    terms = jnp.concatenate(
        [g for s in vector_sums for g in s[0]] + [b for s in vector_sums for b in s[1]], 0
    )
    small = jnp.concatenate(
        [
            terms.reshape(n_vec, n_dev, width).transpose(1, 0, 2).reshape(n_dev, n_vec * width),
            jnp.concatenate(up_sums, 0)
            .reshape(LAYERS, n_dev, up_width)
            .transpose(1, 0, 2)
            .reshape(n_dev, LAYERS * up_width),
        ],
        1,
    )
    n_small = small.shape[1]
    small = after(small, *att_got).reshape(n_d, 2, 4 * n_small)
    small = pick(small, c, 1) + swap(pick(small, 1 - c, 1), "c")
    small = small.reshape(n_d, 2, 2, n_small)
    small = pick(small, zl, 2) + swap(pick(small, 1 - zl, 2), "zl")
    small = small.reshape(n_d, 2 * n_small)
    for bit in reversed(range(n_d.bit_length() - 1)):
        mine = jnp.bitwise_and(jnp.right_shift(d, bit), 1)
        small = halve_small(small, mine, lambda a, bit=bit: flip_d(a, bit, n_d))
    small_sum = halve_small(small.reshape(2, n_small), zh, lambda a: swap(a, "zh"))
    n_gain = LAYERS * 2 * width
    g_gains = small_sum[:, :n_gain].reshape(LAYERS, 2, width)
    g_biases = small_sum[:, n_gain : n_vec * width].reshape(LAYERS, 6, width)
    g_upb = small_sum[:, n_vec * width :].reshape(LAYERS, up_width)
    g_qkv = outs["qkv"].transpose(0, 2, 1, 3)
    return mixed, tokens_grad, g_qkv, outs["out"], outs["up"], outs["down"], g_gains, g_biases, g_upb


def solution(mesh):
    n_dp, n_t = mesh.shape["dp"], mesh.shape["tensor"]
    fine = Mesh(mesh.devices.reshape(n_dp // 2, 2, n_t // 2, 2), ALL)
    dp, t = ("d", "c"), ("zh", "zl")
    return jax.shard_map(
        body,
        mesh=fine,
        in_specs=(
            P(ALL, None),
            P(ALL, None),
            P(),
            P(),
            P(None, dp, None, t),
            P(None, t, dp),
            P(None, dp, t),
            P(None, t, dp),
            P(None, None, ALL),
            P(None, None, ALL),
            P(None, ALL),
        ),
        out_specs=(
            P(ALL, None),
            P(ALL, None),
            P(None, dp, None, t),
            P(None, t, dp),
            P(None, dp, t),
            P(None, t, dp),
            P(None, None, ALL),
            P(None, None, ALL),
            P(None, ALL),
        ),
        check_vma=False,
    )
```

```python
import functools

import jax
import jax.numpy as jnp
from jax import lax
from jax.experimental import pallas as pl
from jax.experimental.pallas import tpu as pltpu
from jax.sharding import Mesh, PartitionSpec as P

D = 1024
HEAD_DIM = 64
FF = 4096
LAYERS = 2
SEQ_GRP = 3

EPS = 1e-05
NEG = -1e30
ALL = ("d", "c", "zh", "zl")
SWAP = [(0, 1), (1, 0)]
bf16 = jnp.bfloat16
f32 = jnp.float32
MIB = 1 << 20

TAIL_STEP = 0.24
TAIL = (
    0.0912286469891869,
    0.14294535326111468,
    -0.11556713177962434,
    0.5630756863681534,
    -0.5892310046041954,
    0.5271447780474939,
    -0.11959632556906954,
)
INV_SQRT_2PI = 0.3989422804014327


def nn(a, b):
    return lax.dot_general(a, b, (((1,), (0,)), ((), ())), preferred_element_type=f32)


def nt(a, b):
    return lax.dot_general(a, b, (((1,), (1,)), ((), ())), preferred_element_type=f32)


def tn(a, b):
    return lax.dot_general(a, b, (((0,), (0,)), ((), ())), preferred_element_type=f32)


def stack_rows(refs):
    return jnp.concatenate([r[...] for r in refs], 0)


def params(limit):
    return pltpu.CompilerParams(vmem_limit_bytes=limit * MIB)


def cost(flops, nbytes, exps=0):
    return pl.CostEstimate(flops=int(flops), bytes_accessed=int(nbytes), transcendentals=int(exps))


def struct(shape, dtype):
    return jax.ShapeDtypeStruct(shape, dtype)


def hbm(shape, dtype):
    return pltpu.HBM(shape, dtype)


def far(*arrays):
    return [pltpu.with_memory_space_constraint(a, pltpu.HBM) for a in arrays]


SCALARS = pl.BlockSpec(memory_space=pltpu.SMEM)
ROWS = pl.BlockSpec(memory_space=pltpu.HBM)


def full(a):
    shape = a.shape
    return pl.BlockSpec(shape, lambda *_: (0,) * len(shape))


def blocks_in(arrays):
    return [full(a) for a in arrays]


def gelu_parts(u):
    z = jnp.abs(u)
    bell = jnp.exp(-0.5 * (u * u))
    below = 1.0 + TAIL_STEP * z
    t = pl.reciprocal(below, approx=True)
    t = t * (2.0 - below * t)
    poly = jnp.full_like(t, TAIL[-1])
    for coef in TAIL[-2::-1]:
        poly = poly * t + coef
    tail = bell * (poly * t)
    phi = jnp.where(u > 0.0, 1.0 - tail, tail)
    return u * phi, phi + u * (INV_SQRT_2PI * bell)


def whole(*at):
    return lambda i: at


def project_kernel(*refs):
    x_refs, (w_ref, add_ref, out_ref, x_ref) = refs[:2], refs[2:]

    @pl.when(pl.program_id(0) == 0)
    def _():
        x_ref[...] = stack_rows(x_refs)

    out_ref[...] = (nn(x_ref[...], w_ref[0]) + add_ref[...]).astype(bf16)


def project(x, w_qkv, add):
    rows = 2 * x[0].shape[0]
    _, d, width = w_qkv.shape
    return pl.pallas_call(
        project_kernel,
        grid=(3,),
        in_specs=blocks_in(x)
        + [pl.BlockSpec((1, d, width), lambda i: (i, 0, 0)), pl.BlockSpec((1, width), lambda i: (0, i))],
        out_specs=[pl.BlockSpec((rows, width), lambda i: (0, i)), pl.BlockSpec((rows, d), whole(0, 0))],
        out_shape=[struct((rows, 3 * width), bf16), hbm((rows, d), bf16)],
        compiler_params=params(12),
        cost_estimate=cost(6 * rows * d * width, 4 * MIB),
        name="project",
    )(*x, w_qkv, add)


def input_grad_kernel(g_ref, w_ref, mine_ref, theirs_ref):
    width = w_ref.shape[2]
    part = sum(nt(g_ref[:, j * width : (j + 1) * width], w_ref[j]) for j in range(3))
    half = part.shape[0] // 2
    mine_ref[...] = part[:half]
    theirs_ref[...] = part[half:].astype(bf16)


def input_grad(d_proj, w_qkv):
    rows = d_proj.shape[0]
    _, d, width = w_qkv.shape
    outs = [struct((rows // 2, d), f32), struct((rows // 2, d), bf16)]
    return pl.pallas_call(
        input_grad_kernel,
        grid=(1,),
        in_specs=blocks_in((d_proj, w_qkv)),
        out_specs=blocks_in(outs),
        out_shape=outs,
        compiler_params=params(16),
        cost_estimate=cost(6 * rows * d * width, 4 * MIB),
        name="input_grad",
    )(d_proj, w_qkv)


def attend_kernel(scale, heads, q_ref, k0_ref, k1_ref, v0_ref, v1_ref, segq_ref, segk_ref, w_ref, *outs):
    att_ref, lse_ref, mine_ref, theirs_ref = outs
    q = q_ref[...] * jnp.asarray(scale, bf16)
    rows, width = q.shape
    ks, vs = (k0_ref, k1_ref), (v0_ref, v1_ref)
    kv_rows = k0_ref.shape[0]
    lane = lax.broadcasted_iota(jnp.int32, (1, width), 1) // HEAD_DIM
    stat_lane = lax.broadcasted_iota(jnp.int32, (1, 128), 1)
    out = jnp.zeros((rows, width), f32)
    lse = jnp.zeros((rows, 128), f32)
    segq = segq_ref[...]
    masks = [
        jnp.where(segq == segk_ref[:, i * kv_rows : (i + 1) * kv_rows], 0.0, NEG) for i in range(2)
    ]
    for h in range(heads):
        hit = lane == h
        qh = jnp.where(hit, q, jnp.zeros_like(q))
        scores = [nt(qh, ks[i][...]) + masks[i] for i in range(2)]
        peak = jnp.maximum(*[jnp.max(s, axis=1, keepdims=True) for s in scores])
        exps = [jnp.exp(s - peak) for s in scores]
        total = sum(jnp.sum(e, axis=1, keepdims=True) for e in exps)
        inv = 1.0 / total
        head_out = sum(nn((exps[i] * inv).astype(bf16), vs[i][...]) for i in range(2))
        out = jnp.where(hit, head_out, out)
        lse = jnp.where(stat_lane == h, peak + jnp.log(total), lse)
    low = out.astype(bf16)
    att_ref[...] = low
    lse_ref[...] = lse
    part = nn(low, w_ref[...])
    half = rows // 2
    mine_ref[...] = part[:half]
    theirs_ref[...] = part[half:].astype(bf16)


def attend(proj_q, proj, seg_q, seg_k, w_out, scale, heads):
    rows, width = proj_q.shape[0], heads * HEAD_DIM
    d = w_out.shape[1]
    return pl.pallas_call(
        functools.partial(attend_kernel, scale, heads),
        grid=(1,),
        in_specs=[pl.BlockSpec((rows, width), whole(0, 0))]
        + [pl.BlockSpec((rows, width), whole(0, 1))] * 2
        + [pl.BlockSpec((rows, width), whole(0, 2))] * 2
        + [
            pl.BlockSpec((rows, 1), whole(0, 0)),
            pl.BlockSpec((1, 2 * rows), whole(0, 0)),
            pl.BlockSpec((width, d), whole(0, 0)),
        ],
        out_specs=[
            pl.BlockSpec((rows, width), whole(0, 0)),
            pl.BlockSpec((rows, 128), whole(0, 0)),
            pl.BlockSpec((rows // 2, d), whole(0, 0)),
            pl.BlockSpec((rows // 2, d), whole(0, 0)),
        ],
        out_shape=[
            hbm((rows, width), bf16),
            hbm((rows, 128), f32),
            struct((rows // 2, d), f32),
            struct((rows // 2, d), bf16),
        ],
        compiler_params=params(28),
        cost_estimate=cost(32 * rows * rows * width, 6 * MIB, rows * rows * 2 * heads),
        name="attend",
    )(proj_q, *proj, *proj, seg_q, seg_k, w_out)


def attend_back_kernel(scale, heads, last, *refs):
    q_ref, k0_ref, k1_ref, v0_ref, v1_ref, segq_ref, segk_ref, lse_ref = refs[:8]
    one_refs, w_ref, refs = refs[8:10], refs[10], refs[11:]
    q = q_ref[...]
    rows, width = q.shape
    ks, vs = (k0_ref, k1_ref), (v0_ref, v1_ref)
    if last:
        dq0_ref, sumq_ref, dk_in, dv_in = refs[:4]
        g0_ref, g1_ref, sums_ref, keep_ref, dk_ref, dv_ref = refs[4:]
    else:
        dq0_ref, sumq_ref, dk_ref, dv_ref, keep_ref = refs
    lane = lax.broadcasted_iota(jnp.int32, (1, width), 1) // HEAD_DIM
    one = stack_rows(one_refs)
    keep_ref[...] = one
    grad = nt(one, w_ref[...]).astype(bf16)
    segq = segq_ref[...]
    masks = [jnp.where(segq == segk_ref[:, i * rows : (i + 1) * rows], 0.0, NEG) for i in range(2)]
    sc = jnp.asarray(scale, bf16)
    zero = jnp.zeros_like(q)
    dq = jnp.zeros((rows, width), f32)
    for h in range(heads):
        hit = lane == h
        qh = jnp.where(hit, q, zero) * sc
        gh = jnp.where(hit, grad, zero)
        lse = lse_ref[:, h : h + 1]
        probs = [jnp.exp(nt(qh, ks[i][...]) + masks[i] - lse) for i in range(2)]
        d_probs = [nt(gh, vs[i][...]) for i in range(2)]
        dot_sum = sum(jnp.sum(p * g, axis=1, keepdims=True) for p, g in zip(probs, d_probs))
        dq_h = 0.0
        for i in range(2):
            low = (probs[i] * (d_probs[i] - dot_sum)).astype(bf16)
            at = pl.ds(i * rows, rows)
            d_k, d_v = tn(low, qh), tn(probs[i].astype(bf16), gh)
            if h > 0:
                d_k, d_v = d_k + dk_ref[at, :], d_v + dv_ref[at, :]
            elif last:
                d_k, d_v = d_k + dk_in[at, :], d_v + dv_in[at, :]
            dk_ref[at, :] = d_k
            dv_ref[at, :] = d_v
            dq_h = dq_h + nn(low, ks[i][...])
        dq = jnp.where(hit, dq_h, dq)
    dq = dq * scale
    sum_q = jnp.sum(dq, axis=0, keepdims=True)
    if not last:
        dq0_ref[...] = dq.astype(bf16)
        sumq_ref[...] = sum_q
        return
    sums_ref[0:1, :] = sum_q + sumq_ref[...]
    sums_ref[1:2, :] = jnp.sum(dv_ref[...], axis=0, keepdims=True)
    g0_ref[:, :width] = dq0_ref[...]
    g1_ref[:, :width] = dq.astype(bf16)
    for i, ref in enumerate((g0_ref, g1_ref)):
        at = pl.ds(i * rows, rows)
        ref[:, width : 2 * width] = dk_ref[at, :].astype(bf16)
        ref[:, 2 * width :] = dv_ref[at, :].astype(bf16)


def attend_back(proj_q, proj, seg_q, seg_k, lse, one, w_out, scale, heads, earlier=None):
    rows, width = proj_q.shape[0], heads * HEAD_DIM
    d = w_out.shape[1]
    last = earlier is not None
    in_specs = (
        [pl.BlockSpec((rows, width), whole(0, 0))]
        + [pl.BlockSpec((rows, width), whole(0, 1))] * 2
        + [pl.BlockSpec((rows, width), whole(0, 2))] * 2
        + [
            pl.BlockSpec((rows, 1), whole(0, 0)),
            pl.BlockSpec((1, 2 * rows), whole(0, 0)),
            pl.BlockSpec((rows, 128), whole(0, 0)),
        ]
        + blocks_in(one)
        + [pl.BlockSpec((width, d), whole(0, 0))]
    )
    args = [proj_q, *proj, *proj, seg_q, seg_k, lse, *one, w_out]
    keep = [hbm((rows, d), bf16)]
    sums = [struct((2 * rows, width), f32)] * 2
    if last:
        in_specs += [pl.BlockSpec(e.shape, whole(0, 0)) for e in earlier]
        args += [*earlier]
        out_shape = [struct((rows, 3 * width), bf16)] * 2 + [struct((2, width), f32)] + keep
        scratch = [pltpu.VMEM(o.shape, f32) for o in sums]
    else:
        out_shape = [struct((rows, width), bf16), struct((1, width), f32)] + sums + keep
        scratch = []
    return pl.pallas_call(
        functools.partial(attend_back_kernel, scale, heads, last),
        grid=(1,),
        in_specs=in_specs,
        out_specs=[pl.BlockSpec(o.shape, whole(0, 0)) for o in out_shape],
        out_shape=out_shape,
        scratch_shapes=scratch,
        compiler_params=params(40),
        cost_estimate=cost(80 * rows * rows * width, 8 * MIB, rows * rows * 2 * heads),
        name="attend_back",
    )(*args)


def ffn_kernel(*refs):
    x_refs, refs = refs[:2], refs[2:]
    up_ref, down_ref, bias_ref, act_ref, slope_ref, mine_ref, theirs_ref, x, acc = refs
    step = pl.program_id(0)

    @pl.when(step == 0)
    def _():
        x[...] = stack_rows(x_refs)

    value, slope = gelu_parts(nn(x[...], up_ref[...]) + bias_ref[...])
    low = value.astype(bf16)
    act_ref[...] = low
    slope_ref[...] = slope
    add_up(step, nn(low, down_ref[...]), acc, mine_ref, theirs_ref)


def add_up(step, part, acc, mine_ref, theirs_ref):
    @pl.when(step == 0)
    def _():
        acc[...] = part

    @pl.when(step > 0)
    def _():
        acc[...] += part

    @pl.when(step == pl.num_programs(0) - 1)
    def _():
        half = acc.shape[0] // 2
        mine_ref[...] = acc[:half]
        theirs_ref[...] = acc[half:].astype(bf16)


def ffn(x, w_up, w_down, bias, tile=1024):
    rows, d = 2 * x[0].shape[0], x[0].shape[1]
    half = rows // 2
    ff = w_up.shape[1]
    moving = lambda i: (0, i)
    return pl.pallas_call(
        ffn_kernel,
        grid=(ff // tile,),
        in_specs=[
            *blocks_in(x),
            pl.BlockSpec((d, tile), moving),
            pl.BlockSpec((tile, d), lambda i: (i, 0)),
            pl.BlockSpec((1, tile), moving),
        ],
        out_specs=[
            pl.BlockSpec((rows, tile), moving),
            pl.BlockSpec((rows, tile), moving),
            pl.BlockSpec((half, d), whole(0, 0)),
            pl.BlockSpec((half, d), whole(0, 0)),
            pl.BlockSpec((rows, d), whole(0, 0)),
        ],
        out_shape=[
            hbm((rows, ff), bf16),
            hbm((rows, ff), f32),
            struct((half, d), f32),
            struct((half, d), bf16),
            hbm((rows, d), bf16),
        ],
        scratch_shapes=[pltpu.VMEM((rows, d), f32)],
        compiler_params=params(20),
        cost_estimate=cost(4 * rows * d * ff, 9 * MIB, rows * ff * 2),
        name="ffn",
    )(*x, w_up, w_down, bias)


def ffn_back_kernel(*refs):
    x_refs, refs = refs[:2], refs[2:]
    up_ref, down_ref, slope_ref, low_ref, sum_ref, mine_ref, theirs_ref, x, acc = refs
    step = pl.program_id(0)

    @pl.when(step == 0)
    def _():
        x[...] = stack_rows(x_refs)

    d_up = nt(x[...], down_ref[...]) * slope_ref[...]
    low = d_up.astype(bf16)
    low_ref[...] = low
    sum_ref[...] = jnp.sum(d_up, axis=0, keepdims=True)
    add_up(step, nt(low, up_ref[...]), acc, mine_ref, theirs_ref)


def ffn_back(x, w_up, w_down, slope, tile=1024):
    rows, d = 2 * x[0].shape[0], x[0].shape[1]
    half = rows // 2
    ff = w_up.shape[1]
    moving = lambda i: (0, i)
    return pl.pallas_call(
        ffn_back_kernel,
        grid=(ff // tile,),
        in_specs=[
            *blocks_in(x),
            pl.BlockSpec((d, tile), moving),
            pl.BlockSpec((tile, d), lambda i: (i, 0)),
            pl.BlockSpec((rows, tile), moving),
        ],
        out_specs=[
            pl.BlockSpec((rows, tile), moving),
            pl.BlockSpec((1, tile), moving),
            pl.BlockSpec((half, d), whole(0, 0)),
            pl.BlockSpec((half, d), whole(0, 0)),
            pl.BlockSpec((rows, d), whole(0, 0)),
        ],
        out_shape=[
            hbm((rows, ff), bf16),
            struct((1, ff), f32),
            struct((half, d), f32),
            struct((half, d), bf16),
            hbm((rows, d), bf16),
        ],
        scratch_shapes=[pltpu.VMEM((rows, d), f32)],
        compiler_params=params(20),
        cost_estimate=cost(4 * rows * d * ff, 9 * MIB),
        name="ffn_back",
    )(*x, w_up, w_down, *far(slope))


def lines_of(field, head_width, ff_width):
    return {"qkv": 3 * head_width, "out": head_width, "up": ff_width, "down": ff_width}[field]


def pack_kernel(fields, *refs):
    out_ref, at = refs[-1], 0
    for field, ref in zip(fields, refs):
        if field == "qkv":
            for j in range(3):
                for h in range(0, ref.shape[3], 128):
                    out_ref[at : at + 128, :] = ref[0, j, :, h : h + 128]
                    at += 128
        elif field == "up":
            for h in range(0, ref.shape[2], 128):
                out_ref[at : at + 128, :] = ref[0, :, h : h + 128]
                at += 128
        else:
            out_ref[at : at + ref.shape[1], :] = ref[0]
            at += ref.shape[1]


def pack(parts, args):
    fields = [f for f, _ in parts]
    ins = [args[f] for f in fields]
    piece = args["up"].shape[1]
    if piece != 128:
        flat = {
            "qkv": lambda a, l: a[l].transpose(0, 2, 1).reshape(-1, piece),
            "up": lambda a, l: a[l].T,
            "out": lambda a, l: a[l],
            "down": lambda a, l: a[l],
        }
        return jnp.concatenate([flat[f](args[f], l) for f, l in parts], 0)
    lines = sum(a.size // a.shape[0] for a in ins) // piece
    return pl.pallas_call(
        functools.partial(pack_kernel, fields),
        grid=(1,),
        in_specs=[
            pl.BlockSpec((1,) + args[f].shape[1:], whole(l, *([0] * (args[f].ndim - 1))))
            for f, l in parts
        ],
        out_specs=pl.BlockSpec((lines, piece), whole(0, 0)),
        out_shape=struct((lines, piece), bf16),
        compiler_params=params(12),
        cost_estimate=cost(0, 4 * lines * piece),
        name="pack",
    )(*far(*ins))


def maps_kernel(group_rows, lengths_ref, order_ref, spot_ref, src_ref, segc_ref, segr_ref):
    group, slot, rows = spot_ref[0], spot_ref[1], group_rows // 4
    base = group * SEQ_GRP
    lens = [lengths_ref[base + i] for i in range(SEQ_GRP)]
    starts = [0, lens[0], lens[0] + lens[1]]
    end, ends, shifts = 0, [], []
    for j in range(SEQ_GRP):
        seq = order_ref[base + j] - base
        length, start = lens[SEQ_GRP - 1], starts[SEQ_GRP - 1]
        for i in range(SEQ_GRP - 1):
            length = jnp.where(seq == i, lens[i], length)
            start = jnp.where(seq == i, starts[i], start)
        shifts.append(start - end)
        end = end + length
        ends.append(end)

    def turn(x):
        return x % 2 * 2 + x // 2

    def position(shape, axis):
        at = lax.broadcasted_iota(jnp.int32, shape, axis)
        return jnp.bitwise_xor(turn(at // rows), slot) * rows + at % rows

    def segment(place):
        return sum((place >= e).astype(jnp.int32) for e in ends)

    segr_ref[...] = segment(position(segr_ref.shape, 1))
    place = position(segc_ref.shape, 0)
    seg = segment(place)
    segc_ref[...] = seg
    source = place
    for j in range(SEQ_GRP):
        source = jnp.where(seg == j, place + shifts[j], source)
    src_ref[...] = turn(jnp.bitwise_xor(source // rows, slot)) * rows + source % rows


def maps(lengths, order, spot, group_rows):
    outs = [struct((group_rows, 1), jnp.int32)] * 2 + [struct((1, group_rows), jnp.int32)]
    return pl.pallas_call(
        functools.partial(maps_kernel, group_rows),
        grid=(1,),
        in_specs=[SCALARS] * 3,
        out_specs=blocks_in(outs),
        out_shape=outs,
        compiler_params=params(8),
        cost_estimate=cost(100 * group_rows, 8 * group_rows),
        name="maps",
    )(lengths, order, spot)


def tile_at(where_ref, spec):
    masked, d, core = spec
    d = jnp.bitwise_xor(where_ref[0], d) if masked else d
    tile = 2 * d + jnp.bitwise_xor(where_ref[1], core)
    return pl.ds(pl.multiple_of(tile * 128, 128), 128)


def tile_order(where, specs):
    return jnp.stack([2 * (where[0] ^ d if m else d) + (where[1] ^ core) for m, d, core in specs])


def place_kernel(fields, counts, specs, where_ref, *refs):
    ins, outs = refs[: len(counts)], refs[len(counts) :]
    k = 0
    for ref, count in zip(ins, counts):
        for i in range(count):
            here = tile_at(where_ref, specs[k])
            at = 0
            for field, out in zip(fields, outs):
                if field == "qkv":
                    for j in range(3):
                        for h in range(0, out.shape[2], 128):
                            out[j, here, h : h + 128] = ref[i, at : at + 128, :]
                            at += 128
                elif field == "up":
                    for h in range(0, out.shape[1], 128):
                        out[here, h : h + 128] = ref[i, at : at + 128, :]
                        at += 128
                else:
                    out[:, here] = ref[i, at : at + out.shape[0], :]
                    at += out.shape[0]
            k += 1


def place(fields, stacks, specs, where, head_width, ff_width):
    counts = [s.shape[0] for s in stacks]
    piece = stacks[0].shape[2]
    if piece != 128:
        tiles = jnp.take(jnp.concatenate(stacks, 0), jnp.argsort(tile_order(where, specs)), axis=0)
        flat = tiles.transpose(1, 0, 2).reshape(-1, D)
        found, at = [], 0
        for f in fields:
            lines = lines_of(f, head_width, ff_width)
            part = flat[at : at + lines]
            at += lines
            if f == "qkv":
                part = part.reshape(3, head_width, D).transpose(0, 2, 1)
            found.append(part.T if f == "up" else part)
        return found
    shapes = {
        "qkv": (3, D, head_width),
        "out": (head_width, D),
        "up": (D, ff_width),
        "down": (ff_width, D),
    }
    outs = [struct(shapes[f], bf16) for f in fields]
    return pl.pallas_call(
        functools.partial(place_kernel, fields, counts, specs),
        grid=(1,),
        in_specs=[SCALARS] + blocks_in(stacks),
        out_specs=blocks_in(outs),
        out_shape=outs,
        compiler_params=params(20),
        cost_estimate=cost(0, 4 * sum(s.size for s in stacks)),
        name="place",
    )(where, *far(*stacks))


def grad_kernel(fields, counts, specs, where_ref, *refs):
    count = len(fields)
    ins, refs = refs[: 4 * count], refs[4 * count :]
    outs, bufs, sems = refs[: len(counts)], refs[len(counts) : -1], refs[-1]
    rows = ins[0].shape[0]
    copies = []
    for n in range(4 * count):
        there = bufs[n // 2].at[pl.ds(n % 2 * rows, rows), :]
        copies.append(pltpu.make_async_copy(ins[n], there, sems.at[n]))
        copies[-1].start()
    spots = [(out, i) for out, total in zip(outs, counts) for i in range(total)]
    at = 0
    for n, field in enumerate(fields):
        for copy in copies[4 * n : 4 * n + 4]:
            copy.wait()
        a_ref, b_ref = bufs[2 * n : 2 * n + 2]
        b = b_ref[...]
        lines = b.shape[1]
        for g in range(0, len(specs), 4):
            a = jnp.concatenate([a_ref[:, tile_at(where_ref, t)] for t in specs[g : g + 4]], 1)
            by_rows = field in ("qkv", "up")
            total = (tn(a, b) if by_rows else tn(b, a)).astype(bf16)
            for k, (out, i) in enumerate(spots[g : g + 4]):
                tile = slice(k * 128, (k + 1) * 128)
                if by_rows:
                    for h in range(0, lines, 128):
                        out[i, at + h : at + h + 128, :] = total[tile, h : h + 128]
                else:
                    out[i, at : at + lines, :] = total[:, tile]
        at += lines


def weight_grad(fields, pairs, specs, counts, where):
    flat = [r for a, b in pairs for r in (*a, *b)]
    lines = sum(b[0].shape[1] for _, b in pairs)
    rows = sum(b.shape[0] for b in pairs[0][1])
    piece = D // len(specs)
    if piece != 128:
        products = [dot(jnp.concatenate(b, 0), jnp.concatenate(a, 0), 0, 0) for a, b in pairs]
        tiles = jnp.concatenate(products, 0).astype(bf16).reshape(lines, len(specs), piece)
        tiles = jnp.take(tiles.transpose(1, 0, 2), tile_order(where, specs), axis=0)
        ends = [sum(counts[: i + 1]) for i in range(len(counts))]
        return [tiles[e - n : e] for e, n in zip(ends, counts)]
    kind = struct if len(counts) > 1 else hbm
    outs = [kind((n, lines, piece), bf16) for n in counts]
    bufs = [pltpu.VMEM((rows, r.shape[1]), bf16) for r in flat[::2]]
    return pl.pallas_call(
        functools.partial(grad_kernel, fields, counts, specs),
        grid=(1,),
        in_specs=[SCALARS] + [ROWS] * len(flat),
        out_specs=blocks_in(outs),
        out_shape=outs,
        scratch_shapes=bufs + [pltpu.SemaphoreType.DMA((len(flat),))],
        compiler_params=params(32),
        cost_estimate=cost(2 * rows * D * lines, 12 * MIB),
        name="weight_grad",
    )(where, *far(*flat))


def finish_kernel(fields, has_prev, keep_ref, got_ref, *refs):
    outs = refs[len(fields) if has_prev else 0 :]
    at = 0
    for field, out in zip(fields, outs):
        if field == "qkv":
            for j in range(3):
                for h in range(0, out.shape[3], 128):
                    out[0, j, :, h : h + 128] = keep_ref[at : at + 128, :] + got_ref[at : at + 128, :].astype(f32)
                    at += 128
        elif field == "up":
            for h in range(0, out.shape[2], 128):
                out[0, :, h : h + 128] = keep_ref[at : at + 128, :] + got_ref[at : at + 128, :].astype(f32)
                at += 128
        else:
            n = out.shape[1]
            out[0] = keep_ref[at : at + n, :] + got_ref[at : at + n, :].astype(f32)
            at += n


def finish(fields, keep, got, layer, prev, head_width, ff_width):
    piece = keep.shape[1]
    shapes = {
        "qkv": (3, piece, head_width),
        "out": (head_width, piece),
        "up": (piece, ff_width),
        "down": (ff_width, piece),
    }
    if piece != 128:
        total, at, found = keep + got.astype(f32), 0, []
        for n, f in enumerate(fields):
            lines = lines_of(f, head_width, ff_width)
            part = total[at : at + lines]
            at += lines
            if f == "qkv":
                part = part.reshape(3, head_width, piece).transpose(0, 2, 1)
            part = part.T if f == "up" else part
            base = jnp.zeros((LAYERS,) + shapes[f], f32) if prev is None else prev[n]
            found.append(base.at[layer].set(part))
        return found
    outs = [struct((LAYERS,) + shapes[f], f32) for f in fields]
    specs = [
        pl.BlockSpec((1,) + o.shape[1:], whole(layer, *([0] * (len(o.shape) - 1)))) for o in outs
    ]
    return pl.pallas_call(
        functools.partial(finish_kernel, fields, prev is not None),
        grid=(1,),
        in_specs=[pl.BlockSpec(keep.shape, whole(0, 0))] * 2
        + ([] if prev is None else [pl.BlockSpec(memory_space=pl.ANY)] * len(outs)),
        out_specs=specs,
        out_shape=outs,
        input_output_aliases={} if prev is None else {2 + n: n for n in range(len(outs))},
        compiler_params=params(16),
        cost_estimate=cost(0, 10 * keep.size),
        name="finish",
    )(keep, got, *([] if prev is None else prev))


def deal_kernel(src_ref, *refs):
    raw, outs = stack_rows(refs[:4]), refs[4:]
    rows = outs[0].shape[0]
    spot = lax.broadcasted_iota(jnp.int32, (1, raw.shape[0]), 1)
    hit = src_ref[...] == spot
    dealt = nn(jnp.where(hit, 1.0, 0.0).astype(bf16), raw)
    for i in range(4):
        outs[i][...] = dealt[i * rows : (i + 1) * rows].astype(bf16)
    outs[4][...] = dealt[:rows]


def deal_rows(src, raw):
    rows, d = raw[0].shape
    outs = [struct((rows, d), bf16)] * 4 + [struct((rows, d), f32)]
    outs = pl.pallas_call(
        deal_kernel,
        grid=(1,),
        in_specs=blocks_in((src, *raw)),
        out_specs=blocks_in(outs),
        out_shape=outs,
        compiler_params=params(20),
        cost_estimate=cost(32 * rows * rows * d, 6 * MIB),
        name="deal_rows",
    )(src, *raw)
    return outs[:2], outs[2:4], outs[4]


def total_of(refs):
    total = refs[0][...]
    for ref in refs[1:]:
        total = total + ref[...].astype(f32)
    return total


def norm_kernel(n_terms, bias_row, gain_row, shift_row, *refs):
    terms, (vec_ref, y_ref, low_ref, n_ref, r_ref) = refs[:n_terms], refs[n_terms:]
    row = lambda i: vec_ref[i : i + 1, :]
    v = total_of(terms) + row(bias_row)
    centred = v - jnp.mean(v, axis=-1, keepdims=True)
    r = lax.rsqrt(jnp.mean(centred * centred, axis=-1, keepdims=True) + EPS)
    n = centred * r
    y = n * row(gain_row) + row(shift_row)
    y_ref[...] = y
    low_ref[...] = y.astype(bf16)
    n_ref[...] = n
    r_ref[...] = r


def term_specs(terms):
    shape = terms[0].shape
    return [pl.BlockSpec(shape, whole(0, 0)) for _ in terms]


def norm(terms, vectors, bias_row, gain_row, shift_row):
    shape = terms[0].shape
    outs = [struct(shape, f32), struct(shape, bf16), hbm(shape, f32), struct((shape[0], 1), f32)]
    return pl.pallas_call(
        functools.partial(norm_kernel, len(terms), bias_row, gain_row, shift_row),
        grid=(1,),
        in_specs=term_specs(terms) + [full(vectors)],
        out_specs=blocks_in(outs),
        out_shape=outs,
        compiler_params=params(8),
        cost_estimate=cost(20 * terms[0].size, 2 * MIB),
        name="norm",
    )(*terms, vectors)


def norm_back_kernel(n_terms, gain_row, has_sums, *refs):
    terms, refs = refs[:n_terms], refs[n_terms:]
    n_ref, r_ref, vec_ref = refs[:3]
    dv_ref, low_ref, sums_ref = refs[-3:]
    d_out, n = total_of(terms), n_ref[...]
    dn = d_out * vec_ref[gain_row : gain_row + 1, :]
    dv = r_ref[...] * (
        dn - jnp.mean(dn, axis=-1, keepdims=True) - n * jnp.mean(dn * n, axis=-1, keepdims=True)
    )
    dv_ref[...] = dv
    low_ref[...] = dv.astype(bf16)
    for i, a in enumerate((d_out * n, d_out, dv)):
        column = jnp.sum(a, axis=0, keepdims=True)
        sums_ref[i : i + 1, :] = column + refs[3][i : i + 1, :] if has_sums else column


def norm_back(terms, n, r, vectors, gain_row, sums=None):
    shape = terms[0].shape
    outs = [struct(shape, f32), struct(shape, bf16), struct((3, shape[1]), f32)]
    more = [] if sums is None else [sums]
    return pl.pallas_call(
        functools.partial(norm_back_kernel, len(terms), gain_row, sums is not None),
        grid=(1,),
        in_specs=term_specs(terms) + blocks_in((n, r, vectors, *more)),
        out_specs=blocks_in(outs),
        out_shape=outs,
        compiler_params=params(8),
        cost_estimate=cost(20 * terms[0].size, 3 * MIB),
        name="norm_back",
    )(*terms, n, r, vectors, *more)


def dot(a, b, ca, cb):
    return lax.dot_general(a, b, (((ca,), (cb,)), ((), ())), preferred_element_type=f32)


def swap(a, axis):
    return lax.ppermute(a, axis, SWAP)


def flip_d(a, bit, n_d):
    return lax.ppermute(a, "d", [(i, i ^ (1 << bit)) for i in range(n_d)])


def to_home(a):
    return lax.ppermute(a, ("c", "zh"), [(1, 2), (2, 1)])


def after(a, *marks):
    return lax.optimization_barrier((a,) + marks)[0]


def send_rows(own):
    return (own, swap(own, "c")), swap(own, "zl")


def far_rows(far, *marks):
    if marks:
        far = after(far, *marks)
    return far, swap(far, "c")


def chip_sum(mine, theirs, *arrivals):
    other = swap(after(theirs, *arrivals) if arrivals else theirs, "c")
    return mine, other


def cross_sum(terms):
    total = (terms[0] + terms[1].astype(f32)).astype(bf16)
    return total, swap(total, "zl")


def masks_of(order):
    masks = [0]
    for bit in order:
        masks = masks + [m ^ (1 << bit) for m in masks]
    return masks


def absolute_specs(n_d):
    return [(False, d, core) for d in range(n_d) for core in range(2)]


def reduce_specs(n_d):
    bits = list(range(n_d.bit_length() - 1))
    half = n_d // 2
    order = []
    for core, masks in ((0, masks_of(bits)), (1, masks_of(bits[::-1]))):
        order += [(True, m, core) for m in masks[half:] + masks[:half]]
    return order


class Gather:
    def __init__(self, fields, tile, crossed, widths, pos, where, n_d):
        self.fields, self.pos, self.where, self.n_d = fields, pos, where, n_d
        self.widths, self.tile, self.crossed = widths, tile, crossed

    def cores(self, *marks):
        _, c, zh, _ = self.pos
        same = c == zh
        crossed = after(self.crossed, *marks) if marks else self.crossed
        self.own = jnp.where(same, self.tile, crossed)
        self.other = swap(jnp.where(same, crossed, self.tile), "c")
        return self.other

    def collect(self, *marks):
        self.both = jnp.stack([self.own, self.other])
        both = after(self.both, *marks) if marks else self.both
        self.stacks = [lax.all_gather(both, "d", axis=0, tiled=True)]
        self.specs = absolute_specs(self.n_d)
        return self.stacks[0]

    def weights(self):
        found = place(self.fields, self.stacks, self.specs, self.where, *self.widths)
        return dict(zip(self.fields, found))


class Reduce:
    def __init__(self, fields, pairs, pos, where, n_d, by_halves):
        self.fields, self.pos, self.n_d, self.step = fields, pos, n_d, 0
        specs = reduce_specs(n_d) if by_halves else absolute_specs(n_d)
        counts = [n_d // 2] * 4 if by_halves else [2 * n_d]
        self.stacks = weight_grad(fields, pairs, specs, counts, where)

    def collect(self, *marks):
        both = lax.psum_scatter(after(self.stacks[0], *marks), "d", scatter_dimension=0, tiled=True)
        self.first, self.second = both[0], both[1]
        return both

    def halve(self, *marks):
        bits = list(range(self.n_d.bit_length() - 1))
        if self.step == len(bits):
            return []
        if self.step == 0:
            self.sends, self.keeps = [self.stacks[0], self.stacks[2]], [self.stacks[1], self.stacks[3]]
        sends = lax.optimization_barrier((*self.sends, *marks))[:2] if marks else self.sends
        orders = (bits[::-1], bits)
        gots = [flip_d(a, o[self.step], self.n_d) for a, o in zip(sends, orders)]
        self.step += 1
        half = self.keeps[0].shape[0] // 2
        if self.step < len(bits):
            self.sends = [
                (k[half:].astype(f32) + g[half:].astype(f32)).astype(bf16)
                for k, g in zip(self.keeps, gots)
            ]
            self.keeps = [k[:half].astype(f32) + g[:half].astype(f32) for k, g in zip(self.keeps, gots)]
        else:
            self.first, self.second = (k[0].astype(f32) + g[0].astype(f32) for k, g in zip(self.keeps, gots))
        return gots

    def cores(self, *marks):
        while len(self.stacks) > 1 and self.step < self.n_d.bit_length() - 1:
            self.halve()
        second = self.second.astype(bf16)
        self.other = swap(after(second, *marks) if marks else second, "c")
        self.crossed, self.at = [], 0
        return self.other

    def cross(self, lines, *marks):
        _, c, zh, _ = self.pos
        same = c == zh
        part = slice(self.at, self.at + lines)
        send = jnp.where(same, self.other[part], self.first[part].astype(bf16))
        self.crossed.append(swap(after(send, *marks) if marks else send, "zh"))
        self.at += lines
        return self.crossed[-1]

    def finish(self, outs, layer, widths, *marks):
        _, c, zh, _ = self.pos
        got = jnp.concatenate(self.crossed, 0) if len(self.crossed) > 1 else self.crossed[0]
        first = after(self.first, *marks) if marks else self.first
        keep = jnp.where(c == zh, first.astype(f32), self.other.astype(f32))
        prev = None if outs[self.fields[0]] is None else [outs[f] for f in self.fields]
        outs.update(zip(self.fields, finish(self.fields, keep, got, layer, prev, *widths)))


def gather_small(own, pos, n_d):
    d, c, _, zl = pos
    cur = own
    for axis, me in (("zl", zl), ("c", c)):
        got = swap(cur, axis)
        cur = jnp.where(me == 0, jnp.concatenate([cur, got]), jnp.concatenate([got, cur]))
    for bit in range(n_d.bit_length() - 1):
        got = flip_d(cur, bit, n_d)
        mine = jnp.bitwise_and(jnp.right_shift(d, bit), 1)
        cur = jnp.where(mine == 0, jnp.concatenate([cur, got]), jnp.concatenate([got, cur]))
    return cur


def pick(a, at, axis):
    return lax.dynamic_index_in_dim(a, at, axis, keepdims=False)


def halve_small(cur, me, send):
    view = cur.reshape(2, -1, cur.shape[1])
    return pick(view, me, 0) + send(pick(view, 1 - me, 0))


def body(tokens, cotangent, lengths, order, w_qkv, w_out, w_up, w_down, gains, biases, up_bias):
    rows = tokens.shape[0]
    n_d = lax.axis_size("d")
    n_dev = n_d * 8
    head_width = D // 4
    heads = head_width // HEAD_DIM
    ff_width = FF // 4
    widths = (head_width, ff_width)
    scale = HEAD_DIM ** (-0.5)
    d, c, zh, zl = (lax.axis_index(a) for a in ALL)
    pos = (d, c, zh, zl)
    slot = 2 * c + zl
    where = jnp.stack([d, c]).astype(jnp.int32)
    stay = c == zh
    args = {"qkv": w_qkv.transpose(0, 2, 1, 3), "out": w_out, "up": w_up, "down": w_down}

    tile_a0 = pack((("qkv", 0), ("out", 0)), args)
    a0_crossed = swap(tile_a0, "zh")
    g_a0 = Gather(("qkv", "out"), tile_a0, a0_crossed, widths, pos, where, n_d)
    rest = [("up", 0), ("down", 0), ("qkv", 1), ("out", 1), ("up", 1), ("down", 1)]
    tile_rest = pack(rest, args)
    small_own = jnp.concatenate([a.reshape(1, -1) for a in (gains, biases, up_bias)], 1)
    src, seg_col, seg_row = maps(
        lengths, order, jnp.stack([d * 2 + zh, slot]).astype(jnp.int32), 4 * rows
    )
    seg_near, seg_far = seg_col[: 2 * rows], seg_col[2 * rows :]
    g_a0.cores(src, small_own, tile_rest)
    g_a0.collect()
    raw_got = to_home(after(tokens, a0_crossed))
    raw = jnp.where(stay, tokens, raw_got)
    raw_near, raw_far = send_rows(raw)
    rest_crossed = swap(after(tile_rest, raw_got), "zh")
    gathers, at = [], 0
    for n in range(0, len(rest), 2):
        fields = (rest[n][0], rest[n + 1][0])
        lines = sum(lines_of(f, *widths) for f in fields)
        part = slice(at, at + lines)
        gathers.append(Gather(fields, tile_rest[part], rest_crossed[part], widths, pos, where, n_d))
        at += lines
    g_f0, g_a1, g_f1 = gathers
    x_near, x_far, hidden = deal_rows(src, [*raw_near, *far_rows(raw_far)])
    small_near = gather_small(after(small_own, x_near[0]), pos, n_d)
    small_far = swap(small_near, "zh")
    width = D // n_dev
    up_width = FF // n_dev
    n_vec = LAYERS * 8
    small_all = jnp.where(zh == 0, jnp.stack([small_near, small_far]), jnp.stack([small_far, small_near]))
    small_all = small_all.reshape(2, n_d * 2, 2, -1)
    vectors = small_all[..., : n_vec * width].reshape(2, n_d * 2, 2, n_vec, width)
    vectors = vectors.transpose(3, 1, 0, 2, 4).reshape(n_vec, D)
    ups = small_all[..., n_vec * width :].reshape(2, n_d * 2, 2, LAYERS, up_width)
    ups = ups.transpose(3, 1, 0, 2, 4).reshape(LAYERS, FF)
    ups = lax.dynamic_slice(ups, (0, slot * ff_width), (LAYERS, ff_width))
    own_vectors = lax.dynamic_slice(vectors, (0, slot * head_width), (n_vec, head_width))
    gain_row = lambda layer, i: 2 * layer + i
    bias_row = lambda layer, i: 2 * LAYERS + 6 * layer + i
    f0_other = g_f0.cores(small_near)
    g_f0.collect()
    cot_got = to_home(after(cotangent, f0_other, small_far))
    cot_near, cot_sent = send_rows(jnp.where(stay, cotangent, cot_got))
    weights = [g_a0.weights(), {}]

    kept = []
    x_sent = None
    for layer in range(LAYERS):
        first = layer == 0
        w = weights[layer]
        q_row, v_row = bias_row(layer, 0), bias_row(layer, 1)
        add = jnp.concatenate(
            [
                own_vectors[q_row : q_row + 1],
                jnp.zeros((1, head_width), f32),
                own_vectors[v_row : v_row + 1],
            ],
            1,
        )
        if first:
            x_near = (after(x_near[0], g_f0.both), x_near[1])
        proj_near, keep_near = project(x_near, w["qkv"], add)
        if not first:
            x_far = far_rows(x_sent, keep_near)
        proj_far, keep_far = project(x_far, w["qkv"], add)
        proj = (proj_near, proj_far)
        x_kept = (keep_near, keep_far)
        due = [cot_got] if first else []
        att_far, lse_far, mine, theirs = attend(
            proj_far, proj, seg_far, seg_row, w["out"], scale, heads
        )
        chip, crossed = cross_sum(chip_sum(mine, theirs, *due))
        att_near, lse_near, mine, theirs = attend(
            after(proj_near, chip), proj, seg_near, seg_row, w["out"], scale, heads
        )
        terms = chip_sum(mine, theirs, crossed)
        terms = (*terms, crossed)
        at = [bias_row(layer, 2), gain_row(layer, 0), bias_row(layer, 3)]
        normed, low, n_one, r_one = norm((hidden, *terms), vectors, *at)
        n_near, n_sent = send_rows(low)
        due = [n_sent]
        if first:
            w.update(g_f0.weights())
            g_a1.cores(low)
            g_a1.collect()
        else:
            w.update(g_f1.weights())
        u_bias = ups[layer : layer + 1]
        act_near, slope_near, mine_near, theirs_near, keep_near = ffn(n_near, w["up"], w["down"], u_bias)
        near = chip_sum(mine_near, theirs_near, *due)
        n_far = far_rows(n_sent, keep_near)
        due = []
        act_far, slope_far, mine, theirs, keep_far = ffn(n_far, w["up"], w["down"], u_bias)
        chip, crossed = cross_sum(chip_sum(mine, theirs, *due))
        if first:
            g_f1.cores(chip)
            g_f1.collect()
        at = [bias_row(layer, 4), gain_row(layer, 1), bias_row(layer, 5)]
        hidden, low, n_two, r_two = norm((normed, *near, crossed), vectors, *at)
        kept.append(
            dict(
                x=x_kept, proj=proj, lse=(lse_near, lse_far), att=(att_near, att_far),
                one=(n_one, r_one), n=(keep_near, keep_far), slope=(slope_near, slope_far),
                act=(act_near, act_far), two=(n_two, r_two),
            )
        )
        if first:
            weights[1].update(g_a1.weights())
            x_near, x_sent = send_rows(low)
    last_low = low

    deal = (src[:rows] == jnp.arange(4 * rows, dtype=jnp.int32)[None, :]).astype(bf16)
    cot = jnp.concatenate([*cot_near, *far_rows(cot_sent)], 0)
    valid = (seg_near[:rows] < SEQ_GRP).astype(f32)
    grad_y = (dot(deal, cot, 1, 0) * valid,)
    vector_sums = [None] * LAYERS
    up_sums = [None] * LAYERS
    late = None

    def spot(vec, full_width):
        return lax.dynamic_update_slice(jnp.zeros((1, full_width), f32), vec, (0, slot * vec.shape[1]))

    for layer in reversed(range(LAYERS)):
        w, k = weights[layer], kept[layer]
        d_two, low, sums_two = norm_back(grad_y, *k["two"], vectors, gain_row(layer, 1))
        two_near, two_sent = send_rows(low)
        if late:
            late[0].cores(low)
        up_near, sum_near, mine_near, theirs_near, keep_two_near = ffn_back(
            two_near, w["up"], w["down"], k["slope"][0]
        )
        near = chip_sum(mine_near, theirs_near, two_sent)
        two_far = far_rows(two_sent, up_near)
        due = []
        if late:
            due += [late[0].cross(ff_width, up_near)]
        up_far, sum_far, mine, theirs, keep_two_far = ffn_back(
            two_far, w["up"], w["down"], k["slope"][1]
        )
        chip, crossed = cross_sum(chip_sum(mine, theirs, *due))
        two_pair = ((keep_two_near, keep_two_far), (k["act"][0], after(k["act"][1], chip)))
        up_pair = (k["n"], (up_near, after(up_far, chip)))
        due = []
        if late:
            due += [late[0].cross(ff_width, chip)]
            r_down = Reduce(("down",), (two_pair,), pos, where, n_d, True)
            down_got = r_down.halve()
            up_pair = (up_pair[0], (up_near, after(up_far, r_down.stacks[0])))
            r_ff = Reduce(("up",), (up_pair,), pos, where, n_d, True)
            up_got = r_ff.halve()
        else:
            r_ff = Reduce(("up", "down"), (up_pair, two_pair), pos, where, n_d, False)
        d_two = after(d_two, r_ff.stacks[0], *due)
        d_one, low, sums_one = norm_back((d_two, *near, crossed), *k["one"], vectors, gain_row(layer, 0))
        one_near, one_sent = send_rows(low)
        if not late:
            r_ff.collect(low)
        *earlier, keep_one_near = attend_back(
            k["proj"][0], k["proj"], seg_near, seg_row, k["lse"][0], one_near, w["out"], scale, heads
        )
        one_far = far_rows(one_sent, earlier[0])
        due = []
        if late:
            earlier[0] = after(earlier[0], *down_got, *up_got)
            due += r_down.halve(earlier[0]) + r_ff.halve(earlier[0])
            late[1].cores(earlier[0])
            due += [late[1].cross(4 * head_width, earlier[0])]
        else:
            mixed_got = to_home(after(last_low, earlier[0]))
            due += [mixed_got]
        d_near, d_far, head_sums, keep_one_far = attend_back(
            k["proj"][1], k["proj"], seg_far, seg_row, k["lse"][1], one_far, w["out"], scale, heads,
            earlier,
        )
        if late:
            outs = {f: None for f in ("qkv", "out", "up", "down")}
            late[0].finish(outs, 1, widths, earlier[0])
            due += [outs["up"]]
        d_far = after(d_far, *due)
        mine, theirs = input_grad(d_far, w["qkv"])
        chip, crossed = cross_sum(chip_sum(mine, theirs))
        att_pairs = ((k["x"], (d_near, after(d_far, chip))), ((keep_one_near, keep_one_far), k["att"]))
        if late:
            r_att = Reduce(("qkv", "out"), att_pairs, pos, where, n_d, True)
            r_att.halve()
            d_near = after(d_near, r_att.stacks[0])
            near = chip_sum(*input_grad(d_near, w["qkv"]))
        else:
            near = chip_sum(*input_grad(after(d_near, chip), w["qkv"]))
            att_pairs = ((k["x"], (after(d_near, near[1]), d_far)), att_pairs[1])
            r_att = Reduce(("qkv", "out"), att_pairs, pos, where, n_d, False)
            late = (r_ff, r_att)
            d_one = after(d_one, r_att.stacks[0])
            r_att.collect(crossed)
        grad_y = (d_one, *near, crossed)
        vector_sums[layer] = (
            [sums_one[0:1], sums_two[0:1]],
            [
                spot(head_sums[0:1], D), spot(head_sums[1:2], D), sums_one[2:3],
                sums_one[1:2], sums_two[2:3], sums_two[1:2],
            ],
        )
        up_sums[layer] = spot(sum_near + sum_far, FF)

    r_down.cores(d_far)
    down_crossed = r_down.cross(ff_width)
    r_ff.cores(d_far)
    up_crossed = r_ff.cross(ff_width, down_crossed)
    att_got = r_att.halve(down_crossed)
    base, mine, other, crossed = grad_y
    own_grad = (base + mine + other.astype(f32) + crossed.astype(f32)).astype(bf16)
    grad_got = to_home(after(own_grad, *att_got))
    r_att.cores(up_crossed)
    r_att.cross(4 * head_width)
    late[1].finish(outs, 1, widths, *att_got)
    r_down.finish(outs, 0, widths, *att_got)
    r_ff.finish(outs, 0, widths, *att_got)
    r_att.finish(outs, 0, widths)
    tokens_grad = jnp.where(stay, own_grad, grad_got).astype(f32)
    mixed = jnp.where(stay, last_low, after(mixed_got, *att_got))

    terms = jnp.concatenate(
        [g for s in vector_sums for g in s[0]] + [b for s in vector_sums for b in s[1]], 0
    )
    small = jnp.concatenate(
        [
            terms.reshape(n_vec, n_dev, width).transpose(1, 0, 2).reshape(n_dev, n_vec * width),
            jnp.concatenate(up_sums, 0)
            .reshape(LAYERS, n_dev, up_width)
            .transpose(1, 0, 2)
            .reshape(n_dev, LAYERS * up_width),
        ],
        1,
    )
    n_small = small.shape[1]
    small = after(small, *att_got).reshape(n_d, 2, 4 * n_small)
    small = pick(small, c, 1) + swap(pick(small, 1 - c, 1), "c")
    small = small.reshape(n_d, 2, 2, n_small)
    small = pick(small, zl, 2) + swap(pick(small, 1 - zl, 2), "zl")
    small = small.reshape(n_d, 2 * n_small)
    for bit in reversed(range(n_d.bit_length() - 1)):
        mine = jnp.bitwise_and(jnp.right_shift(d, bit), 1)
        small = halve_small(small, mine, lambda a, bit=bit: flip_d(a, bit, n_d))
    small_sum = halve_small(small.reshape(2, n_small), zh, lambda a: swap(a, "zh"))
    n_gain = LAYERS * 2 * width
    g_gains = small_sum[:, :n_gain].reshape(LAYERS, 2, width)
    g_biases = small_sum[:, n_gain : n_vec * width].reshape(LAYERS, 6, width)
    g_upb = small_sum[:, n_vec * width :].reshape(LAYERS, up_width)
    g_qkv = outs["qkv"].transpose(0, 2, 1, 3)
    return mixed, tokens_grad, g_qkv, outs["out"], outs["up"], outs["down"], g_gains, g_biases, g_upb


def solution(mesh):
    n_dp, n_t = mesh.shape["dp"], mesh.shape["tensor"]
    fine = Mesh(mesh.devices.reshape(n_dp // 2, 2, n_t // 2, 2), ALL)
    dp, t = ("d", "c"), ("zh", "zl")
    return jax.shard_map(
        body,
        mesh=fine,
        in_specs=(
            P(ALL, None),
            P(ALL, None),
            P(),
            P(),
            P(None, dp, None, t),
            P(None, t, dp),
            P(None, dp, t),
            P(None, t, dp),
            P(None, None, ALL),
            P(None, None, ALL),
            P(None, ALL),
        ),
        out_specs=(
            P(ALL, None),
            P(ALL, None),
            P(None, dp, None, t),
            P(None, t, dp),
            P(None, dp, t),
            P(None, t, dp),
            P(None, None, ALL),
            P(None, None, ALL),
            P(None, ALL),
        ),
        check_vma=False,
    )
```

```python
import functools

import jax
import jax.numpy as jnp
from jax import lax
from jax.experimental import pallas as pl
from jax.experimental.pallas import tpu as pltpu
from jax.sharding import Mesh, PartitionSpec as P

D = 1024
HEAD_DIM = 64
FF = 4096
LAYERS = 2
SEQ_GRP = 3

EPS = 1e-05
NEG = -1e30
ALL = ("d", "c", "zh", "zl")
SWAP = [(0, 1), (1, 0)]
bf16 = jnp.bfloat16
f32 = jnp.float32
MIB = 1 << 20

TAIL_STEP = 0.24
TAIL = (
    0.0912286469891869,
    0.14294535326111468,
    -0.11556713177962434,
    0.5630756863681534,
    -0.5892310046041954,
    0.5271447780474939,
    -0.11959632556906954,
)
INV_SQRT_2PI = 0.3989422804014327


def nn(a, b):
    return lax.dot_general(a, b, (((1,), (0,)), ((), ())), preferred_element_type=f32)


def nt(a, b):
    return lax.dot_general(a, b, (((1,), (1,)), ((), ())), preferred_element_type=f32)


def tn(a, b):
    return lax.dot_general(a, b, (((0,), (0,)), ((), ())), preferred_element_type=f32)


def stack_rows(refs):
    return jnp.concatenate([r[...] for r in refs], 0)


def params(limit):
    return pltpu.CompilerParams(vmem_limit_bytes=limit * MIB)


def cost(flops, nbytes, exps=0):
    return pl.CostEstimate(flops=int(flops), bytes_accessed=int(nbytes), transcendentals=int(exps))


def struct(shape, dtype):
    return jax.ShapeDtypeStruct(shape, dtype)


def hbm(shape, dtype):
    return pltpu.HBM(shape, dtype)


def far(*arrays):
    return [pltpu.with_memory_space_constraint(a, pltpu.HBM) for a in arrays]


SCALARS = pl.BlockSpec(memory_space=pltpu.SMEM)
ROWS = pl.BlockSpec(memory_space=pltpu.HBM)


def full(a):
    shape = a.shape
    return pl.BlockSpec(shape, lambda *_: (0,) * len(shape))


def blocks_in(arrays):
    return [full(a) for a in arrays]


def gelu_parts(u):
    z = jnp.abs(u)
    bell = jnp.exp(-0.5 * (u * u))
    below = 1.0 + TAIL_STEP * z
    t = pl.reciprocal(below, approx=True)
    t = t * (2.0 - below * t)
    poly = jnp.full_like(t, TAIL[-1])
    for coef in TAIL[-2::-1]:
        poly = poly * t + coef
    tail = bell * (poly * t)
    phi = jnp.where(u > 0.0, 1.0 - tail, tail)
    return u * phi, phi + u * (INV_SQRT_2PI * bell)


def whole(*at):
    return lambda i: at


def project_kernel(*refs):
    x_refs, (w_ref, add_ref, out_ref, x_ref) = refs[:2], refs[2:]

    @pl.when(pl.program_id(0) == 0)
    def _():
        x_ref[...] = stack_rows(x_refs)

    out_ref[...] = (nn(x_ref[...], w_ref[0]) + add_ref[...]).astype(bf16)


def project(x, w_qkv, add):
    rows = 2 * x[0].shape[0]
    _, d, width = w_qkv.shape
    return pl.pallas_call(
        project_kernel,
        grid=(3,),
        in_specs=blocks_in(x)
        + [pl.BlockSpec((1, d, width), lambda i: (i, 0, 0)), pl.BlockSpec((1, width), lambda i: (0, i))],
        out_specs=[pl.BlockSpec((rows, width), lambda i: (0, i)), pl.BlockSpec((rows, d), whole(0, 0))],
        out_shape=[struct((rows, 3 * width), bf16), hbm((rows, d), bf16)],
        compiler_params=params(12),
        cost_estimate=cost(6 * rows * d * width, 4 * MIB),
        name="project",
    )(*x, w_qkv, add)


def input_grad_kernel(g_ref, w_ref, mine_ref, theirs_ref):
    width = w_ref.shape[2]
    part = sum(nt(g_ref[:, j * width : (j + 1) * width], w_ref[j]) for j in range(3))
    half = part.shape[0] // 2
    mine_ref[...] = part[:half]
    theirs_ref[...] = part[half:].astype(bf16)


def input_grad(d_proj, w_qkv):
    rows = d_proj.shape[0]
    _, d, width = w_qkv.shape
    outs = [struct((rows // 2, d), f32), struct((rows // 2, d), bf16)]
    return pl.pallas_call(
        input_grad_kernel,
        grid=(1,),
        in_specs=blocks_in((d_proj, w_qkv)),
        out_specs=blocks_in(outs),
        out_shape=outs,
        compiler_params=params(16),
        cost_estimate=cost(6 * rows * d * width, 4 * MIB),
        name="input_grad",
    )(d_proj, w_qkv)


def attend_kernel(scale, heads, q_ref, k0_ref, k1_ref, v0_ref, v1_ref, segq_ref, segk_ref, w_ref, *outs):
    att_ref, lse_ref, mine_ref, theirs_ref = outs
    q = q_ref[...] * jnp.asarray(scale, bf16)
    rows, width = q.shape
    ks, vs = (k0_ref, k1_ref), (v0_ref, v1_ref)
    kv_rows = k0_ref.shape[0]
    lane = lax.broadcasted_iota(jnp.int32, (1, width), 1) // HEAD_DIM
    stat_lane = lax.broadcasted_iota(jnp.int32, (1, 128), 1)
    out = jnp.zeros((rows, width), f32)
    lse = jnp.zeros((rows, 128), f32)
    segq = segq_ref[...]
    masks = [
        jnp.where(segq == segk_ref[:, i * kv_rows : (i + 1) * kv_rows], 0.0, NEG) for i in range(2)
    ]
    for h in range(heads):
        hit = lane == h
        qh = jnp.where(hit, q, jnp.zeros_like(q))
        scores = [nt(qh, ks[i][...]) + masks[i] for i in range(2)]
        peak = jnp.maximum(*[jnp.max(s, axis=1, keepdims=True) for s in scores])
        exps = [jnp.exp(s - peak) for s in scores]
        total = sum(jnp.sum(e, axis=1, keepdims=True) for e in exps)
        inv = 1.0 / total
        head_out = sum(nn((exps[i] * inv).astype(bf16), vs[i][...]) for i in range(2))
        out = jnp.where(hit, head_out, out)
        lse = jnp.where(stat_lane == h, peak + jnp.log(total), lse)
    low = out.astype(bf16)
    att_ref[...] = low
    lse_ref[...] = lse
    part = nn(low, w_ref[...])
    half = rows // 2
    mine_ref[...] = part[:half]
    theirs_ref[...] = part[half:].astype(bf16)


def attend(proj_q, proj, seg_q, seg_k, w_out, scale, heads):
    rows, width = proj_q.shape[0], heads * HEAD_DIM
    d = w_out.shape[1]
    return pl.pallas_call(
        functools.partial(attend_kernel, scale, heads),
        grid=(1,),
        in_specs=[pl.BlockSpec((rows, width), whole(0, 0))]
        + [pl.BlockSpec((rows, width), whole(0, 1))] * 2
        + [pl.BlockSpec((rows, width), whole(0, 2))] * 2
        + [
            pl.BlockSpec((rows, 1), whole(0, 0)),
            pl.BlockSpec((1, 2 * rows), whole(0, 0)),
            pl.BlockSpec((width, d), whole(0, 0)),
        ],
        out_specs=[
            pl.BlockSpec((rows, width), whole(0, 0)),
            pl.BlockSpec((rows, 128), whole(0, 0)),
            pl.BlockSpec((rows // 2, d), whole(0, 0)),
            pl.BlockSpec((rows // 2, d), whole(0, 0)),
        ],
        out_shape=[
            hbm((rows, width), bf16),
            hbm((rows, 128), f32),
            struct((rows // 2, d), f32),
            struct((rows // 2, d), bf16),
        ],
        compiler_params=params(28),
        cost_estimate=cost(32 * rows * rows * width, 6 * MIB, rows * rows * 2 * heads),
        name="attend",
    )(proj_q, *proj, *proj, seg_q, seg_k, w_out)


def attend_back_kernel(scale, heads, last, *refs):
    q_ref, k0_ref, k1_ref, v0_ref, v1_ref, segq_ref, segk_ref, lse_ref = refs[:8]
    one_refs, w_ref, refs = refs[8:10], refs[10], refs[11:]
    q = q_ref[...]
    rows, width = q.shape
    ks, vs = (k0_ref, k1_ref), (v0_ref, v1_ref)
    if last:
        dq0_ref, sumq_ref, dk_in, dv_in = refs[:4]
        g0_ref, g1_ref, sums_ref, keep_ref, dk_ref, dv_ref = refs[4:]
    else:
        dq0_ref, sumq_ref, dk_ref, dv_ref, keep_ref = refs
    lane = lax.broadcasted_iota(jnp.int32, (1, width), 1) // HEAD_DIM
    one = stack_rows(one_refs)
    keep_ref[...] = one
    grad = nt(one, w_ref[...]).astype(bf16)
    segq = segq_ref[...]
    masks = [jnp.where(segq == segk_ref[:, i * rows : (i + 1) * rows], 0.0, NEG) for i in range(2)]
    sc = jnp.asarray(scale, bf16)
    zero = jnp.zeros_like(q)
    dq = jnp.zeros((rows, width), f32)
    for h in range(heads):
        hit = lane == h
        qh = jnp.where(hit, q, zero) * sc
        gh = jnp.where(hit, grad, zero)
        lse = lse_ref[:, h : h + 1]
        probs = [jnp.exp(nt(qh, ks[i][...]) + masks[i] - lse) for i in range(2)]
        d_probs = [nt(gh, vs[i][...]) for i in range(2)]
        dot_sum = sum(jnp.sum(p * g, axis=1, keepdims=True) for p, g in zip(probs, d_probs))
        dq_h = 0.0
        for i in range(2):
            low = (probs[i] * (d_probs[i] - dot_sum)).astype(bf16)
            at = pl.ds(i * rows, rows)
            d_k, d_v = tn(low, qh), tn(probs[i].astype(bf16), gh)
            if h > 0:
                d_k, d_v = d_k + dk_ref[at, :], d_v + dv_ref[at, :]
            elif last:
                d_k, d_v = d_k + dk_in[at, :], d_v + dv_in[at, :]
            dk_ref[at, :] = d_k
            dv_ref[at, :] = d_v
            dq_h = dq_h + nn(low, ks[i][...])
        dq = jnp.where(hit, dq_h, dq)
    dq = dq * scale
    sum_q = jnp.sum(dq, axis=0, keepdims=True)
    if not last:
        dq0_ref[...] = dq.astype(bf16)
        sumq_ref[...] = sum_q
        return
    sums_ref[0:1, :] = sum_q + sumq_ref[...]
    sums_ref[1:2, :] = jnp.sum(dv_ref[...], axis=0, keepdims=True)
    g0_ref[:, :width] = dq0_ref[...]
    g1_ref[:, :width] = dq.astype(bf16)
    for i, ref in enumerate((g0_ref, g1_ref)):
        at = pl.ds(i * rows, rows)
        ref[:, width : 2 * width] = dk_ref[at, :].astype(bf16)
        ref[:, 2 * width :] = dv_ref[at, :].astype(bf16)


def attend_back(proj_q, proj, seg_q, seg_k, lse, one, w_out, scale, heads, earlier=None):
    rows, width = proj_q.shape[0], heads * HEAD_DIM
    d = w_out.shape[1]
    last = earlier is not None
    in_specs = (
        [pl.BlockSpec((rows, width), whole(0, 0))]
        + [pl.BlockSpec((rows, width), whole(0, 1))] * 2
        + [pl.BlockSpec((rows, width), whole(0, 2))] * 2
        + [
            pl.BlockSpec((rows, 1), whole(0, 0)),
            pl.BlockSpec((1, 2 * rows), whole(0, 0)),
            pl.BlockSpec((rows, 128), whole(0, 0)),
        ]
        + blocks_in(one)
        + [pl.BlockSpec((width, d), whole(0, 0))]
    )
    args = [proj_q, *proj, *proj, seg_q, seg_k, lse, *one, w_out]
    keep = [hbm((rows, d), bf16)]
    sums = [struct((2 * rows, width), f32)] * 2
    if last:
        in_specs += [pl.BlockSpec(e.shape, whole(0, 0)) for e in earlier]
        args += [*earlier]
        out_shape = [struct((rows, 3 * width), bf16)] * 2 + [struct((2, width), f32)] + keep
        scratch = [pltpu.VMEM(o.shape, f32) for o in sums]
    else:
        out_shape = [struct((rows, width), bf16), struct((1, width), f32)] + sums + keep
        scratch = []
    return pl.pallas_call(
        functools.partial(attend_back_kernel, scale, heads, last),
        grid=(1,),
        in_specs=in_specs,
        out_specs=[pl.BlockSpec(o.shape, whole(0, 0)) for o in out_shape],
        out_shape=out_shape,
        scratch_shapes=scratch,
        compiler_params=params(40),
        cost_estimate=cost(80 * rows * rows * width, 8 * MIB, rows * rows * 2 * heads),
        name="attend_back",
    )(*args)


def ffn_kernel(*refs):
    x_refs, refs = refs[:2], refs[2:]
    up_ref, down_ref, bias_ref, act_ref, slope_ref, mine_ref, theirs_ref, x, acc = refs
    step = pl.program_id(0)

    @pl.when(step == 0)
    def _():
        x[...] = stack_rows(x_refs)

    value, slope = gelu_parts(nn(x[...], up_ref[...]) + bias_ref[...])
    low = value.astype(bf16)
    act_ref[...] = low
    slope_ref[...] = slope
    add_up(step, nn(low, down_ref[...]), acc, mine_ref, theirs_ref)


def add_up(step, part, acc, mine_ref, theirs_ref):
    @pl.when(step == 0)
    def _():
        acc[...] = part

    @pl.when(step > 0)
    def _():
        acc[...] += part

    @pl.when(step == pl.num_programs(0) - 1)
    def _():
        half = acc.shape[0] // 2
        mine_ref[...] = acc[:half]
        theirs_ref[...] = acc[half:].astype(bf16)


def ffn(x, w_up, w_down, bias, tile=1024):
    rows, d = 2 * x[0].shape[0], x[0].shape[1]
    half = rows // 2
    ff = w_up.shape[1]
    moving = lambda i: (0, i)
    return pl.pallas_call(
        ffn_kernel,
        grid=(ff // tile,),
        in_specs=[
            *blocks_in(x),
            pl.BlockSpec((d, tile), moving),
            pl.BlockSpec((tile, d), lambda i: (i, 0)),
            pl.BlockSpec((1, tile), moving),
        ],
        out_specs=[
            pl.BlockSpec((rows, tile), moving),
            pl.BlockSpec((rows, tile), moving),
            pl.BlockSpec((half, d), whole(0, 0)),
            pl.BlockSpec((half, d), whole(0, 0)),
            pl.BlockSpec((rows, d), whole(0, 0)),
        ],
        out_shape=[
            hbm((rows, ff), bf16),
            hbm((rows, ff), f32),
            struct((half, d), f32),
            struct((half, d), bf16),
            hbm((rows, d), bf16),
        ],
        scratch_shapes=[pltpu.VMEM((rows, d), f32)],
        compiler_params=params(20),
        cost_estimate=cost(4 * rows * d * ff, 9 * MIB, rows * ff * 2),
        name="ffn",
    )(*x, w_up, w_down, bias)


def ffn_back_kernel(*refs):
    x_refs, refs = refs[:2], refs[2:]
    up_ref, down_ref, slope_ref, low_ref, sum_ref, mine_ref, theirs_ref, x, acc = refs
    step = pl.program_id(0)

    @pl.when(step == 0)
    def _():
        x[...] = stack_rows(x_refs)

    d_up = nt(x[...], down_ref[...]) * slope_ref[...]
    low = d_up.astype(bf16)
    low_ref[...] = low
    sum_ref[...] = jnp.sum(d_up, axis=0, keepdims=True)
    add_up(step, nt(low, up_ref[...]), acc, mine_ref, theirs_ref)


def ffn_back(x, w_up, w_down, slope, tile=1024):
    rows, d = 2 * x[0].shape[0], x[0].shape[1]
    half = rows // 2
    ff = w_up.shape[1]
    moving = lambda i: (0, i)
    return pl.pallas_call(
        ffn_back_kernel,
        grid=(ff // tile,),
        in_specs=[
            *blocks_in(x),
            pl.BlockSpec((d, tile), moving),
            pl.BlockSpec((tile, d), lambda i: (i, 0)),
            pl.BlockSpec((rows, tile), moving),
        ],
        out_specs=[
            pl.BlockSpec((rows, tile), moving),
            pl.BlockSpec((1, tile), moving),
            pl.BlockSpec((half, d), whole(0, 0)),
            pl.BlockSpec((half, d), whole(0, 0)),
            pl.BlockSpec((rows, d), whole(0, 0)),
        ],
        out_shape=[
            hbm((rows, ff), bf16),
            struct((1, ff), f32),
            struct((half, d), f32),
            struct((half, d), bf16),
            hbm((rows, d), bf16),
        ],
        scratch_shapes=[pltpu.VMEM((rows, d), f32)],
        compiler_params=params(20),
        cost_estimate=cost(4 * rows * d * ff, 9 * MIB),
        name="ffn_back",
    )(*x, w_up, w_down, *far(slope))


def lines_of(field, head_width, ff_width):
    return {"qkv": 3 * head_width, "out": head_width, "up": ff_width, "down": ff_width}[field]


def pack_kernel(fields, *refs):
    out_ref, at = refs[-1], 0
    for field, ref in zip(fields, refs):
        if field == "qkv":
            for j in range(3):
                for h in range(0, ref.shape[3], 128):
                    out_ref[at : at + 128, :] = ref[0, j, :, h : h + 128]
                    at += 128
        elif field == "up":
            for h in range(0, ref.shape[2], 128):
                out_ref[at : at + 128, :] = ref[0, :, h : h + 128]
                at += 128
        else:
            out_ref[at : at + ref.shape[1], :] = ref[0]
            at += ref.shape[1]


def pack(parts, args):
    fields = [f for f, _ in parts]
    ins = [args[f] for f in fields]
    piece = args["up"].shape[1]
    if piece != 128:
        flat = {
            "qkv": lambda a, l: a[l].transpose(0, 2, 1).reshape(-1, piece),
            "up": lambda a, l: a[l].T,
            "out": lambda a, l: a[l],
            "down": lambda a, l: a[l],
        }
        return jnp.concatenate([flat[f](args[f], l) for f, l in parts], 0)
    lines = sum(a.size // a.shape[0] for a in ins) // piece
    return pl.pallas_call(
        functools.partial(pack_kernel, fields),
        grid=(1,),
        in_specs=[
            pl.BlockSpec((1,) + args[f].shape[1:], whole(l, *([0] * (args[f].ndim - 1))))
            for f, l in parts
        ],
        out_specs=pl.BlockSpec((lines, piece), whole(0, 0)),
        out_shape=struct((lines, piece), bf16),
        compiler_params=params(12),
        cost_estimate=cost(0, 4 * lines * piece),
        name="pack",
    )(*far(*ins))


def maps_kernel(group_rows, lengths_ref, order_ref, spot_ref, src_ref, segc_ref, segr_ref):
    group, slot, rows = spot_ref[0], spot_ref[1], group_rows // 4
    base = group * SEQ_GRP
    lens = [lengths_ref[base + i] for i in range(SEQ_GRP)]
    starts = [0, lens[0], lens[0] + lens[1]]
    end, ends, shifts = 0, [], []
    for j in range(SEQ_GRP):
        seq = order_ref[base + j] - base
        length, start = lens[SEQ_GRP - 1], starts[SEQ_GRP - 1]
        for i in range(SEQ_GRP - 1):
            length = jnp.where(seq == i, lens[i], length)
            start = jnp.where(seq == i, starts[i], start)
        shifts.append(start - end)
        end = end + length
        ends.append(end)

    def turn(x):
        return x % 2 * 2 + x // 2

    def position(shape, axis):
        at = lax.broadcasted_iota(jnp.int32, shape, axis)
        return jnp.bitwise_xor(turn(at // rows), slot) * rows + at % rows

    def segment(place):
        return sum((place >= e).astype(jnp.int32) for e in ends)

    segr_ref[...] = segment(position(segr_ref.shape, 1))
    place = position(segc_ref.shape, 0)
    seg = segment(place)
    segc_ref[...] = seg
    source = place
    for j in range(SEQ_GRP):
        source = jnp.where(seg == j, place + shifts[j], source)
    src_ref[...] = turn(jnp.bitwise_xor(source // rows, slot)) * rows + source % rows


def maps(lengths, order, spot, group_rows):
    outs = [struct((group_rows, 1), jnp.int32)] * 2 + [struct((1, group_rows), jnp.int32)]
    return pl.pallas_call(
        functools.partial(maps_kernel, group_rows),
        grid=(1,),
        in_specs=[SCALARS] * 3,
        out_specs=blocks_in(outs),
        out_shape=outs,
        compiler_params=params(8),
        cost_estimate=cost(100 * group_rows, 8 * group_rows),
        name="maps",
    )(lengths, order, spot)


def tile_at(where_ref, spec):
    masked, d, core = spec
    d = jnp.bitwise_xor(where_ref[0], d) if masked else d
    tile = 2 * d + jnp.bitwise_xor(where_ref[1], core)
    return pl.ds(pl.multiple_of(tile * 128, 128), 128)


def tile_order(where, specs):
    return jnp.stack([2 * (where[0] ^ d if m else d) + (where[1] ^ core) for m, d, core in specs])


def place_kernel(fields, counts, specs, where_ref, *refs):
    ins, outs = refs[: len(counts)], refs[len(counts) :]
    k = 0
    for ref, count in zip(ins, counts):
        for i in range(count):
            here = tile_at(where_ref, specs[k])
            at = 0
            for field, out in zip(fields, outs):
                if field == "qkv":
                    for j in range(3):
                        for h in range(0, out.shape[2], 128):
                            out[j, here, h : h + 128] = ref[i, at : at + 128, :]
                            at += 128
                elif field == "up":
                    for h in range(0, out.shape[1], 128):
                        out[here, h : h + 128] = ref[i, at : at + 128, :]
                        at += 128
                else:
                    out[:, here] = ref[i, at : at + out.shape[0], :]
                    at += out.shape[0]
            k += 1


def place(fields, stacks, specs, where, head_width, ff_width):
    counts = [s.shape[0] for s in stacks]
    piece = stacks[0].shape[2]
    if piece != 128:
        tiles = jnp.take(jnp.concatenate(stacks, 0), jnp.argsort(tile_order(where, specs)), axis=0)
        flat = tiles.transpose(1, 0, 2).reshape(-1, D)
        found, at = [], 0
        for f in fields:
            lines = lines_of(f, head_width, ff_width)
            part = flat[at : at + lines]
            at += lines
            if f == "qkv":
                part = part.reshape(3, head_width, D).transpose(0, 2, 1)
            found.append(part.T if f == "up" else part)
        return found
    shapes = {
        "qkv": (3, D, head_width),
        "out": (head_width, D),
        "up": (D, ff_width),
        "down": (ff_width, D),
    }
    outs = [struct(shapes[f], bf16) for f in fields]
    return pl.pallas_call(
        functools.partial(place_kernel, fields, counts, specs),
        grid=(1,),
        in_specs=[SCALARS] + blocks_in(stacks),
        out_specs=blocks_in(outs),
        out_shape=outs,
        compiler_params=params(20),
        cost_estimate=cost(0, 4 * sum(s.size for s in stacks)),
        name="place",
    )(where, *far(*stacks))


def grad_kernel(fields, counts, specs, where_ref, *refs):
    count = len(fields)
    ins, refs = refs[: 4 * count], refs[4 * count :]
    outs, bufs, sems = refs[: len(counts)], refs[len(counts) : -1], refs[-1]
    rows = ins[0].shape[0]
    copies = []
    for n in range(4 * count):
        there = bufs[n // 2].at[pl.ds(n % 2 * rows, rows), :]
        copies.append(pltpu.make_async_copy(ins[n], there, sems.at[n]))
        copies[-1].start()
    spots = [(out, i) for out, total in zip(outs, counts) for i in range(total)]
    at = 0
    for n, field in enumerate(fields):
        for copy in copies[4 * n : 4 * n + 4]:
            copy.wait()
        a_ref, b_ref = bufs[2 * n : 2 * n + 2]
        b = b_ref[...]
        lines = b.shape[1]
        for g in range(0, len(specs), 4):
            a = jnp.concatenate([a_ref[:, tile_at(where_ref, t)] for t in specs[g : g + 4]], 1)
            by_rows = field in ("qkv", "up")
            total = (tn(a, b) if by_rows else tn(b, a)).astype(bf16)
            for k, (out, i) in enumerate(spots[g : g + 4]):
                tile = slice(k * 128, (k + 1) * 128)
                if by_rows:
                    for h in range(0, lines, 128):
                        out[i, at + h : at + h + 128, :] = total[tile, h : h + 128]
                else:
                    out[i, at : at + lines, :] = total[:, tile]
        at += lines


def weight_grad(fields, pairs, specs, counts, where):
    flat = [r for a, b in pairs for r in (*a, *b)]
    lines = sum(b[0].shape[1] for _, b in pairs)
    rows = sum(b.shape[0] for b in pairs[0][1])
    piece = D // len(specs)
    if piece != 128:
        products = [dot(jnp.concatenate(b, 0), jnp.concatenate(a, 0), 0, 0) for a, b in pairs]
        tiles = jnp.concatenate(products, 0).astype(bf16).reshape(lines, len(specs), piece)
        tiles = jnp.take(tiles.transpose(1, 0, 2), tile_order(where, specs), axis=0)
        ends = [sum(counts[: i + 1]) for i in range(len(counts))]
        return [tiles[e - n : e] for e, n in zip(ends, counts)]
    kind = struct if len(counts) > 1 else hbm
    outs = [kind((n, lines, piece), bf16) for n in counts]
    bufs = [pltpu.VMEM((rows, r.shape[1]), bf16) for r in flat[::2]]
    return pl.pallas_call(
        functools.partial(grad_kernel, fields, counts, specs),
        grid=(1,),
        in_specs=[SCALARS] + [ROWS] * len(flat),
        out_specs=blocks_in(outs),
        out_shape=outs,
        scratch_shapes=bufs + [pltpu.SemaphoreType.DMA((len(flat),))],
        compiler_params=params(32),
        cost_estimate=cost(2 * rows * D * lines, 12 * MIB),
        name="weight_grad",
    )(where, *far(*flat))


def finish_kernel(fields, has_prev, keep_ref, got_ref, *refs):
    outs = refs[len(fields) if has_prev else 0 :]
    at = 0
    for field, out in zip(fields, outs):
        if field == "qkv":
            for j in range(3):
                for h in range(0, out.shape[3], 128):
                    out[0, j, :, h : h + 128] = keep_ref[at : at + 128, :] + got_ref[at : at + 128, :].astype(f32)
                    at += 128
        elif field == "up":
            for h in range(0, out.shape[2], 128):
                out[0, :, h : h + 128] = keep_ref[at : at + 128, :] + got_ref[at : at + 128, :].astype(f32)
                at += 128
        else:
            n = out.shape[1]
            out[0] = keep_ref[at : at + n, :] + got_ref[at : at + n, :].astype(f32)
            at += n


def finish(fields, keep, got, layer, prev, head_width, ff_width):
    piece = keep.shape[1]
    shapes = {
        "qkv": (3, piece, head_width),
        "out": (head_width, piece),
        "up": (piece, ff_width),
        "down": (ff_width, piece),
    }
    if piece != 128:
        total, at, found = keep + got.astype(f32), 0, []
        for n, f in enumerate(fields):
            lines = lines_of(f, head_width, ff_width)
            part = total[at : at + lines]
            at += lines
            if f == "qkv":
                part = part.reshape(3, head_width, piece).transpose(0, 2, 1)
            part = part.T if f == "up" else part
            base = jnp.zeros((LAYERS,) + shapes[f], f32) if prev is None else prev[n]
            found.append(base.at[layer].set(part))
        return found
    outs = [struct((LAYERS,) + shapes[f], f32) for f in fields]
    specs = [
        pl.BlockSpec((1,) + o.shape[1:], whole(layer, *([0] * (len(o.shape) - 1)))) for o in outs
    ]
    return pl.pallas_call(
        functools.partial(finish_kernel, fields, prev is not None),
        grid=(1,),
        in_specs=[pl.BlockSpec(keep.shape, whole(0, 0))] * 2
        + ([] if prev is None else [pl.BlockSpec(memory_space=pl.ANY)] * len(outs)),
        out_specs=specs,
        out_shape=outs,
        input_output_aliases={} if prev is None else {2 + n: n for n in range(len(outs))},
        compiler_params=params(16),
        cost_estimate=cost(0, 10 * keep.size),
        name="finish",
    )(keep, got, *([] if prev is None else prev))


def deal_kernel(src_ref, *refs):
    raw, outs = stack_rows(refs[:4]), refs[4:]
    rows = outs[0].shape[0]
    spot = lax.broadcasted_iota(jnp.int32, (1, raw.shape[0]), 1)
    hit = src_ref[...] == spot
    dealt = nn(jnp.where(hit, 1.0, 0.0).astype(bf16), raw)
    for i in range(4):
        outs[i][...] = dealt[i * rows : (i + 1) * rows].astype(bf16)
    outs[4][...] = dealt[:rows]


def deal_rows(src, raw):
    rows, d = raw[0].shape
    outs = [struct((rows, d), bf16)] * 4 + [struct((rows, d), f32)]
    outs = pl.pallas_call(
        deal_kernel,
        grid=(1,),
        in_specs=blocks_in((src, *raw)),
        out_specs=blocks_in(outs),
        out_shape=outs,
        compiler_params=params(20),
        cost_estimate=cost(32 * rows * rows * d, 6 * MIB),
        name="deal_rows",
    )(src, *raw)
    return outs[:2], outs[2:4], outs[4]


def total_of(refs):
    total = refs[0][...]
    for ref in refs[1:]:
        total = total + ref[...].astype(f32)
    return total


def norm_kernel(n_terms, bias_row, gain_row, shift_row, *refs):
    terms, (vec_ref, y_ref, low_ref, n_ref, r_ref) = refs[:n_terms], refs[n_terms:]
    row = lambda i: vec_ref[i : i + 1, :]
    v = total_of(terms) + row(bias_row)
    centred = v - jnp.mean(v, axis=-1, keepdims=True)
    r = lax.rsqrt(jnp.mean(centred * centred, axis=-1, keepdims=True) + EPS)
    n = centred * r
    y = n * row(gain_row) + row(shift_row)
    y_ref[...] = y
    low_ref[...] = y.astype(bf16)
    n_ref[...] = n
    r_ref[...] = r


def term_specs(terms):
    shape = terms[0].shape
    return [pl.BlockSpec(shape, whole(0, 0)) for _ in terms]


def norm(terms, vectors, bias_row, gain_row, shift_row):
    shape = terms[0].shape
    outs = [struct(shape, f32), struct(shape, bf16), hbm(shape, f32), struct((shape[0], 1), f32)]
    return pl.pallas_call(
        functools.partial(norm_kernel, len(terms), bias_row, gain_row, shift_row),
        grid=(1,),
        in_specs=term_specs(terms) + [full(vectors)],
        out_specs=blocks_in(outs),
        out_shape=outs,
        compiler_params=params(8),
        cost_estimate=cost(20 * terms[0].size, 2 * MIB),
        name="norm",
    )(*terms, vectors)


def norm_back_kernel(n_terms, gain_row, has_sums, *refs):
    terms, refs = refs[:n_terms], refs[n_terms:]
    n_ref, r_ref, vec_ref = refs[:3]
    dv_ref, low_ref, sums_ref = refs[-3:]
    d_out, n = total_of(terms), n_ref[...]
    dn = d_out * vec_ref[gain_row : gain_row + 1, :]
    dv = r_ref[...] * (
        dn - jnp.mean(dn, axis=-1, keepdims=True) - n * jnp.mean(dn * n, axis=-1, keepdims=True)
    )
    dv_ref[...] = dv
    low_ref[...] = dv.astype(bf16)
    for i, a in enumerate((d_out * n, d_out, dv)):
        column = jnp.sum(a, axis=0, keepdims=True)
        sums_ref[i : i + 1, :] = column + refs[3][i : i + 1, :] if has_sums else column


def norm_back(terms, n, r, vectors, gain_row, sums=None):
    shape = terms[0].shape
    outs = [struct(shape, f32), struct(shape, bf16), struct((3, shape[1]), f32)]
    more = [] if sums is None else [sums]
    return pl.pallas_call(
        functools.partial(norm_back_kernel, len(terms), gain_row, sums is not None),
        grid=(1,),
        in_specs=term_specs(terms) + blocks_in((n, r, vectors, *more)),
        out_specs=blocks_in(outs),
        out_shape=outs,
        compiler_params=params(8),
        cost_estimate=cost(20 * terms[0].size, 3 * MIB),
        name="norm_back",
    )(*terms, n, r, vectors, *more)


def dot(a, b, ca, cb):
    return lax.dot_general(a, b, (((ca,), (cb,)), ((), ())), preferred_element_type=f32)


def swap(a, axis):
    return lax.ppermute(a, axis, SWAP)


def flip_d(a, bit, n_d):
    return lax.ppermute(a, "d", [(i, i ^ (1 << bit)) for i in range(n_d)])


def to_home(a):
    return lax.ppermute(a, ("c", "zh"), [(1, 2), (2, 1)])


def after(a, *marks):
    return lax.optimization_barrier((a,) + marks)[0]


def send_rows(own):
    return (own, swap(own, "c")), swap(own, "zl")


def far_rows(far, *marks):
    if marks:
        far = after(far, *marks)
    return far, swap(far, "c")


def chip_sum(mine, theirs, *arrivals):
    other = swap(after(theirs, *arrivals) if arrivals else theirs, "c")
    return mine, other


def cross_sum(terms):
    total = (terms[0] + terms[1].astype(f32)).astype(bf16)
    return total, swap(total, "zl")


def masks_of(order):
    masks = [0]
    for bit in order:
        masks = masks + [m ^ (1 << bit) for m in masks]
    return masks


def absolute_specs(n_d):
    return [(False, d, core) for d in range(n_d) for core in range(2)]


def reduce_specs(n_d):
    bits = list(range(n_d.bit_length() - 1))
    half = n_d // 2
    order = []
    for core, masks in ((0, masks_of(bits)), (1, masks_of(bits[::-1]))):
        order += [(True, m, core) for m in masks[half:] + masks[:half]]
    return order


class Gather:
    def __init__(self, fields, tile, crossed, widths, pos, where, n_d):
        self.fields, self.pos, self.where, self.n_d = fields, pos, where, n_d
        self.widths, self.tile, self.crossed = widths, tile, crossed

    def cores(self, *marks):
        _, c, zh, _ = self.pos
        same = c == zh
        crossed = after(self.crossed, *marks) if marks else self.crossed
        self.own = jnp.where(same, self.tile, crossed)
        self.other = swap(jnp.where(same, crossed, self.tile), "c")
        return self.other

    def collect(self, *marks):
        self.both = jnp.stack([self.own, self.other])
        both = after(self.both, *marks) if marks else self.both
        self.stacks = [lax.all_gather(both, "d", axis=0, tiled=True)]
        self.specs = absolute_specs(self.n_d)
        return self.stacks[0]

    def weights(self):
        found = place(self.fields, self.stacks, self.specs, self.where, *self.widths)
        return dict(zip(self.fields, found))


class Reduce:
    def __init__(self, fields, pairs, pos, where, n_d, by_halves):
        self.fields, self.pos, self.n_d, self.step = fields, pos, n_d, 0
        specs = reduce_specs(n_d) if by_halves else absolute_specs(n_d)
        counts = [n_d // 2] * 4 if by_halves else [2 * n_d]
        self.stacks = weight_grad(fields, pairs, specs, counts, where)

    def collect(self, *marks):
        both = lax.psum_scatter(after(self.stacks[0], *marks), "d", scatter_dimension=0, tiled=True)
        self.first, self.second = both[0], both[1]
        return both

    def halve(self, *marks):
        bits = list(range(self.n_d.bit_length() - 1))
        if self.step == len(bits):
            return []
        if self.step == 0:
            self.sends, self.keeps = [self.stacks[0], self.stacks[2]], [self.stacks[1], self.stacks[3]]
        sends = lax.optimization_barrier((*self.sends, *marks))[:2] if marks else self.sends
        orders = (bits[::-1], bits)
        gots = [flip_d(a, o[self.step], self.n_d) for a, o in zip(sends, orders)]
        self.step += 1
        half = self.keeps[0].shape[0] // 2
        if self.step < len(bits):
            self.sends = [
                (k[half:].astype(f32) + g[half:].astype(f32)).astype(bf16)
                for k, g in zip(self.keeps, gots)
            ]
            self.keeps = [k[:half].astype(f32) + g[:half].astype(f32) for k, g in zip(self.keeps, gots)]
        else:
            self.first, self.second = (k[0].astype(f32) + g[0].astype(f32) for k, g in zip(self.keeps, gots))
        return gots

    def cores(self, *marks):
        while len(self.stacks) > 1 and self.step < self.n_d.bit_length() - 1:
            self.halve()
        second = self.second.astype(bf16)
        self.other = swap(after(second, *marks) if marks else second, "c")
        self.crossed, self.at = [], 0
        return self.other

    def cross(self, lines, *marks):
        _, c, zh, _ = self.pos
        same = c == zh
        part = slice(self.at, self.at + lines)
        send = jnp.where(same, self.other[part], self.first[part].astype(bf16))
        self.crossed.append(swap(after(send, *marks) if marks else send, "zh"))
        self.at += lines
        return self.crossed[-1]

    def finish(self, outs, layer, widths, *marks):
        _, c, zh, _ = self.pos
        got = jnp.concatenate(self.crossed, 0) if len(self.crossed) > 1 else self.crossed[0]
        first = after(self.first, *marks) if marks else self.first
        keep = jnp.where(c == zh, first.astype(f32), self.other.astype(f32))
        prev = None if outs[self.fields[0]] is None else [outs[f] for f in self.fields]
        outs.update(zip(self.fields, finish(self.fields, keep, got, layer, prev, *widths)))


def gather_small(own, pos, n_d):
    d, c, _, zl = pos
    cur = own
    for axis, me in (("zl", zl), ("c", c)):
        got = swap(cur, axis)
        cur = jnp.where(me == 0, jnp.concatenate([cur, got]), jnp.concatenate([got, cur]))
    for bit in range(n_d.bit_length() - 1):
        got = flip_d(cur, bit, n_d)
        mine = jnp.bitwise_and(jnp.right_shift(d, bit), 1)
        cur = jnp.where(mine == 0, jnp.concatenate([cur, got]), jnp.concatenate([got, cur]))
    return cur


def pick(a, at, axis):
    return lax.dynamic_index_in_dim(a, at, axis, keepdims=False)


def halve_small(cur, me, send):
    view = cur.reshape(2, -1, cur.shape[1])
    return pick(view, me, 0) + send(pick(view, 1 - me, 0))


def body(tokens, cotangent, lengths, order, w_qkv, w_out, w_up, w_down, gains, biases, up_bias):
    rows = tokens.shape[0]
    n_d = lax.axis_size("d")
    n_dev = n_d * 8
    head_width = D // 4
    heads = head_width // HEAD_DIM
    ff_width = FF // 4
    widths = (head_width, ff_width)
    scale = HEAD_DIM ** (-0.5)
    d, c, zh, zl = (lax.axis_index(a) for a in ALL)
    pos = (d, c, zh, zl)
    slot = 2 * c + zl
    where = jnp.stack([d, c]).astype(jnp.int32)
    stay = c == zh
    args = {"qkv": w_qkv.transpose(0, 2, 1, 3), "out": w_out, "up": w_up, "down": w_down}

    tile_a0 = pack((("qkv", 0), ("out", 0)), args)
    a0_crossed = swap(tile_a0, "zh")
    g_a0 = Gather(("qkv", "out"), tile_a0, a0_crossed, widths, pos, where, n_d)
    rest = [("up", 0), ("down", 0), ("qkv", 1), ("out", 1)]
    tile_f1 = pack((("up", 1), ("down", 1)), args)
    tile_rest = pack(rest, args)
    small_own = jnp.concatenate([a.reshape(1, -1) for a in (gains, biases, up_bias)], 1)
    src, seg_col, seg_row = maps(
        lengths, order, jnp.stack([d * 2 + zh, slot]).astype(jnp.int32), 4 * rows
    )
    seg_near, seg_far = seg_col[: 2 * rows], seg_col[2 * rows :]
    g_a0.cores(src, small_own, tile_rest, tile_f1)
    g_a0.collect()
    raw_got = to_home(after(tokens, a0_crossed))
    raw = jnp.where(stay, tokens, raw_got)
    raw_near, raw_far = send_rows(raw)
    rest_crossed = swap(after(tile_rest, raw_got), "zh")
    gathers, at = [], 0
    for n in range(0, len(rest), 2):
        fields = (rest[n][0], rest[n + 1][0])
        lines = sum(lines_of(f, *widths) for f in fields)
        part = slice(at, at + lines)
        gathers.append(Gather(fields, tile_rest[part], rest_crossed[part], widths, pos, where, n_d))
        at += lines
    g_f0, g_a1 = gathers
    x_near, x_far, hidden = deal_rows(src, [*raw_near, *far_rows(raw_far)])
    small_near = gather_small(after(small_own, x_near[0]), pos, n_d)
    small_far = swap(small_near, "zh")
    width = D // n_dev
    up_width = FF // n_dev
    n_vec = LAYERS * 8
    small_all = jnp.where(zh == 0, jnp.stack([small_near, small_far]), jnp.stack([small_far, small_near]))
    small_all = small_all.reshape(2, n_d * 2, 2, -1)
    vectors = small_all[..., : n_vec * width].reshape(2, n_d * 2, 2, n_vec, width)
    vectors = vectors.transpose(3, 1, 0, 2, 4).reshape(n_vec, D)
    ups = small_all[..., n_vec * width :].reshape(2, n_d * 2, 2, LAYERS, up_width)
    ups = ups.transpose(3, 1, 0, 2, 4).reshape(LAYERS, FF)
    ups = lax.dynamic_slice(ups, (0, slot * ff_width), (LAYERS, ff_width))
    own_vectors = lax.dynamic_slice(vectors, (0, slot * head_width), (n_vec, head_width))
    gain_row = lambda layer, i: 2 * layer + i
    bias_row = lambda layer, i: 2 * LAYERS + 6 * layer + i
    f0_other = g_f0.cores(small_near)
    g_f0.collect()
    cot_got = to_home(after(cotangent, f0_other, small_far))
    cot_near, cot_sent = send_rows(jnp.where(stay, cotangent, cot_got))
    f1_crossed = swap(after(tile_f1, cot_got), "zh")
    g_f1 = Gather(("up", "down"), tile_f1, f1_crossed, widths, pos, where, n_d)
    weights = [g_a0.weights(), {}]

    kept = []
    x_sent = None
    for layer in range(LAYERS):
        first = layer == 0
        w = weights[layer]
        q_row, v_row = bias_row(layer, 0), bias_row(layer, 1)
        add = jnp.concatenate(
            [
                own_vectors[q_row : q_row + 1],
                jnp.zeros((1, head_width), f32),
                own_vectors[v_row : v_row + 1],
            ],
            1,
        )
        if first:
            x_near = (after(x_near[0], g_f0.both), x_near[1])
        proj_near, keep_near = project(x_near, w["qkv"], add)
        if not first:
            x_far = far_rows(x_sent, keep_near)
        proj_far, keep_far = project(x_far, w["qkv"], add)
        proj = (proj_near, proj_far)
        x_kept = (keep_near, keep_far)
        due = [cot_got] if first else []
        att_far, lse_far, mine, theirs = attend(
            proj_far, proj, seg_far, seg_row, w["out"], scale, heads
        )
        chip, crossed = cross_sum(chip_sum(mine, theirs, *due))
        att_near, lse_near, mine, theirs = attend(
            after(proj_near, chip), proj, seg_near, seg_row, w["out"], scale, heads
        )
        terms = chip_sum(mine, theirs, crossed)
        if first:
            terms = (terms[0], after(terms[1], f1_crossed))
        terms = (*terms, crossed)
        at = [bias_row(layer, 2), gain_row(layer, 0), bias_row(layer, 3)]
        normed, low, n_one, r_one = norm((hidden, *terms), vectors, *at)
        n_near, n_sent = send_rows(low)
        due = [n_sent]
        if first:
            w.update(g_f0.weights())
            g_a1.cores(low)
            g_a1.collect()
        else:
            w.update(g_f1.weights())
        u_bias = ups[layer : layer + 1]
        act_near, slope_near, mine_near, theirs_near, keep_near = ffn(n_near, w["up"], w["down"], u_bias)
        near = chip_sum(mine_near, theirs_near, *due)
        n_far = far_rows(n_sent, keep_near)
        due = []
        act_far, slope_far, mine, theirs, keep_far = ffn(n_far, w["up"], w["down"], u_bias)
        chip, crossed = cross_sum(chip_sum(mine, theirs, *due))
        if first:
            g_f1.cores(chip)
            g_f1.collect()
        at = [bias_row(layer, 4), gain_row(layer, 1), bias_row(layer, 5)]
        hidden, low, n_two, r_two = norm((normed, *near, crossed), vectors, *at)
        kept.append(
            dict(
                x=x_kept, proj=proj, lse=(lse_near, lse_far), att=(att_near, att_far),
                one=(n_one, r_one), n=(keep_near, keep_far), slope=(slope_near, slope_far),
                act=(act_near, act_far), two=(n_two, r_two),
            )
        )
        if first:
            weights[1].update(g_a1.weights())
            x_near, x_sent = send_rows(low)
    last_low = low

    deal = (src[:rows] == jnp.arange(4 * rows, dtype=jnp.int32)[None, :]).astype(bf16)
    cot = jnp.concatenate([*cot_near, *far_rows(cot_sent)], 0)
    valid = (seg_near[:rows] < SEQ_GRP).astype(f32)
    grad_y = (dot(deal, cot, 1, 0) * valid,)
    vector_sums = [None] * LAYERS
    up_sums = [None] * LAYERS
    late = None

    def spot(vec, full_width):
        return lax.dynamic_update_slice(jnp.zeros((1, full_width), f32), vec, (0, slot * vec.shape[1]))

    for layer in reversed(range(LAYERS)):
        w, k = weights[layer], kept[layer]
        d_two, low, sums_two = norm_back(grad_y, *k["two"], vectors, gain_row(layer, 1))
        two_near, two_sent = send_rows(low)
        if late:
            late[0].cores(low)
        up_near, sum_near, mine_near, theirs_near, keep_two_near = ffn_back(
            two_near, w["up"], w["down"], k["slope"][0]
        )
        near = chip_sum(mine_near, theirs_near, two_sent)
        two_far = far_rows(two_sent, up_near)
        due = []
        if late:
            due += [late[0].cross(ff_width, up_near)]
        up_far, sum_far, mine, theirs, keep_two_far = ffn_back(
            two_far, w["up"], w["down"], k["slope"][1]
        )
        chip, crossed = cross_sum(chip_sum(mine, theirs, *due))
        two_pair = ((keep_two_near, keep_two_far), (k["act"][0], after(k["act"][1], chip)))
        up_pair = (k["n"], (up_near, after(up_far, chip)))
        due = []
        if late:
            due += [late[0].cross(ff_width, chip)]
            r_down = Reduce(("down",), (two_pair,), pos, where, n_d, True)
            down_got = r_down.halve()
            up_pair = (up_pair[0], (up_near, after(up_far, r_down.stacks[0])))
            r_ff = Reduce(("up",), (up_pair,), pos, where, n_d, True)
            up_got = r_ff.halve()
        else:
            r_ff = Reduce(("up", "down"), (up_pair, two_pair), pos, where, n_d, False)
        d_two = after(d_two, r_ff.stacks[0], *due)
        d_one, low, sums_one = norm_back((d_two, *near, crossed), *k["one"], vectors, gain_row(layer, 0))
        one_near, one_sent = send_rows(low)
        if not late:
            r_ff.collect(low)
        *earlier, keep_one_near = attend_back(
            k["proj"][0], k["proj"], seg_near, seg_row, k["lse"][0], one_near, w["out"], scale, heads
        )
        one_far = far_rows(one_sent, earlier[0])
        due = []
        if late:
            earlier[0] = after(earlier[0], *down_got, *up_got)
            due += r_down.halve(earlier[0]) + r_ff.halve(earlier[0])
            late[1].cores(earlier[0])
            due += [late[1].cross(4 * head_width, earlier[0])]
        else:
            mixed_got = to_home(after(last_low, earlier[0]))
            due += [mixed_got]
        d_near, d_far, head_sums, keep_one_far = attend_back(
            k["proj"][1], k["proj"], seg_far, seg_row, k["lse"][1], one_far, w["out"], scale, heads,
            earlier,
        )
        if late:
            outs = {f: None for f in ("qkv", "out", "up", "down")}
            late[0].finish(outs, 1, widths, earlier[0])
            due += [outs["up"]]
        d_far = after(d_far, *due)
        mine, theirs = input_grad(d_far, w["qkv"])
        chip, crossed = cross_sum(chip_sum(mine, theirs))
        att_pairs = ((k["x"], (d_near, after(d_far, chip))), ((keep_one_near, keep_one_far), k["att"]))
        if late:
            r_att = Reduce(("qkv", "out"), att_pairs, pos, where, n_d, True)
            r_att.halve()
            d_near = after(d_near, r_att.stacks[0])
            near = chip_sum(*input_grad(d_near, w["qkv"]))
        else:
            near = chip_sum(*input_grad(after(d_near, chip), w["qkv"]))
            att_pairs = ((k["x"], (after(d_near, near[1]), d_far)), att_pairs[1])
            r_att = Reduce(("qkv", "out"), att_pairs, pos, where, n_d, False)
            late = (r_ff, r_att)
            d_one = after(d_one, r_att.stacks[0])
            r_att.collect(crossed)
        grad_y = (d_one, *near, crossed)
        vector_sums[layer] = (
            [sums_one[0:1], sums_two[0:1]],
            [
                spot(head_sums[0:1], D), spot(head_sums[1:2], D), sums_one[2:3],
                sums_one[1:2], sums_two[2:3], sums_two[1:2],
            ],
        )
        up_sums[layer] = spot(sum_near + sum_far, FF)

    r_down.cores(d_far)
    down_crossed = r_down.cross(ff_width)
    r_ff.cores(d_far)
    up_crossed = r_ff.cross(ff_width, down_crossed)
    att_got = r_att.halve(down_crossed)
    base, mine, other, crossed = grad_y
    own_grad = (base + mine + other.astype(f32) + crossed.astype(f32)).astype(bf16)
    grad_got = to_home(after(own_grad, *att_got))
    r_att.cores(up_crossed)
    r_att.cross(4 * head_width)
    late[1].finish(outs, 1, widths, *att_got)
    r_down.finish(outs, 0, widths, *att_got)
    r_ff.finish(outs, 0, widths, *att_got)
    r_att.finish(outs, 0, widths)
    tokens_grad = jnp.where(stay, own_grad, grad_got).astype(f32)
    mixed = jnp.where(stay, last_low, after(mixed_got, *att_got))

    terms = jnp.concatenate(
        [g for s in vector_sums for g in s[0]] + [b for s in vector_sums for b in s[1]], 0
    )
    small = jnp.concatenate(
        [
            terms.reshape(n_vec, n_dev, width).transpose(1, 0, 2).reshape(n_dev, n_vec * width),
            jnp.concatenate(up_sums, 0)
            .reshape(LAYERS, n_dev, up_width)
            .transpose(1, 0, 2)
            .reshape(n_dev, LAYERS * up_width),
        ],
        1,
    )
    n_small = small.shape[1]
    small = after(small, *att_got).reshape(n_d, 2, 4 * n_small)
    small = pick(small, c, 1) + swap(pick(small, 1 - c, 1), "c")
    small = small.reshape(n_d, 2, 2, n_small)
    small = pick(small, zl, 2) + swap(pick(small, 1 - zl, 2), "zl")
    small = small.reshape(n_d, 2 * n_small)
    for bit in reversed(range(n_d.bit_length() - 1)):
        mine = jnp.bitwise_and(jnp.right_shift(d, bit), 1)
        small = halve_small(small, mine, lambda a, bit=bit: flip_d(a, bit, n_d))
    small_sum = halve_small(small.reshape(2, n_small), zh, lambda a: swap(a, "zh"))
    n_gain = LAYERS * 2 * width
    g_gains = small_sum[:, :n_gain].reshape(LAYERS, 2, width)
    g_biases = small_sum[:, n_gain : n_vec * width].reshape(LAYERS, 6, width)
    g_upb = small_sum[:, n_vec * width :].reshape(LAYERS, up_width)
    g_qkv = outs["qkv"].transpose(0, 2, 1, 3)
    return mixed, tokens_grad, g_qkv, outs["out"], outs["up"], outs["down"], g_gains, g_biases, g_upb


def solution(mesh):
    n_dp, n_t = mesh.shape["dp"], mesh.shape["tensor"]
    fine = Mesh(mesh.devices.reshape(n_dp // 2, 2, n_t // 2, 2), ALL)
    dp, t = ("d", "c"), ("zh", "zl")
    return jax.shard_map(
        body,
        mesh=fine,
        in_specs=(
            P(ALL, None),
            P(ALL, None),
            P(),
            P(),
            P(None, dp, None, t),
            P(None, t, dp),
            P(None, dp, t),
            P(None, t, dp),
            P(None, None, ALL),
            P(None, None, ALL),
            P(None, ALL),
        ),
        out_specs=(
            P(ALL, None),
            P(ALL, None),
            P(None, dp, None, t),
            P(None, t, dp),
            P(None, dp, t),
            P(None, t, dp),
            P(None, None, ALL),
            P(None, None, ALL),
            P(None, ALL),
        ),
        check_vma=False,
    )
```

```python
import functools

import jax
import jax.numpy as jnp
from jax import lax
from jax.experimental import pallas as pl
from jax.experimental.pallas import tpu as pltpu
from jax.sharding import Mesh, PartitionSpec as P

D = 1024
HEAD_DIM = 64
FF = 4096
LAYERS = 2
SEQ_GRP = 3

EPS = 1e-05
NEG = -1e30
ALL = ("d", "c", "zh", "zl")
SWAP = [(0, 1), (1, 0)]
bf16 = jnp.bfloat16
f32 = jnp.float32
MIB = 1 << 20

TAIL_STEP = 0.24
TAIL = (
    0.0912286469891869,
    0.14294535326111468,
    -0.11556713177962434,
    0.5630756863681534,
    -0.5892310046041954,
    0.5271447780474939,
    -0.11959632556906954,
)
INV_SQRT_2PI = 0.3989422804014327


def nn(a, b):
    return lax.dot_general(a, b, (((1,), (0,)), ((), ())), preferred_element_type=f32)


def nt(a, b):
    return lax.dot_general(a, b, (((1,), (1,)), ((), ())), preferred_element_type=f32)


def tn(a, b):
    return lax.dot_general(a, b, (((0,), (0,)), ((), ())), preferred_element_type=f32)


def stack_rows(refs):
    return jnp.concatenate([r[...] for r in refs], 0)


def params(limit):
    return pltpu.CompilerParams(vmem_limit_bytes=limit * MIB)


def cost(flops, nbytes, exps=0):
    return pl.CostEstimate(flops=int(flops), bytes_accessed=int(nbytes), transcendentals=int(exps))


def struct(shape, dtype):
    return jax.ShapeDtypeStruct(shape, dtype)


def hbm(shape, dtype):
    return pltpu.HBM(shape, dtype)


def far(*arrays):
    return [pltpu.with_memory_space_constraint(a, pltpu.HBM) for a in arrays]


SCALARS = pl.BlockSpec(memory_space=pltpu.SMEM)
ROWS = pl.BlockSpec(memory_space=pltpu.HBM)


def full(a):
    shape = a.shape
    return pl.BlockSpec(shape, lambda *_: (0,) * len(shape))


def blocks_in(arrays):
    return [full(a) for a in arrays]


def gelu_parts(u):
    z = jnp.abs(u)
    bell = jnp.exp(-0.5 * (u * u))
    below = 1.0 + TAIL_STEP * z
    t = pl.reciprocal(below, approx=True)
    t = t * (2.0 - below * t)
    poly = jnp.full_like(t, TAIL[-1])
    for coef in TAIL[-2::-1]:
        poly = poly * t + coef
    tail = bell * (poly * t)
    phi = jnp.where(u > 0.0, 1.0 - tail, tail)
    return u * phi, phi + u * (INV_SQRT_2PI * bell)


def whole(*at):
    return lambda i: at


def project_kernel(*refs):
    x_refs, (w_ref, add_ref, out_ref, x_ref) = refs[:2], refs[2:]
    x = stack_rows(x_refs)
    x_ref[...] = x
    width = w_ref.shape[2]
    for j in range(3):
        at = slice(j * width, (j + 1) * width)
        out_ref[:, at] = (nn(x, w_ref[j]) + add_ref[:, at]).astype(bf16)


def project(x, w_qkv, add):
    rows = 2 * x[0].shape[0]
    _, d, width = w_qkv.shape
    outs = [struct((rows, 3 * width), bf16), hbm((rows, d), bf16)]
    return pl.pallas_call(
        project_kernel,
        grid=(1,),
        in_specs=blocks_in((*x, w_qkv, add)),
        out_specs=blocks_in(outs),
        out_shape=outs,
        compiler_params=params(16),
        cost_estimate=cost(6 * rows * d * width, 4 * MIB),
        name="project",
    )(*x, w_qkv, add)


def input_grad_kernel(g_ref, w_ref, mine_ref, theirs_ref):
    width = w_ref.shape[2]
    part = sum(nt(g_ref[:, j * width : (j + 1) * width], w_ref[j]) for j in range(3))
    half = part.shape[0] // 2
    mine_ref[...] = part[:half]
    theirs_ref[...] = part[half:].astype(bf16)


def input_grad(d_proj, w_qkv):
    rows = d_proj.shape[0]
    _, d, width = w_qkv.shape
    outs = [struct((rows // 2, d), f32), struct((rows // 2, d), bf16)]
    return pl.pallas_call(
        input_grad_kernel,
        grid=(1,),
        in_specs=blocks_in((d_proj, w_qkv)),
        out_specs=blocks_in(outs),
        out_shape=outs,
        compiler_params=params(16),
        cost_estimate=cost(6 * rows * d * width, 4 * MIB),
        name="input_grad",
    )(d_proj, w_qkv)


def attend_kernel(scale, heads, q_ref, k0_ref, k1_ref, v0_ref, v1_ref, segq_ref, segk_ref, w_ref, *outs):
    att_ref, lse_ref, mine_ref, theirs_ref = outs
    q = q_ref[...] * jnp.asarray(scale, bf16)
    rows, width = q.shape
    ks, vs = (k0_ref, k1_ref), (v0_ref, v1_ref)
    kv_rows = k0_ref.shape[0]
    lane = lax.broadcasted_iota(jnp.int32, (1, width), 1) // HEAD_DIM
    stat_lane = lax.broadcasted_iota(jnp.int32, (1, 128), 1)
    out = jnp.zeros((rows, width), f32)
    lse = jnp.zeros((rows, 128), f32)
    segq = segq_ref[...]
    masks = [
        jnp.where(segq == segk_ref[:, i * kv_rows : (i + 1) * kv_rows], 0.0, NEG) for i in range(2)
    ]
    for h in range(heads):
        hit = lane == h
        qh = jnp.where(hit, q, jnp.zeros_like(q))
        scores = [nt(qh, ks[i][...]) + masks[i] for i in range(2)]
        peak = jnp.maximum(*[jnp.max(s, axis=1, keepdims=True) for s in scores])
        exps = [jnp.exp(s - peak) for s in scores]
        total = sum(jnp.sum(e, axis=1, keepdims=True) for e in exps)
        inv = 1.0 / total
        head_out = sum(nn((exps[i] * inv).astype(bf16), vs[i][...]) for i in range(2))
        out = jnp.where(hit, head_out, out)
        lse = jnp.where(stat_lane == h, peak + jnp.log(total), lse)
    low = out.astype(bf16)
    att_ref[...] = low
    lse_ref[...] = lse
    part = nn(low, w_ref[...])
    half = rows // 2
    mine_ref[...] = part[:half]
    theirs_ref[...] = part[half:].astype(bf16)


def attend(proj_q, proj, seg_q, seg_k, w_out, scale, heads):
    rows, width = proj_q.shape[0], heads * HEAD_DIM
    d = w_out.shape[1]
    return pl.pallas_call(
        functools.partial(attend_kernel, scale, heads),
        grid=(1,),
        in_specs=[pl.BlockSpec((rows, width), whole(0, 0))]
        + [pl.BlockSpec((rows, width), whole(0, 1))] * 2
        + [pl.BlockSpec((rows, width), whole(0, 2))] * 2
        + [
            pl.BlockSpec((rows, 1), whole(0, 0)),
            pl.BlockSpec((1, 2 * rows), whole(0, 0)),
            pl.BlockSpec((width, d), whole(0, 0)),
        ],
        out_specs=[
            pl.BlockSpec((rows, width), whole(0, 0)),
            pl.BlockSpec((rows, 128), whole(0, 0)),
            pl.BlockSpec((rows // 2, d), whole(0, 0)),
            pl.BlockSpec((rows // 2, d), whole(0, 0)),
        ],
        out_shape=[
            hbm((rows, width), bf16),
            hbm((rows, 128), f32),
            struct((rows // 2, d), f32),
            struct((rows // 2, d), bf16),
        ],
        compiler_params=params(28),
        cost_estimate=cost(32 * rows * rows * width, 6 * MIB, rows * rows * 2 * heads),
        name="attend",
    )(proj_q, *proj, *proj, seg_q, seg_k, w_out)


def attend_back_kernel(scale, heads, last, *refs):
    q_ref, k0_ref, k1_ref, v0_ref, v1_ref, segq_ref, segk_ref, lse_ref = refs[:8]
    one_refs, w_ref, refs = refs[8:10], refs[10], refs[11:]
    q = q_ref[...]
    rows, width = q.shape
    ks, vs = (k0_ref, k1_ref), (v0_ref, v1_ref)
    if last:
        dq0_ref, sumq_ref, dk_in, dv_in = refs[:4]
        g0_ref, g1_ref, sums_ref, keep_ref, dk_ref, dv_ref = refs[4:]
    else:
        dq0_ref, sumq_ref, dk_ref, dv_ref, keep_ref = refs
    lane = lax.broadcasted_iota(jnp.int32, (1, width), 1) // HEAD_DIM
    one = stack_rows(one_refs)
    keep_ref[...] = one
    grad = nt(one, w_ref[...]).astype(bf16)
    segq = segq_ref[...]
    masks = [jnp.where(segq == segk_ref[:, i * rows : (i + 1) * rows], 0.0, NEG) for i in range(2)]
    sc = jnp.asarray(scale, bf16)
    zero = jnp.zeros_like(q)
    dq = jnp.zeros((rows, width), f32)
    for h in range(heads):
        hit = lane == h
        qh = jnp.where(hit, q, zero) * sc
        gh = jnp.where(hit, grad, zero)
        lse = lse_ref[:, h : h + 1]
        probs = [jnp.exp(nt(qh, ks[i][...]) + masks[i] - lse) for i in range(2)]
        d_probs = [nt(gh, vs[i][...]) for i in range(2)]
        dot_sum = sum(jnp.sum(p * g, axis=1, keepdims=True) for p, g in zip(probs, d_probs))
        dq_h = 0.0
        for i in range(2):
            low = (probs[i] * (d_probs[i] - dot_sum)).astype(bf16)
            at = pl.ds(i * rows, rows)
            d_k, d_v = tn(low, qh), tn(probs[i].astype(bf16), gh)
            if h > 0:
                d_k, d_v = d_k + dk_ref[at, :], d_v + dv_ref[at, :]
            elif last:
                d_k, d_v = d_k + dk_in[at, :], d_v + dv_in[at, :]
            dk_ref[at, :] = d_k
            dv_ref[at, :] = d_v
            dq_h = dq_h + nn(low, ks[i][...])
        dq = jnp.where(hit, dq_h, dq)
    dq = dq * scale
    sum_q = jnp.sum(dq, axis=0, keepdims=True)
    if not last:
        dq0_ref[...] = dq.astype(bf16)
        sumq_ref[...] = sum_q
        return
    sums_ref[0:1, :] = sum_q + sumq_ref[...]
    sums_ref[1:2, :] = jnp.sum(dv_ref[...], axis=0, keepdims=True)
    g0_ref[:, :width] = dq0_ref[...]
    g1_ref[:, :width] = dq.astype(bf16)
    for i, ref in enumerate((g0_ref, g1_ref)):
        at = pl.ds(i * rows, rows)
        ref[:, width : 2 * width] = dk_ref[at, :].astype(bf16)
        ref[:, 2 * width :] = dv_ref[at, :].astype(bf16)


def attend_back(proj_q, proj, seg_q, seg_k, lse, one, w_out, scale, heads, earlier=None):
    rows, width = proj_q.shape[0], heads * HEAD_DIM
    d = w_out.shape[1]
    last = earlier is not None
    in_specs = (
        [pl.BlockSpec((rows, width), whole(0, 0))]
        + [pl.BlockSpec((rows, width), whole(0, 1))] * 2
        + [pl.BlockSpec((rows, width), whole(0, 2))] * 2
        + [
            pl.BlockSpec((rows, 1), whole(0, 0)),
            pl.BlockSpec((1, 2 * rows), whole(0, 0)),
            pl.BlockSpec((rows, 128), whole(0, 0)),
        ]
        + blocks_in(one)
        + [pl.BlockSpec((width, d), whole(0, 0))]
    )
    args = [proj_q, *proj, *proj, seg_q, seg_k, lse, *one, w_out]
    keep = [hbm((rows, d), bf16)]
    sums = [struct((2 * rows, width), f32)] * 2
    if last:
        in_specs += [pl.BlockSpec(e.shape, whole(0, 0)) for e in earlier]
        args += [*earlier]
        out_shape = [struct((rows, 3 * width), bf16)] * 2 + [struct((2, width), f32)] + keep
        scratch = [pltpu.VMEM(o.shape, f32) for o in sums]
    else:
        out_shape = [struct((rows, width), bf16), struct((1, width), f32)] + sums + keep
        scratch = []
    return pl.pallas_call(
        functools.partial(attend_back_kernel, scale, heads, last),
        grid=(1,),
        in_specs=in_specs,
        out_specs=[pl.BlockSpec(o.shape, whole(0, 0)) for o in out_shape],
        out_shape=out_shape,
        scratch_shapes=scratch,
        compiler_params=params(40),
        cost_estimate=cost(80 * rows * rows * width, 8 * MIB, rows * rows * 2 * heads),
        name="attend_back",
    )(*args)


def ffn_kernel(*refs):
    x_refs, refs = refs[:2], refs[2:]
    up_ref, down_ref, bias_ref, act_ref, slope_ref, mine_ref, theirs_ref, x, acc = refs
    step = pl.program_id(0)

    @pl.when(step == 0)
    def _():
        x[...] = stack_rows(x_refs)

    value, slope = gelu_parts(nn(x[...], up_ref[...]) + bias_ref[...])
    low = value.astype(bf16)
    act_ref[...] = low
    slope_ref[...] = slope
    add_up(step, nn(low, down_ref[...]), acc, mine_ref, theirs_ref)


def add_up(step, part, acc, mine_ref, theirs_ref):
    @pl.when(step == 0)
    def _():
        acc[...] = part

    @pl.when(step > 0)
    def _():
        acc[...] += part

    @pl.when(step == pl.num_programs(0) - 1)
    def _():
        half = acc.shape[0] // 2
        mine_ref[...] = acc[:half]
        theirs_ref[...] = acc[half:].astype(bf16)


def ffn(x, w_up, w_down, bias, tile=1024):
    rows, d = 2 * x[0].shape[0], x[0].shape[1]
    half = rows // 2
    ff = w_up.shape[1]
    moving = lambda i: (0, i)
    return pl.pallas_call(
        ffn_kernel,
        grid=(ff // tile,),
        in_specs=[
            *blocks_in(x),
            pl.BlockSpec((d, tile), moving),
            pl.BlockSpec((tile, d), lambda i: (i, 0)),
            pl.BlockSpec((1, tile), moving),
        ],
        out_specs=[
            pl.BlockSpec((rows, tile), moving),
            pl.BlockSpec((rows, tile), moving),
            pl.BlockSpec((half, d), whole(0, 0)),
            pl.BlockSpec((half, d), whole(0, 0)),
            pl.BlockSpec((rows, d), whole(0, 0)),
        ],
        out_shape=[
            hbm((rows, ff), bf16),
            hbm((rows, ff), f32),
            struct((half, d), f32),
            struct((half, d), bf16),
            hbm((rows, d), bf16),
        ],
        scratch_shapes=[pltpu.VMEM((rows, d), f32)],
        compiler_params=params(20),
        cost_estimate=cost(4 * rows * d * ff, 9 * MIB, rows * ff * 2),
        name="ffn",
    )(*x, w_up, w_down, bias)


def ffn_back_kernel(*refs):
    x_refs, refs = refs[:2], refs[2:]
    up_ref, down_ref, slope_ref, low_ref, sum_ref, mine_ref, theirs_ref, x, acc = refs
    step = pl.program_id(0)

    @pl.when(step == 0)
    def _():
        x[...] = stack_rows(x_refs)

    d_up = nt(x[...], down_ref[...]) * slope_ref[...]
    low = d_up.astype(bf16)
    low_ref[...] = low
    sum_ref[...] = jnp.sum(d_up, axis=0, keepdims=True)
    add_up(step, nt(low, up_ref[...]), acc, mine_ref, theirs_ref)


def ffn_back(x, w_up, w_down, slope, tile=1024):
    rows, d = 2 * x[0].shape[0], x[0].shape[1]
    half = rows // 2
    ff = w_up.shape[1]
    moving = lambda i: (0, i)
    return pl.pallas_call(
        ffn_back_kernel,
        grid=(ff // tile,),
        in_specs=[
            *blocks_in(x),
            pl.BlockSpec((d, tile), moving),
            pl.BlockSpec((tile, d), lambda i: (i, 0)),
            pl.BlockSpec((rows, tile), moving),
        ],
        out_specs=[
            pl.BlockSpec((rows, tile), moving),
            pl.BlockSpec((1, tile), moving),
            pl.BlockSpec((half, d), whole(0, 0)),
            pl.BlockSpec((half, d), whole(0, 0)),
            pl.BlockSpec((rows, d), whole(0, 0)),
        ],
        out_shape=[
            hbm((rows, ff), bf16),
            struct((1, ff), f32),
            struct((half, d), f32),
            struct((half, d), bf16),
            hbm((rows, d), bf16),
        ],
        scratch_shapes=[pltpu.VMEM((rows, d), f32)],
        compiler_params=params(20),
        cost_estimate=cost(4 * rows * d * ff, 9 * MIB),
        name="ffn_back",
    )(*x, w_up, w_down, *far(slope))


def lines_of(field, head_width, ff_width):
    return {"qkv": 3 * head_width, "out": head_width, "up": ff_width, "down": ff_width}[field]


def pack_kernel(fields, *refs):
    out_ref, at = refs[-1], 0
    for field, ref in zip(fields, refs):
        if field == "qkv":
            for j in range(3):
                for h in range(0, ref.shape[3], 128):
                    out_ref[at : at + 128, :] = ref[0, j, :, h : h + 128]
                    at += 128
        elif field == "up":
            for h in range(0, ref.shape[2], 128):
                out_ref[at : at + 128, :] = ref[0, :, h : h + 128]
                at += 128
        else:
            out_ref[at : at + ref.shape[1], :] = ref[0]
            at += ref.shape[1]


def pack(parts, args):
    fields = [f for f, _ in parts]
    ins = [args[f] for f in fields]
    piece = args["up"].shape[1]
    if piece != 128:
        flat = {
            "qkv": lambda a, l: a[l].transpose(0, 2, 1).reshape(-1, piece),
            "up": lambda a, l: a[l].T,
            "out": lambda a, l: a[l],
            "down": lambda a, l: a[l],
        }
        return jnp.concatenate([flat[f](args[f], l) for f, l in parts], 0)
    lines = sum(a.size // a.shape[0] for a in ins) // piece
    return pl.pallas_call(
        functools.partial(pack_kernel, fields),
        grid=(1,),
        in_specs=[
            pl.BlockSpec((1,) + args[f].shape[1:], whole(l, *([0] * (args[f].ndim - 1))))
            for f, l in parts
        ],
        out_specs=pl.BlockSpec((lines, piece), whole(0, 0)),
        out_shape=struct((lines, piece), bf16),
        compiler_params=params(12),
        cost_estimate=cost(0, 4 * lines * piece),
        name="pack",
    )(*far(*ins))


def maps_kernel(group_rows, lengths_ref, order_ref, spot_ref, src_ref, segc_ref, segr_ref):
    group, slot, rows = spot_ref[0], spot_ref[1], group_rows // 4
    base = group * SEQ_GRP
    lens = [lengths_ref[base + i] for i in range(SEQ_GRP)]
    starts = [0, lens[0], lens[0] + lens[1]]
    end, ends, shifts = 0, [], []
    for j in range(SEQ_GRP):
        seq = order_ref[base + j] - base
        length, start = lens[SEQ_GRP - 1], starts[SEQ_GRP - 1]
        for i in range(SEQ_GRP - 1):
            length = jnp.where(seq == i, lens[i], length)
            start = jnp.where(seq == i, starts[i], start)
        shifts.append(start - end)
        end = end + length
        ends.append(end)

    def turn(x):
        return x % 2 * 2 + x // 2

    def position(shape, axis):
        at = lax.broadcasted_iota(jnp.int32, shape, axis)
        return jnp.bitwise_xor(turn(at // rows), slot) * rows + at % rows

    def segment(place):
        return sum((place >= e).astype(jnp.int32) for e in ends)

    segr_ref[...] = segment(position(segr_ref.shape, 1))
    place = position(segc_ref.shape, 0)
    seg = segment(place)
    segc_ref[...] = seg
    source = place
    for j in range(SEQ_GRP):
        source = jnp.where(seg == j, place + shifts[j], source)
    src_ref[...] = turn(jnp.bitwise_xor(source // rows, slot)) * rows + source % rows


def maps(lengths, order, spot, group_rows):
    outs = [struct((group_rows, 1), jnp.int32)] * 2 + [struct((1, group_rows), jnp.int32)]
    return pl.pallas_call(
        functools.partial(maps_kernel, group_rows),
        grid=(1,),
        in_specs=[SCALARS] * 3,
        out_specs=blocks_in(outs),
        out_shape=outs,
        compiler_params=params(8),
        cost_estimate=cost(100 * group_rows, 8 * group_rows),
        name="maps",
    )(lengths, order, spot)


def tile_at(where_ref, spec):
    masked, d, core = spec
    d = jnp.bitwise_xor(where_ref[0], d) if masked else d
    tile = 2 * d + jnp.bitwise_xor(where_ref[1], core)
    return pl.ds(pl.multiple_of(tile * 128, 128), 128)


def tile_order(where, specs):
    return jnp.stack([2 * (where[0] ^ d if m else d) + (where[1] ^ core) for m, d, core in specs])


def place_kernel(fields, counts, specs, where_ref, *refs):
    ins, outs = refs[: len(counts)], refs[len(counts) :]
    k = 0
    for ref, count in zip(ins, counts):
        for i in range(count):
            here = tile_at(where_ref, specs[k])
            at = 0
            for field, out in zip(fields, outs):
                if field == "qkv":
                    for j in range(3):
                        for h in range(0, out.shape[2], 128):
                            out[j, here, h : h + 128] = ref[i, at : at + 128, :]
                            at += 128
                elif field == "up":
                    for h in range(0, out.shape[1], 128):
                        out[here, h : h + 128] = ref[i, at : at + 128, :]
                        at += 128
                else:
                    out[:, here] = ref[i, at : at + out.shape[0], :]
                    at += out.shape[0]
            k += 1


def place(fields, stacks, specs, where, head_width, ff_width):
    counts = [s.shape[0] for s in stacks]
    piece = stacks[0].shape[2]
    if piece != 128:
        tiles = jnp.take(jnp.concatenate(stacks, 0), jnp.argsort(tile_order(where, specs)), axis=0)
        flat = tiles.transpose(1, 0, 2).reshape(-1, D)
        found, at = [], 0
        for f in fields:
            lines = lines_of(f, head_width, ff_width)
            part = flat[at : at + lines]
            at += lines
            if f == "qkv":
                part = part.reshape(3, head_width, D).transpose(0, 2, 1)
            found.append(part.T if f == "up" else part)
        return found
    shapes = {
        "qkv": (3, D, head_width),
        "out": (head_width, D),
        "up": (D, ff_width),
        "down": (ff_width, D),
    }
    outs = [struct(shapes[f], bf16) for f in fields]
    return pl.pallas_call(
        functools.partial(place_kernel, fields, counts, specs),
        grid=(1,),
        in_specs=[SCALARS] + blocks_in(stacks),
        out_specs=blocks_in(outs),
        out_shape=outs,
        compiler_params=params(20),
        cost_estimate=cost(0, 4 * sum(s.size for s in stacks)),
        name="place",
    )(where, *far(*stacks))


def grad_kernel(fields, counts, specs, where_ref, *refs):
    count = len(fields)
    ins, refs = refs[: 4 * count], refs[4 * count :]
    outs, bufs, sems = refs[: len(counts)], refs[len(counts) : -1], refs[-1]
    rows = ins[0].shape[0]
    copies = []
    for n in range(4 * count):
        there = bufs[n // 2].at[pl.ds(n % 2 * rows, rows), :]
        copies.append(pltpu.make_async_copy(ins[n], there, sems.at[n]))
        copies[-1].start()
    spots = [(out, i) for out, total in zip(outs, counts) for i in range(total)]
    at = 0
    for n, field in enumerate(fields):
        for copy in copies[4 * n : 4 * n + 4]:
            copy.wait()
        a_ref, b_ref = bufs[2 * n : 2 * n + 2]
        b = b_ref[...]
        lines = b.shape[1]
        for g in range(0, len(specs), 4):
            a = jnp.concatenate([a_ref[:, tile_at(where_ref, t)] for t in specs[g : g + 4]], 1)
            by_rows = field in ("qkv", "up")
            total = (tn(a, b) if by_rows else tn(b, a)).astype(bf16)
            for k, (out, i) in enumerate(spots[g : g + 4]):
                tile = slice(k * 128, (k + 1) * 128)
                if by_rows:
                    for h in range(0, lines, 128):
                        out[i, at + h : at + h + 128, :] = total[tile, h : h + 128]
                else:
                    out[i, at : at + lines, :] = total[:, tile]
        at += lines


def weight_grad(fields, pairs, specs, counts, where):
    flat = [r for a, b in pairs for r in (*a, *b)]
    lines = sum(b[0].shape[1] for _, b in pairs)
    rows = sum(b.shape[0] for b in pairs[0][1])
    piece = D // len(specs)
    if piece != 128:
        products = [dot(jnp.concatenate(b, 0), jnp.concatenate(a, 0), 0, 0) for a, b in pairs]
        tiles = jnp.concatenate(products, 0).astype(bf16).reshape(lines, len(specs), piece)
        tiles = jnp.take(tiles.transpose(1, 0, 2), tile_order(where, specs), axis=0)
        ends = [sum(counts[: i + 1]) for i in range(len(counts))]
        return [tiles[e - n : e] for e, n in zip(ends, counts)]
    kind = struct if len(counts) > 1 else hbm
    outs = [kind((n, lines, piece), bf16) for n in counts]
    bufs = [pltpu.VMEM((rows, r.shape[1]), bf16) for r in flat[::2]]
    return pl.pallas_call(
        functools.partial(grad_kernel, fields, counts, specs),
        grid=(1,),
        in_specs=[SCALARS] + [ROWS] * len(flat),
        out_specs=blocks_in(outs),
        out_shape=outs,
        scratch_shapes=bufs + [pltpu.SemaphoreType.DMA((len(flat),))],
        compiler_params=params(32),
        cost_estimate=cost(2 * rows * D * lines, 12 * MIB),
        name="weight_grad",
    )(where, *far(*flat))


def finish_kernel(fields, has_prev, keep_ref, got_ref, *refs):
    outs = refs[len(fields) if has_prev else 0 :]
    at = 0
    for field, out in zip(fields, outs):
        if field == "qkv":
            for j in range(3):
                for h in range(0, out.shape[3], 128):
                    out[0, j, :, h : h + 128] = keep_ref[at : at + 128, :] + got_ref[at : at + 128, :].astype(f32)
                    at += 128
        elif field == "up":
            for h in range(0, out.shape[2], 128):
                out[0, :, h : h + 128] = keep_ref[at : at + 128, :] + got_ref[at : at + 128, :].astype(f32)
                at += 128
        else:
            n = out.shape[1]
            out[0] = keep_ref[at : at + n, :] + got_ref[at : at + n, :].astype(f32)
            at += n


def finish(fields, keep, got, layer, prev, head_width, ff_width):
    piece = keep.shape[1]
    shapes = {
        "qkv": (3, piece, head_width),
        "out": (head_width, piece),
        "up": (piece, ff_width),
        "down": (ff_width, piece),
    }
    if piece != 128:
        total, at, found = keep + got.astype(f32), 0, []
        for n, f in enumerate(fields):
            lines = lines_of(f, head_width, ff_width)
            part = total[at : at + lines]
            at += lines
            if f == "qkv":
                part = part.reshape(3, head_width, piece).transpose(0, 2, 1)
            part = part.T if f == "up" else part
            base = jnp.zeros((LAYERS,) + shapes[f], f32) if prev is None else prev[n]
            found.append(base.at[layer].set(part))
        return found
    outs = [struct((LAYERS,) + shapes[f], f32) for f in fields]
    specs = [
        pl.BlockSpec((1,) + o.shape[1:], whole(layer, *([0] * (len(o.shape) - 1)))) for o in outs
    ]
    return pl.pallas_call(
        functools.partial(finish_kernel, fields, prev is not None),
        grid=(1,),
        in_specs=[pl.BlockSpec(keep.shape, whole(0, 0))] * 2
        + ([] if prev is None else [pl.BlockSpec(memory_space=pl.ANY)] * len(outs)),
        out_specs=specs,
        out_shape=outs,
        input_output_aliases={} if prev is None else {2 + n: n for n in range(len(outs))},
        compiler_params=params(16),
        cost_estimate=cost(0, 10 * keep.size),
        name="finish",
    )(keep, got, *([] if prev is None else prev))


def deal_kernel(src_ref, *refs):
    raw, outs = stack_rows(refs[:4]), refs[4:]
    rows = outs[0].shape[0]
    spot = lax.broadcasted_iota(jnp.int32, (1, raw.shape[0]), 1)
    hit = src_ref[...] == spot
    dealt = nn(jnp.where(hit, 1.0, 0.0).astype(bf16), raw)
    for i in range(4):
        outs[i][...] = dealt[i * rows : (i + 1) * rows].astype(bf16)
    outs[4][...] = dealt[:rows]


def deal_rows(src, raw):
    rows, d = raw[0].shape
    outs = [struct((rows, d), bf16)] * 4 + [struct((rows, d), f32)]
    outs = pl.pallas_call(
        deal_kernel,
        grid=(1,),
        in_specs=blocks_in((src, *raw)),
        out_specs=blocks_in(outs),
        out_shape=outs,
        compiler_params=params(20),
        cost_estimate=cost(32 * rows * rows * d, 6 * MIB),
        name="deal_rows",
    )(src, *raw)
    return outs[:2], outs[2:4], outs[4]


def total_of(refs):
    total = refs[0][...]
    for ref in refs[1:]:
        total = total + ref[...].astype(f32)
    return total


def norm_kernel(n_terms, bias_row, gain_row, shift_row, *refs):
    terms, (vec_ref, y_ref, low_ref, n_ref, r_ref) = refs[:n_terms], refs[n_terms:]
    row = lambda i: vec_ref[i : i + 1, :]
    v = total_of(terms) + row(bias_row)
    centred = v - jnp.mean(v, axis=-1, keepdims=True)
    r = lax.rsqrt(jnp.mean(centred * centred, axis=-1, keepdims=True) + EPS)
    n = centred * r
    y = n * row(gain_row) + row(shift_row)
    y_ref[...] = y
    low_ref[...] = y.astype(bf16)
    n_ref[...] = n
    r_ref[...] = r


def term_specs(terms):
    shape = terms[0].shape
    return [pl.BlockSpec(shape, whole(0, 0)) for _ in terms]


def norm(terms, vectors, bias_row, gain_row, shift_row):
    shape = terms[0].shape
    outs = [struct(shape, f32), struct(shape, bf16), hbm(shape, f32), struct((shape[0], 1), f32)]
    return pl.pallas_call(
        functools.partial(norm_kernel, len(terms), bias_row, gain_row, shift_row),
        grid=(1,),
        in_specs=term_specs(terms) + [full(vectors)],
        out_specs=blocks_in(outs),
        out_shape=outs,
        compiler_params=params(8),
        cost_estimate=cost(20 * terms[0].size, 2 * MIB),
        name="norm",
    )(*terms, vectors)


def norm_back_kernel(n_terms, gain_row, has_sums, *refs):
    terms, refs = refs[:n_terms], refs[n_terms:]
    n_ref, r_ref, vec_ref = refs[:3]
    dv_ref, low_ref, sums_ref = refs[-3:]
    d_out, n = total_of(terms), n_ref[...]
    dn = d_out * vec_ref[gain_row : gain_row + 1, :]
    dv = r_ref[...] * (
        dn - jnp.mean(dn, axis=-1, keepdims=True) - n * jnp.mean(dn * n, axis=-1, keepdims=True)
    )
    dv_ref[...] = dv
    low_ref[...] = dv.astype(bf16)
    for i, a in enumerate((d_out * n, d_out, dv)):
        column = jnp.sum(a, axis=0, keepdims=True)
        sums_ref[i : i + 1, :] = column + refs[3][i : i + 1, :] if has_sums else column


def norm_back(terms, n, r, vectors, gain_row, sums=None):
    shape = terms[0].shape
    outs = [struct(shape, f32), struct(shape, bf16), struct((3, shape[1]), f32)]
    more = [] if sums is None else [sums]
    return pl.pallas_call(
        functools.partial(norm_back_kernel, len(terms), gain_row, sums is not None),
        grid=(1,),
        in_specs=term_specs(terms) + blocks_in((n, r, vectors, *more)),
        out_specs=blocks_in(outs),
        out_shape=outs,
        compiler_params=params(8),
        cost_estimate=cost(20 * terms[0].size, 3 * MIB),
        name="norm_back",
    )(*terms, n, r, vectors, *more)


def dot(a, b, ca, cb):
    return lax.dot_general(a, b, (((ca,), (cb,)), ((), ())), preferred_element_type=f32)


def swap(a, axis):
    return lax.ppermute(a, axis, SWAP)


def flip_d(a, bit, n_d):
    return lax.ppermute(a, "d", [(i, i ^ (1 << bit)) for i in range(n_d)])


def to_home(a):
    return lax.ppermute(a, ("c", "zh"), [(1, 2), (2, 1)])


def after(a, *marks):
    return lax.optimization_barrier((a,) + marks)[0]


def send_rows(own):
    return (own, swap(own, "c")), swap(own, "zl")


def far_rows(far, *marks):
    if marks:
        far = after(far, *marks)
    return far, swap(far, "c")


def chip_sum(mine, theirs, *arrivals):
    other = swap(after(theirs, *arrivals) if arrivals else theirs, "c")
    return mine, other


def cross_sum(terms):
    total = (terms[0] + terms[1].astype(f32)).astype(bf16)
    return total, swap(total, "zl")


def masks_of(order):
    masks = [0]
    for bit in order:
        masks = masks + [m ^ (1 << bit) for m in masks]
    return masks


def absolute_specs(n_d):
    return [(False, d, core) for d in range(n_d) for core in range(2)]


def reduce_specs(n_d):
    bits = list(range(n_d.bit_length() - 1))
    half = n_d // 2
    order = []
    for core, masks in ((0, masks_of(bits)), (1, masks_of(bits[::-1]))):
        order += [(True, m, core) for m in masks[half:] + masks[:half]]
    return order


class Gather:
    def __init__(self, fields, tile, crossed, widths, pos, where, n_d):
        self.fields, self.pos, self.where, self.n_d = fields, pos, where, n_d
        self.widths, self.tile, self.crossed = widths, tile, crossed

    def cores(self, *marks):
        _, c, zh, _ = self.pos
        same = c == zh
        crossed = after(self.crossed, *marks) if marks else self.crossed
        self.own = jnp.where(same, self.tile, crossed)
        self.other = swap(jnp.where(same, crossed, self.tile), "c")
        return self.other

    def collect(self, *marks):
        self.both = jnp.stack([self.own, self.other])
        both = after(self.both, *marks) if marks else self.both
        self.stacks = [lax.all_gather(both, "d", axis=0, tiled=True)]
        self.specs = absolute_specs(self.n_d)
        return self.stacks[0]

    def weights(self):
        found = place(self.fields, self.stacks, self.specs, self.where, *self.widths)
        return dict(zip(self.fields, found))


class Reduce:
    def __init__(self, fields, pairs, pos, where, n_d, by_halves):
        self.fields, self.pos, self.n_d, self.step = fields, pos, n_d, 0
        specs = reduce_specs(n_d) if by_halves else absolute_specs(n_d)
        counts = [n_d // 2] * 4 if by_halves else [2 * n_d]
        self.stacks = weight_grad(fields, pairs, specs, counts, where)

    def collect(self, *marks):
        both = lax.psum_scatter(after(self.stacks[0], *marks), "d", scatter_dimension=0, tiled=True)
        self.first, self.second = both[0], both[1]
        return both

    def halve(self, *marks):
        bits = list(range(self.n_d.bit_length() - 1))
        if self.step == len(bits):
            return []
        if self.step == 0:
            self.sends, self.keeps = [self.stacks[0], self.stacks[2]], [self.stacks[1], self.stacks[3]]
        sends = lax.optimization_barrier((*self.sends, *marks))[:2] if marks else self.sends
        orders = (bits[::-1], bits)
        gots = [flip_d(a, o[self.step], self.n_d) for a, o in zip(sends, orders)]
        self.step += 1
        half = self.keeps[0].shape[0] // 2
        if self.step < len(bits):
            self.sends = [
                (k[half:].astype(f32) + g[half:].astype(f32)).astype(bf16)
                for k, g in zip(self.keeps, gots)
            ]
            self.keeps = [k[:half].astype(f32) + g[:half].astype(f32) for k, g in zip(self.keeps, gots)]
        else:
            self.first, self.second = (k[0].astype(f32) + g[0].astype(f32) for k, g in zip(self.keeps, gots))
        return gots

    def cores(self, *marks):
        while len(self.stacks) > 1 and self.step < self.n_d.bit_length() - 1:
            self.halve()
        second = self.second.astype(bf16)
        self.other = swap(after(second, *marks) if marks else second, "c")
        self.crossed, self.at = [], 0
        return self.other

    def cross(self, lines, *marks):
        _, c, zh, _ = self.pos
        same = c == zh
        part = slice(self.at, self.at + lines)
        send = jnp.where(same, self.other[part], self.first[part].astype(bf16))
        self.crossed.append(swap(after(send, *marks) if marks else send, "zh"))
        self.at += lines
        return self.crossed[-1]

    def finish(self, outs, layer, widths, *marks):
        _, c, zh, _ = self.pos
        got = jnp.concatenate(self.crossed, 0) if len(self.crossed) > 1 else self.crossed[0]
        first = after(self.first, *marks) if marks else self.first
        keep = jnp.where(c == zh, first.astype(f32), self.other.astype(f32))
        prev = None if outs[self.fields[0]] is None else [outs[f] for f in self.fields]
        outs.update(zip(self.fields, finish(self.fields, keep, got, layer, prev, *widths)))


def gather_small(own, pos, n_d):
    d, c, _, zl = pos
    cur = own
    for axis, me in (("zl", zl), ("c", c)):
        got = swap(cur, axis)
        cur = jnp.where(me == 0, jnp.concatenate([cur, got]), jnp.concatenate([got, cur]))
    for bit in range(n_d.bit_length() - 1):
        got = flip_d(cur, bit, n_d)
        mine = jnp.bitwise_and(jnp.right_shift(d, bit), 1)
        cur = jnp.where(mine == 0, jnp.concatenate([cur, got]), jnp.concatenate([got, cur]))
    return cur


def pick(a, at, axis):
    return lax.dynamic_index_in_dim(a, at, axis, keepdims=False)


def halve_small(cur, me, send):
    view = cur.reshape(2, -1, cur.shape[1])
    return pick(view, me, 0) + send(pick(view, 1 - me, 0))


def body(tokens, cotangent, lengths, order, w_qkv, w_out, w_up, w_down, gains, biases, up_bias):
    rows = tokens.shape[0]
    n_d = lax.axis_size("d")
    n_dev = n_d * 8
    head_width = D // 4
    heads = head_width // HEAD_DIM
    ff_width = FF // 4
    widths = (head_width, ff_width)
    scale = HEAD_DIM ** (-0.5)
    d, c, zh, zl = (lax.axis_index(a) for a in ALL)
    pos = (d, c, zh, zl)
    slot = 2 * c + zl
    where = jnp.stack([d, c]).astype(jnp.int32)
    stay = c == zh
    args = {"qkv": w_qkv.transpose(0, 2, 1, 3), "out": w_out, "up": w_up, "down": w_down}

    tile_a0 = pack((("qkv", 0), ("out", 0)), args)
    a0_crossed = swap(tile_a0, "zh")
    g_a0 = Gather(("qkv", "out"), tile_a0, a0_crossed, widths, pos, where, n_d)
    rest = [("up", 0), ("down", 0), ("qkv", 1), ("out", 1)]
    tile_f1 = pack((("up", 1), ("down", 1)), args)
    tile_rest = pack(rest, args)
    small_own = jnp.concatenate([a.reshape(1, -1) for a in (gains, biases, up_bias)], 1)
    src, seg_col, seg_row = maps(
        lengths, order, jnp.stack([d * 2 + zh, slot]).astype(jnp.int32), 4 * rows
    )
    seg_near, seg_far = seg_col[: 2 * rows], seg_col[2 * rows :]
    g_a0.cores(src, small_own, tile_rest, tile_f1)
    g_a0.collect()
    raw_got = to_home(after(tokens, a0_crossed))
    raw = jnp.where(stay, tokens, raw_got)
    raw_near, raw_far = send_rows(raw)
    rest_crossed = swap(after(tile_rest, raw_got), "zh")
    gathers, at = [], 0
    for n in range(0, len(rest), 2):
        fields = (rest[n][0], rest[n + 1][0])
        lines = sum(lines_of(f, *widths) for f in fields)
        part = slice(at, at + lines)
        gathers.append(Gather(fields, tile_rest[part], rest_crossed[part], widths, pos, where, n_d))
        at += lines
    g_f0, g_a1 = gathers
    x_near, x_far, hidden = deal_rows(src, [*raw_near, *far_rows(raw_far)])
    small_near = gather_small(after(small_own, x_near[0]), pos, n_d)
    small_far = swap(small_near, "zh")
    width = D // n_dev
    up_width = FF // n_dev
    n_vec = LAYERS * 8
    small_all = jnp.where(zh == 0, jnp.stack([small_near, small_far]), jnp.stack([small_far, small_near]))
    small_all = small_all.reshape(2, n_d * 2, 2, -1)
    vectors = small_all[..., : n_vec * width].reshape(2, n_d * 2, 2, n_vec, width)
    vectors = vectors.transpose(3, 1, 0, 2, 4).reshape(n_vec, D)
    ups = small_all[..., n_vec * width :].reshape(2, n_d * 2, 2, LAYERS, up_width)
    ups = ups.transpose(3, 1, 0, 2, 4).reshape(LAYERS, FF)
    ups = lax.dynamic_slice(ups, (0, slot * ff_width), (LAYERS, ff_width))
    own_vectors = lax.dynamic_slice(vectors, (0, slot * head_width), (n_vec, head_width))
    gain_row = lambda layer, i: 2 * layer + i
    bias_row = lambda layer, i: 2 * LAYERS + 6 * layer + i
    f0_other = g_f0.cores(small_near)
    g_f0.collect()
    cot_got = to_home(after(cotangent, f0_other, small_far))
    cot_near, cot_sent = send_rows(jnp.where(stay, cotangent, cot_got))
    f1_crossed = swap(after(tile_f1, cot_got), "zh")
    g_f1 = Gather(("up", "down"), tile_f1, f1_crossed, widths, pos, where, n_d)
    weights = [g_a0.weights(), {}]

    kept = []
    x_sent = None
    for layer in range(LAYERS):
        first = layer == 0
        w = weights[layer]
        q_row, v_row = bias_row(layer, 0), bias_row(layer, 1)
        add = jnp.concatenate(
            [
                own_vectors[q_row : q_row + 1],
                jnp.zeros((1, head_width), f32),
                own_vectors[v_row : v_row + 1],
            ],
            1,
        )
        if first:
            x_near = (after(x_near[0], g_f0.both), x_near[1])
        proj_near, keep_near = project(x_near, w["qkv"], add)
        if not first:
            x_far = far_rows(x_sent, keep_near)
        proj_far, keep_far = project(x_far, w["qkv"], add)
        proj = (proj_near, proj_far)
        x_kept = (keep_near, keep_far)
        due = [cot_got] if first else []
        att_far, lse_far, mine, theirs = attend(
            proj_far, proj, seg_far, seg_row, w["out"], scale, heads
        )
        chip, crossed = cross_sum(chip_sum(mine, theirs, *due))
        att_near, lse_near, mine, theirs = attend(
            after(proj_near, chip), proj, seg_near, seg_row, w["out"], scale, heads
        )
        terms = chip_sum(mine, theirs, crossed)
        if first:
            terms = (terms[0], after(terms[1], f1_crossed))
        terms = (*terms, crossed)
        at = [bias_row(layer, 2), gain_row(layer, 0), bias_row(layer, 3)]
        normed, low, n_one, r_one = norm((hidden, *terms), vectors, *at)
        n_near, n_sent = send_rows(low)
        due = [n_sent]
        if first:
            w.update(g_f0.weights())
            g_a1.cores(low)
            g_a1.collect()
        else:
            w.update(g_f1.weights())
        u_bias = ups[layer : layer + 1]
        act_near, slope_near, mine_near, theirs_near, keep_near = ffn(n_near, w["up"], w["down"], u_bias)
        near = chip_sum(mine_near, theirs_near, *due)
        n_far = far_rows(n_sent, keep_near)
        due = []
        act_far, slope_far, mine, theirs, keep_far = ffn(n_far, w["up"], w["down"], u_bias)
        chip, crossed = cross_sum(chip_sum(mine, theirs, *due))
        if first:
            g_f1.cores(chip)
            g_f1.collect()
        at = [bias_row(layer, 4), gain_row(layer, 1), bias_row(layer, 5)]
        hidden, low, n_two, r_two = norm((normed, *near, crossed), vectors, *at)
        kept.append(
            dict(
                x=x_kept, proj=proj, lse=(lse_near, lse_far), att=(att_near, att_far),
                one=(n_one, r_one), n=(keep_near, keep_far), slope=(slope_near, slope_far),
                act=(act_near, act_far), two=(n_two, r_two),
            )
        )
        if first:
            weights[1].update(g_a1.weights())
            x_near, x_sent = send_rows(low)
    last_low = low

    deal = (src[:rows] == jnp.arange(4 * rows, dtype=jnp.int32)[None, :]).astype(bf16)
    cot = jnp.concatenate([*cot_near, *far_rows(cot_sent)], 0)
    valid = (seg_near[:rows] < SEQ_GRP).astype(f32)
    grad_y = (dot(deal, cot, 1, 0) * valid,)
    vector_sums = [None] * LAYERS
    up_sums = [None] * LAYERS
    late = None

    def spot(vec, full_width):
        return lax.dynamic_update_slice(jnp.zeros((1, full_width), f32), vec, (0, slot * vec.shape[1]))

    for layer in reversed(range(LAYERS)):
        w, k = weights[layer], kept[layer]
        d_two, low, sums_two = norm_back(grad_y, *k["two"], vectors, gain_row(layer, 1))
        two_near, two_sent = send_rows(low)
        if late:
            late[0].cores(low)
        up_near, sum_near, mine_near, theirs_near, keep_two_near = ffn_back(
            two_near, w["up"], w["down"], k["slope"][0]
        )
        near = chip_sum(mine_near, theirs_near, two_sent)
        two_far = far_rows(two_sent, up_near)
        due = []
        if late:
            due += [late[0].cross(ff_width, up_near)]
        up_far, sum_far, mine, theirs, keep_two_far = ffn_back(
            two_far, w["up"], w["down"], k["slope"][1]
        )
        chip, crossed = cross_sum(chip_sum(mine, theirs, *due))
        two_pair = ((keep_two_near, keep_two_far), (k["act"][0], after(k["act"][1], chip)))
        up_pair = (k["n"], (up_near, after(up_far, chip)))
        due = []
        if late:
            due += [late[0].cross(ff_width, chip)]
            r_down = Reduce(("down",), (two_pair,), pos, where, n_d, True)
            down_got = r_down.halve()
            up_pair = (up_pair[0], (up_near, after(up_far, r_down.stacks[0])))
            r_ff = Reduce(("up",), (up_pair,), pos, where, n_d, True)
            up_got = r_ff.halve()
        else:
            r_ff = Reduce(("up", "down"), (up_pair, two_pair), pos, where, n_d, False)
        d_two = after(d_two, r_ff.stacks[0], *due)
        d_one, low, sums_one = norm_back((d_two, *near, crossed), *k["one"], vectors, gain_row(layer, 0))
        one_near, one_sent = send_rows(low)
        if not late:
            r_ff.collect(low)
        *earlier, keep_one_near = attend_back(
            k["proj"][0], k["proj"], seg_near, seg_row, k["lse"][0], one_near, w["out"], scale, heads
        )
        one_far = far_rows(one_sent, earlier[0])
        due = []
        if late:
            earlier[0] = after(earlier[0], *down_got, *up_got)
            due += r_down.halve(earlier[0]) + r_ff.halve(earlier[0])
            late[1].cores(earlier[0])
            due += [late[1].cross(4 * head_width, earlier[0])]
        else:
            mixed_got = to_home(after(last_low, earlier[0]))
            due += [mixed_got]
        d_near, d_far, head_sums, keep_one_far = attend_back(
            k["proj"][1], k["proj"], seg_far, seg_row, k["lse"][1], one_far, w["out"], scale, heads,
            earlier,
        )
        if late:
            outs = {f: None for f in ("qkv", "out", "up", "down")}
            late[0].finish(outs, 1, widths, earlier[0])
            due += [outs["up"]]
        d_far = after(d_far, *due)
        mine, theirs = input_grad(d_far, w["qkv"])
        chip, crossed = cross_sum(chip_sum(mine, theirs))
        att_pairs = ((k["x"], (d_near, after(d_far, chip))), ((keep_one_near, keep_one_far), k["att"]))
        if late:
            r_att = Reduce(("qkv", "out"), att_pairs, pos, where, n_d, True)
            r_att.halve()
            d_near = after(d_near, r_att.stacks[0])
            near = chip_sum(*input_grad(d_near, w["qkv"]))
        else:
            near = chip_sum(*input_grad(after(d_near, chip), w["qkv"]))
            att_pairs = ((k["x"], (after(d_near, near[1]), d_far)), att_pairs[1])
            r_att = Reduce(("qkv", "out"), att_pairs, pos, where, n_d, False)
            late = (r_ff, r_att)
            d_one = after(d_one, r_att.stacks[0])
            r_att.collect(crossed)
        grad_y = (d_one, *near, crossed)
        vector_sums[layer] = (
            [sums_one[0:1], sums_two[0:1]],
            [
                spot(head_sums[0:1], D), spot(head_sums[1:2], D), sums_one[2:3],
                sums_one[1:2], sums_two[2:3], sums_two[1:2],
            ],
        )
        up_sums[layer] = spot(sum_near + sum_far, FF)

    r_down.cores(d_far)
    down_crossed = r_down.cross(ff_width)
    r_ff.cores(d_far)
    up_crossed = r_ff.cross(ff_width, down_crossed)
    att_got = r_att.halve(down_crossed)
    base, mine, other, crossed = grad_y
    own_grad = (base + mine + other.astype(f32) + crossed.astype(f32)).astype(bf16)
    grad_got = to_home(after(own_grad, *att_got))
    r_att.cores(up_crossed)
    r_att.cross(4 * head_width)
    late[1].finish(outs, 1, widths, *att_got)
    r_down.finish(outs, 0, widths, *att_got)
    r_ff.finish(outs, 0, widths, *att_got)
    r_att.finish(outs, 0, widths)
    tokens_grad = jnp.where(stay, own_grad, grad_got).astype(f32)
    mixed = jnp.where(stay, last_low, after(mixed_got, *att_got))

    terms = jnp.concatenate(
        [g for s in vector_sums for g in s[0]] + [b for s in vector_sums for b in s[1]], 0
    )
    small = jnp.concatenate(
        [
            terms.reshape(n_vec, n_dev, width).transpose(1, 0, 2).reshape(n_dev, n_vec * width),
            jnp.concatenate(up_sums, 0)
            .reshape(LAYERS, n_dev, up_width)
            .transpose(1, 0, 2)
            .reshape(n_dev, LAYERS * up_width),
        ],
        1,
    )
    n_small = small.shape[1]
    small = after(small, *att_got).reshape(n_d, 2, 4 * n_small)
    small = pick(small, c, 1) + swap(pick(small, 1 - c, 1), "c")
    small = small.reshape(n_d, 2, 2, n_small)
    small = pick(small, zl, 2) + swap(pick(small, 1 - zl, 2), "zl")
    small = small.reshape(n_d, 2 * n_small)
    for bit in reversed(range(n_d.bit_length() - 1)):
        mine = jnp.bitwise_and(jnp.right_shift(d, bit), 1)
        small = halve_small(small, mine, lambda a, bit=bit: flip_d(a, bit, n_d))
    small_sum = halve_small(small.reshape(2, n_small), zh, lambda a: swap(a, "zh"))
    n_gain = LAYERS * 2 * width
    g_gains = small_sum[:, :n_gain].reshape(LAYERS, 2, width)
    g_biases = small_sum[:, n_gain : n_vec * width].reshape(LAYERS, 6, width)
    g_upb = small_sum[:, n_vec * width :].reshape(LAYERS, up_width)
    g_qkv = outs["qkv"].transpose(0, 2, 1, 3)
    return mixed, tokens_grad, g_qkv, outs["out"], outs["up"], outs["down"], g_gains, g_biases, g_upb


def solution(mesh):
    n_dp, n_t = mesh.shape["dp"], mesh.shape["tensor"]
    fine = Mesh(mesh.devices.reshape(n_dp // 2, 2, n_t // 2, 2), ALL)
    dp, t = ("d", "c"), ("zh", "zl")
    return jax.shard_map(
        body,
        mesh=fine,
        in_specs=(
            P(ALL, None),
            P(ALL, None),
            P(),
            P(),
            P(None, dp, None, t),
            P(None, t, dp),
            P(None, dp, t),
            P(None, t, dp),
            P(None, None, ALL),
            P(None, None, ALL),
            P(None, ALL),
        ),
        out_specs=(
            P(ALL, None),
            P(ALL, None),
            P(None, dp, None, t),
            P(None, t, dp),
            P(None, dp, t),
            P(None, t, dp),
            P(None, None, ALL),
            P(None, None, ALL),
            P(None, ALL),
        ),
        check_vma=False,
    )
```
